32 devices in a mesh: group: 2 (over x), node: 16 (over z, y, core).
Axes of the slice: x: 2, y: 2, z: 4, core: 2. Of those that a mesh axis runs over, the one named last changes fastest.
Arguments:
- tokens: bfloat16 [512, 7168], P(('group', 'node')), parts along dimension 0, may hold values from -6 to 6
- expert_ids: int32 [512, 2], P(('group', 'node')), parts along dimension 0, may hold values from 0 to 3, all different within a row; in each aligned block of 16 rows (0 to 15, 16 to 31, ...) at most 12 rows name the same one
- gates: float32 [512, 2], P(('group', 'node')), parts along dimension 0, may hold values from 0.05 to 1
- placement: int32 [4], replicated, may hold values from 0 to 3, each once
- gate_weight: bfloat16 [7168, 4096], P(None, 'node'), may hold values from -0.0625 to 0.0625
- up_weight: bfloat16 [7168, 4096], P(None, 'node'), may hold values from -0.0625 to 0.0625
- down_weight: bfloat16 [4096, 7168], P('node'), may hold values from -0.1875 to 0.1875
Outputs:
- mixed: bfloat16 [512, 7168], P(('group', 'node')), parts along dimension 0
The draws below stay inside these ranges and needn't reach their ends.
There are 2 independent parts, one for each index of `group`. The reference program is written for one: setup_inputs(seed, part) draws one part's arguments, and reference() takes and returns one part's arrays. A program takes and returns all parts, laid end to end along the dimension named above; an argument that names none is the same for every part. Nothing has to cross between parts.
Inputs may be any that keep to these rules, and one draw needn't show every extreme that they name: `expert_ids`: each row names 2 different experts; within the rows of one device no expert is named more than 12 times. `placement`: each block index holds one expert.
All inputs are finite; a program needn't handle non-finite values.
Results may differ from the reference program's by a relative error of at most 0.0095.
Values may be sent and summed in bfloat16 or wider, within the bound.
No kernel may reach another device: no remote copies, remote signals or barrier semaphores. Data moves between devices by JAX's collectives and lax.ppermute only.
A program may use at most 128 MiB of HBM per device.

```python
import math
import jax
import jax.numpy as jnp
import numpy as np
from jax import lax

D = 7168
HID_DEV = 256
FF = 1024
TOK_DEV = 16
CAP = 12
EXPERTS = 4
TOP = 2
TOKENS = 256
N_NODE = 16


def steps_of(rng, extent, shards, low, largest):
    def one(dim, blocks):
        steps = jax.random.uniform(jax.random.fold_in(jax.random.fold_in(rng, 6), dim), (blocks,), jnp.float32, low / len(shards), largest / len(shards))
        return jnp.repeat(jnp.exp(steps), extent[dim] // blocks).reshape((-1,) + (1,) * (len(extent) - dim - 1))

    factor_of = one(*shards[0])
    for cut in shards[1:]:
        factor_of = factor_of * one(*cut)
    return factor_of


def deal_out(stream_key, own, number, rows, count, top, most, lean):
    sequence = jax.random.permutation(stream_key, count)
    heavy_load, common = portions_of(count, rows * top, most, lean, True), portions_of(count, rows * top, most, lean, False)
    places = jnp.arange(count)

    def named(sizes, turn):
        used = int((sizes > 0).sum())
        fixed = max(1, used // 4)
        moved = fixed + (places - fixed + turn * (used - fixed)) % max(1, count - fixed)
        return jnp.zeros((count,), jnp.int32).at[sequence[jnp.where(places < fixed, places, moved)]].set(jnp.asarray(sizes, jnp.int32))

    sizes = jnp.where(number % 4 == 0, named(heavy_load, number // 4), named(common, number - number // 4 - 1))
    mixed = jax.random.permutation(jax.random.fold_in(own, 3), count)
    donor, taker = mixed[0:count // 2 * 2:2], mixed[1:count // 2 * 2:2]
    slack = jnp.minimum(sizes[donor] - 1, most - sizes[taker]) // 2
    slack = jnp.where((donor == sequence[0]) | (taker == sequence[0]) | (sizes[taker] == 0), 0, jnp.maximum(slack, 0))
    moved = jax.random.randint(jax.random.fold_in(own, 4), (count // 2,), 0, 1 << 20) % (slack + 1)
    sizes = sizes.at[donor].add(-moved).at[taker].add(moved)
    members = jnp.searchsorted(jnp.cumsum(sizes), jnp.arange(rows * top), side="right").astype(jnp.int32)
    grid = members.reshape(top, rows).T
    grid = grid[jax.random.permutation(jax.random.fold_in(own, 1), rows)]
    turn = jax.random.randint(jax.random.fold_in(own, 2), (rows, 1), 0, top)
    return jnp.take_along_axis(grid, (jnp.arange(top)[None, :] + turn) % top, axis=1)


def portions_of(count, total, limit, skew, full):
    weights = [(1 << 20) // math.isqrt(standing ** skew) + 1 for standing in range(1, count + 1)]
    largest = limit if full else min(limit, max(-(-total // count), total * weights[0] // sum(weights)))
    least = 1 if total - largest >= count - 1 else 0
    given, spare = [largest] + [least] * (count - 1), total - largest - least * (count - 1)
    while spare > 0:
        candidates = [i for i in range(1, count) if given[i] < largest] or [i for i in range(1, count) if given[i] < limit]
        mass, budget = sum([weights[i] for i in candidates]), spare
        for i in candidates:
            addition = min(limit - given[i], max(1, budget * weights[i] // mass), spare)
            given[i] = given[i] + addition
            spare = spare - addition
    return np.array(given)


def scatter_about(own_key, extent, spread, most, cuts=(), held_as=jnp.bfloat16):
    values = spread * jax.random.normal(own_key, extent, jnp.float32)
    if cuts:
        values = values * steps_of(own_key, extent, cuts, -0.22, 0.18)
    return jnp.clip(values, -most, most).astype(held_as)


def setup_inputs(seed: int = 0, part: int = 0) -> dict:
    streams_of = jax.random.split(jax.random.key(seed), 8)
    part_splits = jax.random.split(jax.random.fold_in(streams_of[7], part), 8)
    tokens = scatter_about(part_splits[0], (TOKENS, D), 1.0, 6.0, ((0, 16),))
    expert_ids_keys = jax.random.split(jax.random.fold_in(part_splits[1], 1), TOKENS // TOK_DEV)
    expert_ids_turns = jax.random.permutation(jax.random.fold_in(part_splits[1], 3), TOKENS // TOK_DEV)
    expert_ids = jax.vmap(lambda own, number: deal_out(jax.random.fold_in(part_splits[1], 2), own, number, TOK_DEV, EXPERTS, TOP, CAP, 2))(expert_ids_keys, expert_ids_turns).reshape((TOKENS, TOP))
    gates = jnp.clip(jnp.exp(math.log(1.0) - 2.9957323 * jax.random.uniform(part_splits[2], (TOKENS, TOP), jnp.float32) ** steps_of(part_splits[2], (TOKENS, TOP), ((0, 16),), -0.2, 0.2)), 0.05, 1.0)
    placement = jax.random.permutation(streams_of[3], EXPERTS).astype(jnp.int32)
    gate_weight = scatter_about(streams_of[4], (D, EXPERTS * FF), D ** -0.5, 0.0625, ((1, 16),))
    up_weight = scatter_about(streams_of[5], (D, EXPERTS * FF), D ** -0.5, 0.0625, ((1, 16),))
    down_weight = scatter_about(streams_of[6], (EXPERTS * FF, D), FF ** -0.5, 0.1875, ((0, 16),))
    return dict(tokens=tokens, expert_ids=expert_ids, gates=gates, placement=placement, gate_weight=gate_weight, up_weight=up_weight, down_weight=down_weight)


def reference(tokens, expert_ids, gates, placement, gate_weight, up_weight, down_weight):
    toks = tokens.reshape(N_NODE, TOK_DEV, D)
    ids = expert_ids.reshape(N_NODE, TOK_DEV, TOP)
    picks = (ids[:, :, :, None] == jnp.arange(EXPERTS, dtype=jnp.int32)[None, None, None, :]).astype(jnp.int32)
    routed = jnp.sum(picks, axis=2)
    earlier = jnp.cumsum(routed, axis=1) - routed
    slot = jnp.sum(picks * earlier[:, :, None, :], axis=3).astype(jnp.int32)
    quad = jnp.sum(picks * placement[None, None, None, :], axis=3).astype(jnp.int32)
    target = quad * CAP + slot
    source = jnp.arange(N_NODE, dtype=jnp.int32)[:, None, None]
    values = jnp.broadcast_to(toks[:, :, None, :], (N_NODE, TOK_DEV, TOP, D))
    buckets = jnp.zeros((N_NODE, EXPERTS * CAP, D), jnp.bfloat16).at[source, target].set(values)
    buckets = buckets.reshape(N_NODE, EXPERTS, CAP, D)

    def one_block(index):
        rows = lax.dynamic_index_in_dim(buckets, index, 1, keepdims=False).reshape(N_NODE * CAP, D)
        start = (index * FF).astype(jnp.int32)
        w_gate = lax.dynamic_slice_in_dim(gate_weight, start, FF, 1)
        w_up = lax.dynamic_slice_in_dim(up_weight, start, FF, 1)
        w_down = lax.dynamic_slice_in_dim(down_weight, start, FF, 0).reshape(4, HID_DEV, D)
        gate_rows = jnp.dot(rows, w_gate, preferred_element_type=jnp.float32)
        up_rows = jnp.dot(rows, w_up, preferred_element_type=jnp.float32)
        hidden = (jax.nn.silu(gate_rows) * up_rows).astype(jnp.bfloat16)
        split = hidden.reshape(N_NODE * CAP, 4, HID_DEV).astype(jnp.float32)
        pieces = jnp.einsum("rsh,shd->srd", split, w_down.astype(jnp.float32)).astype(jnp.bfloat16)
        total = jnp.sum(pieces.astype(jnp.float32), axis=0).astype(jnp.bfloat16)
        return total.reshape(N_NODE, CAP, D)

    expert_out = lax.map(one_block, jnp.arange(EXPERTS, dtype=jnp.int32))
    picked = expert_out[quad, source, slot]
    mixed = jnp.sum(picked.astype(jnp.float32) * gates.reshape(N_NODE, TOK_DEV, TOP)[:, :, :, None], axis=2)
    return mixed.astype(jnp.bfloat16).reshape(TOKENS, D)
```

```python
import jax
import jax.numpy as jnp
from jax import lax
from jax.sharding import PartitionSpec as P

LANES = 128


def block_weights(expert_ids, gates, placement):
    n_blocks = placement.shape[0]
    experts = jnp.arange(n_blocks, dtype=jnp.int32)
    picks = (expert_ids[:, :, None] == experts[None, None, :]).astype(jnp.int32)
    block_of = jnp.sum(picks * placement[None, None, :], axis=2)
    chosen = block_of[:, :, None] == experts[None, None, :]
    return jnp.sum(jnp.where(chosen, gates[:, :, None], 0.0), axis=1)


def split_three(values):
    high = lax.reduce_precision(values, 8, 7)
    rest = values - high
    middle = lax.reduce_precision(rest, 8, 7)
    return high, middle, rest - middle


def local(tokens, expert_ids, gates, placement, gate_weight, up_weight, down_weight):
    tok_rows, width = tokens.shape
    n_blocks = placement.shape[0]
    parts = lax.axis_size("node") // n_blocks
    block = lax.axis_index("node") // parts
    weights = jnp.concatenate(split_three(block_weights(expert_ids, gates, placement)), axis=1)
    weights = jnp.pad(weights, ((0, 0), (0, LANES - 3 * n_blocks))).astype(jnp.bfloat16)
    outgoing = jnp.concatenate([tokens, weights], axis=1)
    gathered = lax.all_gather(outgoing, "node", axis=0, tiled=True)
    rows = gathered[:, :width]
    tail = gathered[:, width:].astype(jnp.float32)
    lane = jnp.arange(LANES, dtype=jnp.int32)
    mine = (lane % n_blocks == block) & (lane < 3 * n_blocks)
    scale = jnp.sum(jnp.where(mine[None, :], tail, 0.0), axis=1, keepdims=True)
    gate_rows = jnp.dot(rows, gate_weight, preferred_element_type=jnp.float32)
    up_rows = jnp.dot(rows, up_weight, preferred_element_type=jnp.float32)
    hidden = (jax.nn.silu(gate_rows) * up_rows * scale).astype(jnp.bfloat16)
    piece = jnp.dot(hidden, down_weight, preferred_element_type=jnp.float32).astype(jnp.bfloat16)
    return lax.psum_scatter(piece, "node", scatter_dimension=0, tiled=True)


def solution(mesh):
    placed = (
        P(("group", "node"), None),
        P(("group", "node"), None),
        P(("group", "node"), None),
        P(),
        P(None, "node"),
        P(None, "node"),
        P("node", None),
    )
    return jax.shard_map(
        local, mesh=mesh, in_specs=placed, out_specs=P(("group", "node"), None), check_vma=False
    )
```

```python
import functools

import jax
import jax.numpy as jnp
from jax import lax
from jax.experimental import pallas as pl
from jax.experimental.pallas import tpu as pltpu
from jax.sharding import PartitionSpec as P

CHUNKS = 4
VMEM_BYTES = 56 * 2**20


def slots_of(expert_ids, n_blocks):
    rows, top = expert_ids.shape
    experts = lax.broadcasted_iota(jnp.int32, (rows, n_blocks), 1)
    picks = jnp.zeros((rows, n_blocks), jnp.float32)
    for k in range(top):
        picks = picks + jnp.where(expert_ids[:, k : k + 1] == experts, 1.0, 0.0)
    before = lax.broadcasted_iota(jnp.int32, (rows, rows), 1) < lax.broadcasted_iota(
        jnp.int32, (rows, rows), 0
    )
    earlier = jnp.dot(
        jnp.where(before, 1.0, 0.0).astype(jnp.bfloat16),
        picks.astype(jnp.bfloat16),
        preferred_element_type=jnp.float32,
    )
    return experts, picks, earlier


def expert_at(placement_ref, block):
    found = jnp.int32(0)
    for e in range(placement_ref.shape[0]):
        found = jnp.where(placement_ref[e] == block, jnp.int32(e), found)
    return found


def column_of(values, experts, expert):
    return jnp.sum(jnp.where(experts == expert, values, 0.0), axis=1, keepdims=True)


def bucket_row(rows, lanes):
    lane = lax.broadcasted_iota(jnp.int32, (rows, lanes), 1)
    half, quarter = rows // 2, rows // 4
    return jnp.where(lane < half, lane, half + lane % quarter).astype(jnp.float32)


def pack_kernel(n_blocks, parts, placement_ref, ids_ref, tokens_ref, *out_refs):
    rows, width = tokens_ref.shape
    half, quarter = rows // 2, rows // 4
    block = lax.axis_index("node") // parts
    experts, picks, earlier = slots_of(ids_ref[...], n_blocks)
    wanted = bucket_row(rows, rows)
    upper = lax.broadcasted_iota(jnp.int32, (half, width // 2), 0) < quarter
    for k, out_ref in enumerate(out_refs):
        expert = expert_at(placement_ref, lax.rem(block + k, n_blocks))
        named = column_of(picks, experts, expert) > 0.5
        slot = column_of(earlier, experts, expert)
        chooser = jnp.where(named & (slot == wanted), 1.0, 0.0).astype(jnp.bfloat16)
        packed = lax.dot_general(
            chooser, tokens_ref[...], (((0,), (0,)), ((), ())), preferred_element_type=jnp.float32
        )
        out_ref[:, :width] = packed[:half].astype(jnp.bfloat16)
        rest = jnp.where(upper, packed[half:, : width // 2], packed[half:, width // 2 :])
        out_ref[:, width:] = rest.astype(jnp.bfloat16)


def pack(placement, expert_ids, tokens, n_blocks, parts):
    rows, width = tokens.shape
    vmem = pl.BlockSpec(memory_space=pltpu.VMEM)
    shape = jax.ShapeDtypeStruct((rows // 2, width + width // 2), jnp.bfloat16)
    return pl.pallas_call(
        functools.partial(pack_kernel, n_blocks, parts),
        out_shape=[shape] * n_blocks,
        in_specs=[pl.BlockSpec(memory_space=pltpu.SMEM), vmem, vmem],
        out_specs=[vmem] * n_blocks,
        compiler_params=pltpu.CompilerParams(vmem_limit_bytes=VMEM_BYTES),
        cost_estimate=pl.CostEstimate(
            flops=2 * n_blocks * rows * rows * width,
            bytes_accessed=2 * (n_blocks + 1) * rows * width,
            transcendentals=0,
        ),
    )(placement, expert_ids, tokens)


def experts_kernel(count, *refs):
    pieces, (gate_hbm, up_hbm, down_hbm) = refs[:count], refs[count : count + 3]
    outs = refs[count + 3 : 2 * count + 3]
    gate_ref, up_ref, down_ref, sems = refs[2 * count + 3 :]
    width, hid = gate_hbm.shape
    height = pieces[0].shape[0]
    step = width // CHUNKS
    copies = []
    for j in range(CHUNKS):
        part = pl.ds(j * step, step)
        copies.append(
            (
                pltpu.make_async_copy(gate_hbm.at[part], gate_ref.at[part], sems.at[0, j]),
                pltpu.make_async_copy(up_hbm.at[part], up_ref.at[part], sems.at[1, j]),
            )
        )
    for pair in copies:
        for copy in pair:
            copy.start()
    down_copies = []
    for j in range(CHUNKS):
        part = pl.ds(j * step, step)
        down_copies.append(
            pltpu.make_async_copy(down_hbm.at[:, part], down_ref.at[:, part], sems.at[2, j])
        )
    order = [j for i in range(CHUNKS // 2) for j in (i, i + CHUNKS // 2)]
    for j in order:
        down_copies[j].start()

    total = count * height
    sums = {}
    for j in range(CHUNKS):
        start = j * step
        rest_start = width + (j % (CHUNKS // 2)) * step
        whole = [p[:, start : start + step] for p in pieces]
        rest = [p[:, rest_start : rest_start + step] for p in pieces]
        rows = jnp.concatenate(whole + rest, axis=0)
        side = j // (CHUNKS // 2)
        for name, ref, copy in (("g", gate_ref, copies[j][0]), ("u", up_ref, copies[j][1])):
            copy.wait()
            part = jnp.dot(
                rows, ref[start : start + step, :], preferred_element_type=jnp.float32
            )
            for key, value in (((name, 2), part[:total]), ((name, side), part[total:])):
                sums[key] = sums[key] + value if key in sums else value

    upper = lax.broadcasted_iota(jnp.int32, (total, hid), 0) % height < height // 2

    def whole_rows(name):
        left, right = sums[(name, 0)], sums[(name, 1)]
        shift = height // 2
        rest = jnp.where(
            upper,
            left + pltpu.roll(right, total - shift, axis=0),
            right + pltpu.roll(left, shift, axis=0),
        )
        return jnp.concatenate([sums[(name, 2)], rest], axis=0)

    gate_rows, up_rows = whole_rows("g"), whole_rows("u")
    hidden = (jax.nn.silu(gate_rows) * up_rows).astype(jnp.bfloat16)
    upper_out = lax.broadcasted_iota(jnp.int32, (total, step), 0) % height < height // 2
    for i in range(CHUNKS // 2):
        both = []
        for j in (i, i + CHUNKS // 2):
            down_copies[j].wait()
            part = jnp.dot(
                hidden, down_ref[:, j * step : (j + 1) * step], preferred_element_type=jnp.float32
            )
            for p, out in enumerate(outs):
                out[:, j * step : (j + 1) * step] = part[p * height : (p + 1) * height].astype(
                    jnp.bfloat16
                )
            both.append(part[total:])
        rest = jnp.where(upper_out, both[0], both[1]).astype(jnp.bfloat16)
        for p, out in enumerate(outs):
            out[:, width + i * step : width + (i + 1) * step] = rest[p * height : (p + 1) * height]


def run_experts(pieces, gate_weight, up_weight, down_weight):
    count = len(pieces)
    width, hid = gate_weight.shape
    height = pieces[0].shape[0]
    vmem = pl.BlockSpec(memory_space=pltpu.VMEM)
    hbm = pl.BlockSpec(memory_space=pl.ANY)
    return pl.pallas_call(
        functools.partial(experts_kernel, count),
        out_shape=[jax.ShapeDtypeStruct(pieces[0].shape, jnp.bfloat16)] * count,
        in_specs=[vmem] * count + [hbm] * 3,
        out_specs=[vmem] * count,
        scratch_shapes=[
            pltpu.VMEM((width, hid), jnp.bfloat16),
            pltpu.VMEM((width, hid), jnp.bfloat16),
            pltpu.VMEM((hid, width), jnp.bfloat16),
            pltpu.SemaphoreType.DMA((3, CHUNKS)),
        ],
        compiler_params=pltpu.CompilerParams(vmem_limit_bytes=VMEM_BYTES),
        cost_estimate=pl.CostEstimate(
            flops=12 * count * height * width * hid,
            bytes_accessed=6 * width * hid + 6 * count * height * width,
            transcendentals=2 * count * height * hid,
        ),
    )(*pieces, gate_weight, up_weight, down_weight)


def mix_kernel(n_blocks, parts, placement_ref, ids_ref, gates_ref, *refs):
    results, out_ref = refs[:-1], refs[-1]
    rows, width = out_ref.shape
    half, quarter = rows // 2, rows // 4
    block = lax.axis_index("node") // parts
    ids, gates = ids_ref[...], gates_ref[...]
    experts, picks, earlier = slots_of(ids, n_blocks)
    lane = lax.broadcasted_iota(jnp.int32, (rows, rows), 1)
    wanted = bucket_row(rows, rows)
    terms = []
    for k in range(n_blocks):
        expert = expert_at(placement_ref, lax.rem(block + k, n_blocks))
        named = column_of(picks, experts, expert) > 0.5
        slot = column_of(earlier, experts, expert)
        weight = jnp.sum(jnp.where(ids == expert, gates, 0.0), axis=1, keepdims=True)
        terms.append(jnp.where(named & (slot == wanted), weight, 0.0))

    def product(lhs, rhs):
        high = lhs.astype(jnp.bfloat16)
        left = lhs - high.astype(jnp.float32)
        middle = left.astype(jnp.bfloat16)
        low = (left - middle.astype(jnp.float32)).astype(jnp.bfloat16)
        both = jnp.dot(
            jnp.concatenate([high, middle, low], axis=0), rhs, preferred_element_type=jnp.float32
        )
        return both[:rows] + both[rows : 2 * rows] + both[2 * rows :]

    for side in range(2):
        begin = side * (width // 2)
        total = None
        for term, result in zip(terms, results):
            mine = (lane < half) | ((lane >= half + side * quarter) & (lane < half + (side + 1) * quarter))
            rhs = jnp.concatenate(
                [result[:, begin : begin + width // 2], result[:, width:]], axis=0
            )
            value = product(jnp.where(mine, term, 0.0), rhs)
            total = value if total is None else total + value
        out_ref[:, begin : begin + width // 2] = total.astype(jnp.bfloat16)


def mix(placement, expert_ids, gates, results, n_blocks, parts):
    rows = expert_ids.shape[0]
    width = results[0].shape[1] // 3 * 2
    vmem = pl.BlockSpec(memory_space=pltpu.VMEM)
    return pl.pallas_call(
        functools.partial(mix_kernel, n_blocks, parts),
        out_shape=jax.ShapeDtypeStruct((rows, width), jnp.bfloat16),
        in_specs=[pl.BlockSpec(memory_space=pltpu.SMEM)] + [vmem] * (2 + n_blocks),
        out_specs=vmem,
        compiler_params=pltpu.CompilerParams(vmem_limit_bytes=VMEM_BYTES),
        cost_estimate=pl.CostEstimate(
            flops=6 * n_blocks * rows * rows * width,
            bytes_accessed=2 * (n_blocks + 1) * rows * width,
            transcendentals=0,
        ),
    )(placement, expert_ids, gates, *results)


def add(*values):
    return sum(v.astype(jnp.float32) for v in values).astype(jnp.bfloat16)


def local(tokens, expert_ids, gates, placement, gate_weight, up_weight, down_weight):
    n_blocks = placement.shape[0]
    devices = lax.axis_size("node")
    parts = devices // n_blocks

    def along_z(value, k):
        pairs = [(i, (i + k * parts) % devices) for i in range(devices)]
        return lax.ppermute(value, "node", pairs)

    def along_y(value):
        return lax.ppermute(value, "node", [(i, i ^ 2) for i in range(devices)])

    def along_core(value):
        return lax.ppermute(value, "node", [(i, i ^ 1) for i in range(devices)])

    buckets = pack(placement, expert_ids, tokens, n_blocks, parts)
    straight = [buckets[0]] + [along_z(buckets[k], k) for k in range(1, n_blocks)]
    across = [along_y(piece) for piece in straight]
    mine = [piece for pair in zip(straight, across) for piece in pair]
    theirs = [along_core(piece) for piece in mine]
    outs = run_experts(mine + theirs, gate_weight, up_weight, down_weight)
    kept = outs[: len(mine)]
    returned = [along_core(piece) for piece in outs[len(mine) :]]
    results = []
    for k in range(n_blocks):
        back = along_y(add(kept[2 * k + 1], returned[2 * k + 1]))
        home = add(kept[2 * k], returned[2 * k], back)
        results.append(along_z(home, -k) if k else home)
    return mix(placement, expert_ids, gates, results, n_blocks, parts)


def solution(mesh):
    placed = (
        P(("group", "node"), None),
        P(("group", "node"), None),
        P(("group", "node"), None),
        P(),
        P(None, "node"),
        P(None, "node"),
        P("node", None),
    )
    return jax.shard_map(
        local, mesh=mesh, in_specs=placed, out_specs=P(("group", "node"), None), check_vma=False
    )
```

```python
import functools

import jax
import jax.numpy as jnp
from jax import lax
from jax.experimental import pallas as pl
from jax.experimental.pallas import tpu as pltpu
from jax.sharding import PartitionSpec as P

VMEM_BYTES = 24 * 2**20
VMEM = pl.BlockSpec(memory_space=pltpu.VMEM)
SMEM = pl.BlockSpec(memory_space=pltpu.SMEM)
ANYWHERE = pl.BlockSpec(memory_space=pl.ANY)
LOADS = 4


def in_vmem(value):
    return pltpu.with_memory_space_constraint(value, pltpu.VMEM)


def product(lhs, rhs):
    return jnp.dot(lhs, rhs, preferred_element_type=jnp.float32)


def slots_of(ids, n_blocks):
    top, rows = ids.shape
    experts = lax.broadcasted_iota(jnp.int32, (n_blocks, rows), 0)
    picks = jnp.zeros((n_blocks, rows), jnp.float32)
    for k in range(top):
        picks = picks + jnp.where(ids[k : k + 1, :] == experts, 1.0, 0.0)
    before = lax.broadcasted_iota(jnp.int32, (rows, rows), 0) < lax.broadcasted_iota(
        jnp.int32, (rows, rows), 1
    )
    earlier = product(picks.astype(jnp.bfloat16), jnp.where(before, 1.0, 0.0).astype(jnp.bfloat16))
    return experts, picks, earlier


def expert_at(placement_ref, block):
    found = jnp.int32(0)
    for e in range(placement_ref.shape[0]):
        found = jnp.where(placement_ref[e] == block, jnp.int32(e), found)
    return found


def row_of(values, experts, expert):
    return jnp.sum(jnp.where(experts == expert, values, 0.0), axis=0, keepdims=True)


def bucket_rows(rows):
    row = lax.broadcasted_iota(jnp.int32, (rows, rows), 0)
    half, quarter = rows // 2, rows // 4
    return jnp.where(row < half, row, half + row % quarter).astype(jnp.float32)


def pack_kernel(n_blocks, parts, placement_ref, ids_ref, tokens_ref, *out_refs):
    rows, width = tokens_ref.shape
    half, quarter = rows // 2, rows // 4
    block = lax.axis_index("node") // parts
    experts, picks, earlier = slots_of(ids_ref[...], n_blocks)
    wanted = bucket_rows(rows)
    upper = lax.broadcasted_iota(jnp.int32, (half, width // 2), 0) < quarter
    for k, out_ref in enumerate(out_refs):
        expert = expert_at(placement_ref, lax.rem(block + k, n_blocks))
        named = row_of(picks, experts, expert) > 0.5
        slot = row_of(earlier, experts, expert)
        chooser = jnp.where(named & (slot == wanted), 1.0, 0.0).astype(jnp.bfloat16)
        packed = product(chooser, tokens_ref[...])
        out_ref[:, :width] = packed[:half].astype(jnp.bfloat16)
        rest = jnp.where(upper, packed[half:, : width // 2], packed[half:, width // 2 :])
        out_ref[:, width:] = rest.astype(jnp.bfloat16)


def pack(placement, ids, tokens, n_blocks, parts):
    rows, width = tokens.shape
    shape = pltpu.VMEM((rows // 2, width + width // 2), jnp.bfloat16)
    return pl.pallas_call(
        functools.partial(pack_kernel, n_blocks, parts),
        out_shape=[shape] * n_blocks,
        in_specs=[SMEM, VMEM, VMEM],
        out_specs=[VMEM] * n_blocks,
        compiler_params=pltpu.CompilerParams(vmem_limit_bytes=VMEM_BYTES),
        cost_estimate=pl.CostEstimate(
            flops=2 * n_blocks * rows * rows * width,
            bytes_accessed=2 * (n_blocks + 1) * rows * width,
            transcendentals=0,
        ),
    )(placement, ids, tokens)


def load_kernel(*refs):
    sources, targets, sems = refs[:3], refs[4:7], refs[7]
    copies = []
    for i, (source, target) in enumerate(zip(sources, targets)):
        rows = source.shape[0] // LOADS
        for j in range(LOADS):
            part = pl.ds(j * rows, rows)
            copies.append(pltpu.make_async_copy(source.at[part], target.at[part], sems.at[i, j]))
    for copy in copies:
        copy.start()
    for copy in copies:
        copy.wait()


def load(weights, after):
    return pl.pallas_call(
        load_kernel,
        out_shape=[pltpu.VMEM(w.shape, w.dtype) for w in weights],
        in_specs=[pl.BlockSpec(memory_space=pltpu.HBM)] * 3 + [ANYWHERE],
        out_specs=[VMEM] * 3,
        scratch_shapes=[pltpu.SemaphoreType.DMA((3, LOADS))],
        compiler_params=pltpu.CompilerParams(vmem_limit_bytes=VMEM_BYTES),
        cost_estimate=pl.CostEstimate(
            flops=0, bytes_accessed=0, transcendentals=0
        ),
    )(*[pltpu.with_memory_space_constraint(w, pltpu.HBM) for w in weights], after)


def experts_kernel(*refs):
    straight_ref, across_ref, straight_other_ref, across_other_ref = refs[:4]
    gate_ref, up_ref, down_ref = refs[4:7]
    kept_ref, sent_ref = refs[-2:]
    pieces = (straight_ref, across_ref, straight_other_ref, across_other_ref)
    width, hid = gate_ref.shape
    middle = width // 2
    height = straight_ref.shape[0]
    total = len(pieces) * height
    rest = jnp.concatenate([p[:, width:] for p in pieces], axis=0)
    left = jnp.concatenate([p[:, :middle] for p in pieces] + [rest], axis=0)
    right = jnp.concatenate([p[:, middle:width] for p in pieces] + [rest], axis=0)
    upper = lax.broadcasted_iota(jnp.int32, (total, 1), 0) % height < height // 2
    shift = height // 2

    def whole_rows(ref):
        a, b = product(left, ref[:middle, :]), product(right, ref[middle:, :])
        tail = jnp.where(
            upper,
            a[total:] + pltpu.roll(b[total:], total - shift, axis=0),
            b[total:] + pltpu.roll(a[total:], shift, axis=0),
        )
        return jnp.concatenate([a[:total] + b[:total], tail], axis=0)

    gate_rows, up_rows = whole_rows(gate_ref), whole_rows(up_ref)
    hidden = (jax.nn.silu(gate_rows) * up_rows).astype(jnp.bfloat16)

    def store(start, values):
        values = values.astype(jnp.bfloat16)
        stop = start + values.shape[1]
        kept_ref[:, start:stop] = values[: 2 * height]
        sent_ref[:, start:stop] = values[2 * height :]

    step = middle // 4
    for i in range(4):
        begin = i * step
        a = product(hidden, down_ref[:, begin : begin + step])
        b = product(hidden, down_ref[:, middle + begin : middle + begin + step])
        store(begin, a[:total])
        store(middle + begin, b[:total])
        store(width + begin, jnp.where(upper, a[total:], b[total:]))


def run_experts(pieces, weights, after):
    width, hid = weights[0].shape
    height, packed_width = pieces[0].shape
    rows = len(pieces) * height
    shape = pltpu.VMEM((rows // 2, packed_width), jnp.bfloat16)
    operands = [in_vmem(p) for p in pieces] + [in_vmem(w) for w in weights]
    return pl.pallas_call(
        experts_kernel,
        out_shape=[shape] * 2,
        in_specs=[VMEM] * 7 + [ANYWHERE] * len(after),
        out_specs=[VMEM] * 2,
        compiler_params=pltpu.CompilerParams(vmem_limit_bytes=VMEM_BYTES),
        cost_estimate=pl.CostEstimate(
            flops=0, bytes_accessed=0, transcendentals=0
        ),
    )(*operands, *after)


def mix_kernel(n_blocks, parts, placement_ref, ids_ref, gates_ref, *refs):
    results, out_ref = refs[:-1], refs[-1]
    rows, width = out_ref.shape
    half, quarter, middle = rows // 2, rows // 4, width // 2
    block = lax.axis_index("node") // parts
    ids, gates = ids_ref[...], gates_ref[...]
    experts, picks, earlier = slots_of(ids, n_blocks)
    wanted = bucket_rows(rows)
    terms = []
    for k in range(n_blocks):
        expert = expert_at(placement_ref, lax.rem(block + k, n_blocks))
        named = row_of(picks, experts, expert) > 0.5
        slot = row_of(earlier, experts, expert)
        weight = jnp.sum(jnp.where(ids == expert, gates, 0.0), axis=0, keepdims=True)
        terms.append(jnp.where(named & (slot == wanted), weight, 0.0))
    term = jnp.concatenate(terms, axis=0)
    row = lax.broadcasted_iota(jnp.int32, term.shape, 0) % rows
    rest = jnp.concatenate([r[:, width:] for r in results], axis=0)
    for side in range(2):
        first = half + side * quarter
        mine = jnp.where((row < half) | ((row >= first) & (row < first + quarter)), term, 0.0)
        high = mine.astype(jnp.bfloat16)
        lower = mine - high.astype(jnp.float32)
        mid = lower.astype(jnp.bfloat16)
        low = (lower - mid.astype(jnp.float32)).astype(jnp.bfloat16)
        lhs = jnp.concatenate([high, mid, low], axis=1)
        pieces = []
        for r in results:
            pieces += [r[:, side * middle : (side + 1) * middle], r[:, width:]]
        rhs = jnp.concatenate(pieces, axis=0)
        value = lax.dot_general(
            lhs, rhs, (((0,), (0,)), ((), ())), preferred_element_type=jnp.float32
        )
        value = value[:rows] + value[rows : 2 * rows] + value[2 * rows :]
        out_ref[:, side * middle : (side + 1) * middle] = value.astype(jnp.bfloat16)


def mix(placement, ids, gates, results, n_blocks, parts):
    rows = ids.shape[1]
    width = results[0].shape[1] // 3 * 2
    return pl.pallas_call(
        functools.partial(mix_kernel, n_blocks, parts),
        out_shape=jax.ShapeDtypeStruct((rows, width), jnp.bfloat16),
        in_specs=[SMEM] + [VMEM] * (2 + n_blocks),
        out_specs=VMEM,
        compiler_params=pltpu.CompilerParams(vmem_limit_bytes=VMEM_BYTES),
        cost_estimate=pl.CostEstimate(
            flops=6 * n_blocks * rows * rows * width,
            bytes_accessed=2 * (n_blocks + 1) * rows * width,
            transcendentals=0,
        ),
    )(placement, ids, gates, *[in_vmem(r) for r in results])


def add(*values):
    return sum(v.astype(jnp.float32) for v in values).astype(jnp.bfloat16)


def local(tokens, expert_ids, gates, placement, gate_weight, up_weight, down_weight):
    n_blocks = placement.shape[0]
    devices = lax.axis_size("node")
    parts = devices // n_blocks
    half = tokens.shape[0] // 2

    def along_z(value, k):
        pairs = [(i, (i + k * parts) % devices) for i in range(devices)]
        return lax.ppermute(value, "node", pairs)

    def along_y(value):
        return lax.ppermute(value, "node", [(i, i ^ 2) for i in range(devices)])

    def along_core(value):
        return lax.ppermute(value, "node", [(i, i ^ 1) for i in range(devices)])

    order = sorted(range(n_blocks), key=lambda k: (min(k, n_blocks - k), k))
    ids = expert_ids.T
    buckets = pack(placement, ids, tokens, n_blocks, parts)
    across, straight = {0: along_y(buckets[0])}, {0: buckets[0]}
    for k in order[1:]:
        straight[k] = along_z(buckets[k], k)
    weights = load((gate_weight, up_weight, down_weight), buckets[0])
    results = [None] * n_blocks
    after = []
    for k in order:
        if k:
            across[k] = along_y(straight[k])
        pieces = [straight[k], across[k], along_core(straight[k]), along_core(across[k])]
        kept, sent = run_experts(pieces, weights, after)
        returned = along_core(sent)
        both = add(kept[half:], returned[half:])
        after = [both]
        back = along_y(both)
        home = add(kept[:half], returned[:half], back)
        results[k] = along_z(home, -k) if k else home
    return mix(placement, ids, gates.T, results, n_blocks, parts)


def solution(mesh):
    placed = (
        P(("group", "node"), None),
        P(("group", "node"), None),
        P(("group", "node"), None),
        P(),
        P(None, "node"),
        P(None, "node"),
        P("node", None),
    )
    return jax.shard_map(
        local, mesh=mesh, in_specs=placed, out_specs=P(("group", "node"), None), check_vma=False
    )
```

```python
import functools

import jax
import jax.numpy as jnp
from jax import lax
from jax.experimental import pallas as pl
from jax.experimental.pallas import tpu as pltpu
from jax.sharding import PartitionSpec as P

VMEM_BYTES = 24 * 2**20
VMEM = pl.BlockSpec(memory_space=pltpu.VMEM)
SMEM = pl.BlockSpec(memory_space=pltpu.SMEM)
ANYWHERE = pl.BlockSpec(memory_space=pl.ANY)
LOADS = 4
NO_COST = pl.CostEstimate(flops=0, bytes_accessed=0, transcendentals=0)


def in_vmem(value):
    return pltpu.with_memory_space_constraint(value, pltpu.VMEM)


def in_hbm(value):
    return pltpu.with_memory_space_constraint(value, pltpu.HBM)


def product(lhs, rhs):
    return jnp.dot(lhs, rhs, preferred_element_type=jnp.float32)


def slots_of(ids, n_blocks):
    top, rows = ids.shape
    experts = lax.broadcasted_iota(jnp.int32, (n_blocks, rows), 0)
    picks = jnp.zeros((n_blocks, rows), jnp.float32)
    for k in range(top):
        picks = picks + jnp.where(ids[k : k + 1, :] == experts, 1.0, 0.0)
    before = lax.broadcasted_iota(jnp.int32, (rows, rows), 0) < lax.broadcasted_iota(
        jnp.int32, (rows, rows), 1
    )
    earlier = product(picks.astype(jnp.bfloat16), jnp.where(before, 1.0, 0.0).astype(jnp.bfloat16))
    return experts, picks, earlier


def expert_at(placement_ref, block):
    found = jnp.int32(0)
    for e in range(placement_ref.shape[0]):
        found = jnp.where(placement_ref[e] == block, jnp.int32(e), found)
    return found


def row_of(values, experts, expert):
    return jnp.sum(jnp.where(experts == expert, values, 0.0), axis=0, keepdims=True)


def bucket_rows(rows):
    row = lax.broadcasted_iota(jnp.int32, (rows, rows), 0)
    half, quarter = rows // 2, rows // 4
    return jnp.where(row < half, row, half + row % quarter).astype(jnp.float32)


def pack_kernel(n_blocks, parts, distances, placement_ref, ids_ref, tokens_ref, *refs):
    rows, width = tokens_ref.shape
    half, quarter = rows // 2, rows // 4
    block = lax.axis_index("node") // parts
    experts, picks, earlier = slots_of(ids_ref[...], n_blocks)
    wanted = bucket_rows(rows)
    upper = lax.broadcasted_iota(jnp.int32, (half, width // 2), 0) < quarter
    for k, out_ref in zip(distances, refs[-len(distances) :]):
        expert = expert_at(placement_ref, lax.rem(block + k, n_blocks))
        named = row_of(picks, experts, expert) > 0.5
        slot = row_of(earlier, experts, expert)
        chooser = jnp.where(named & (slot == wanted), 1.0, 0.0).astype(jnp.bfloat16)
        packed = product(chooser, tokens_ref[...])
        out_ref[:, :width] = packed[:half].astype(jnp.bfloat16)
        rest = jnp.where(upper, packed[half:, : width // 2], packed[half:, width // 2 :])
        out_ref[:, width:] = rest.astype(jnp.bfloat16)


def pack(placement, ids, tokens, n_blocks, parts, distances, after):
    rows, width = tokens.shape
    shape = pltpu.VMEM((rows // 2, width + width // 2), jnp.bfloat16)
    out = pl.pallas_call(
        functools.partial(pack_kernel, n_blocks, parts, distances),
        out_shape=[shape] * len(distances),
        in_specs=[SMEM, VMEM, VMEM] + [ANYWHERE] * len(after),
        out_specs=[VMEM] * len(distances),
        compiler_params=pltpu.CompilerParams(vmem_limit_bytes=VMEM_BYTES),
        cost_estimate=NO_COST,
    )(in_hbm(placement), in_hbm(ids), in_hbm(tokens), *after)
    return dict(zip(distances, out))


def nothing(*refs):
    pass


def when(value, after):
    return pl.pallas_call(
        nothing,
        out_shape=pltpu.VMEM(value.shape, value.dtype),
        in_specs=[ANYWHERE] * (1 + len(after)),
        out_specs=ANYWHERE,
        input_output_aliases={0: 0},
        compiler_params=pltpu.CompilerParams(vmem_limit_bytes=VMEM_BYTES),
        cost_estimate=NO_COST,
    )(in_vmem(value), *after)


def load_kernel(*refs):
    sources, targets, sems = refs[:3], refs[4:7], refs[7]
    copies = []
    for i, (source, target) in enumerate(zip(sources, targets)):
        rows = source.shape[0] // LOADS
        for j in range(LOADS):
            part = pl.ds(j * rows, rows)
            copies.append(pltpu.make_async_copy(source.at[part], target.at[part], sems.at[i, j]))
    for copy in copies:
        copy.start()
    for copy in copies:
        copy.wait()


def load(weights, after):
    return pl.pallas_call(
        load_kernel,
        out_shape=[pltpu.VMEM(w.shape, w.dtype) for w in weights],
        in_specs=[pl.BlockSpec(memory_space=pltpu.HBM)] * 3 + [ANYWHERE],
        out_specs=[VMEM] * 3,
        scratch_shapes=[pltpu.SemaphoreType.DMA((3, LOADS))],
        compiler_params=pltpu.CompilerParams(vmem_limit_bytes=VMEM_BYTES),
        cost_estimate=NO_COST,
    )(*[pltpu.with_memory_space_constraint(w, pltpu.HBM) for w in weights], after)


def experts_kernel(*refs):
    straight_ref, across_ref, straight_other_ref, across_other_ref = refs[:4]
    gate_ref, up_ref, down_ref = refs[4:7]
    kept_ref, sent_ref = refs[-2:]
    pieces = (straight_ref, across_ref, straight_other_ref, across_other_ref)
    width, hid = gate_ref.shape
    middle = width // 2
    height = straight_ref.shape[0]
    total = len(pieces) * height
    rest = jnp.concatenate([p[:, width:] for p in pieces], axis=0)
    left = jnp.concatenate([p[:, :middle] for p in pieces] + [rest], axis=0)
    right = jnp.concatenate([p[:, middle:width] for p in pieces] + [rest], axis=0)
    upper = lax.broadcasted_iota(jnp.int32, (total, 1), 0) % height < height // 2
    shift = height // 2

    def whole_rows(ref):
        a, b = product(left, ref[:middle, :]), product(right, ref[middle:, :])
        tail = jnp.where(
            upper,
            a[total:] + pltpu.roll(b[total:], total - shift, axis=0),
            b[total:] + pltpu.roll(a[total:], shift, axis=0),
        )
        return jnp.concatenate([a[:total] + b[:total], tail], axis=0)

    gate_rows, up_rows = whole_rows(gate_ref), whole_rows(up_ref)
    hidden = (jax.nn.silu(gate_rows) * up_rows).astype(jnp.bfloat16)

    def store(start, values):
        values = values.astype(jnp.bfloat16)
        stop = start + values.shape[1]
        kept_ref[:, start:stop] = values[: 2 * height]
        sent_ref[:, start:stop] = values[2 * height :]

    step = middle // 4
    for i in range(4):
        begin = i * step
        a = product(hidden, down_ref[:, begin : begin + step])
        b = product(hidden, down_ref[:, middle + begin : middle + begin + step])
        store(begin, a[:total])
        store(middle + begin, b[:total])
        store(width + begin, jnp.where(upper, a[total:], b[total:]))


def run_experts(pieces, weights, after):
    width, hid = weights[0].shape
    height, packed_width = pieces[0].shape
    rows = len(pieces) * height
    shape = pltpu.VMEM((rows // 2, packed_width), jnp.bfloat16)
    operands = [in_vmem(p) for p in pieces] + [in_vmem(w) for w in weights]
    return pl.pallas_call(
        experts_kernel,
        out_shape=[shape] * 2,
        in_specs=[VMEM] * 7 + [ANYWHERE] * len(after),
        out_specs=[VMEM] * 2,
        compiler_params=pltpu.CompilerParams(vmem_limit_bytes=VMEM_BYTES),
        cost_estimate=NO_COST,
    )(*operands, *after)


def mix_kernel(n_blocks, parts, placement_ref, ids_ref, gates_ref, *refs):
    results, out_ref = refs[:-1], refs[-1]
    rows, width = out_ref.shape
    half, quarter, middle = rows // 2, rows // 4, width // 2
    block = lax.axis_index("node") // parts
    ids, gates = ids_ref[...], gates_ref[...]
    experts, picks, earlier = slots_of(ids, n_blocks)
    wanted = bucket_rows(rows)
    terms = []
    for k in range(n_blocks):
        expert = expert_at(placement_ref, lax.rem(block + k, n_blocks))
        named = row_of(picks, experts, expert) > 0.5
        slot = row_of(earlier, experts, expert)
        weight = jnp.sum(jnp.where(ids == expert, gates, 0.0), axis=0, keepdims=True)
        terms.append(jnp.where(named & (slot == wanted), weight, 0.0))
    term = jnp.concatenate(terms, axis=0)
    row = lax.broadcasted_iota(jnp.int32, term.shape, 0) % rows
    rest = jnp.concatenate([r[:, width:] for r in results], axis=0)
    for side in range(2):
        first = half + side * quarter
        mine = jnp.where((row < half) | ((row >= first) & (row < first + quarter)), term, 0.0)
        high = mine.astype(jnp.bfloat16)
        lower = mine - high.astype(jnp.float32)
        mid = lower.astype(jnp.bfloat16)
        low = (lower - mid.astype(jnp.float32)).astype(jnp.bfloat16)
        lhs = jnp.concatenate([high, mid, low], axis=1)
        pieces = []
        for r in results:
            pieces += [r[:, side * middle : (side + 1) * middle], r[:, width:]]
        rhs = jnp.concatenate(pieces, axis=0)
        value = lax.dot_general(
            lhs, rhs, (((0,), (0,)), ((), ())), preferred_element_type=jnp.float32
        )
        value = value[:rows] + value[rows : 2 * rows] + value[2 * rows :]
        out_ref[:, side * middle : (side + 1) * middle] = value.astype(jnp.bfloat16)


def mix(placement, ids, gates, results, n_blocks, parts):
    rows = ids.shape[1]
    width = results[0].shape[1] // 3 * 2
    return pl.pallas_call(
        functools.partial(mix_kernel, n_blocks, parts),
        out_shape=jax.ShapeDtypeStruct((rows, width), jnp.bfloat16),
        in_specs=[SMEM] + [VMEM] * (2 + n_blocks),
        out_specs=VMEM,
        compiler_params=pltpu.CompilerParams(vmem_limit_bytes=VMEM_BYTES),
        cost_estimate=pl.CostEstimate(
            flops=6 * n_blocks * rows * rows * width,
            bytes_accessed=2 * (n_blocks + 1) * rows * width,
            transcendentals=0,
        ),
    )(placement, ids, gates, *[in_vmem(r) for r in results])


def add(*values):
    return sum(v.astype(jnp.float32) for v in values).astype(jnp.bfloat16)


def local(tokens, expert_ids, gates, placement, gate_weight, up_weight, down_weight):
    n_blocks = placement.shape[0]
    devices = lax.axis_size("node")
    parts = devices // n_blocks
    half = tokens.shape[0] // 2

    def along_z(value, k):
        pairs = [(i, (i + k * parts) % devices) for i in range(devices)]
        return lax.ppermute(value, "node", pairs)

    def along_y(value):
        return lax.ppermute(value, "node", [(i, i ^ 2) for i in range(devices)])

    def along_core(value):
        return lax.ppermute(value, "node", [(i, i ^ 1) for i in range(devices)])

    ids = expert_ids.T
    groups = [sorted({d, n_blocks - d}) for d in range(1, n_blocks // 2 + 1)]
    buckets = pack(placement, ids, tokens, n_blocks, parts, [0] + groups[0], [])
    straight, across, theirs = {0: buckets[0]}, {0: along_y(buckets[0])}, {}
    results, both, home, kept, sent, returned = {}, {}, {}, {}, {}, {}
    for k in groups[0]:
        straight[k] = along_z(buckets[k], k)
    weights = load((gate_weight, up_weight, down_weight), buckets[0])

    def compute(k, after):
        theirs[k] = [along_core(straight[k]), along_core(across[k])]
        pieces = [straight[k], across[k]] + theirs[k]
        kept[k], sent[k] = run_experts(pieces, weights, after)
        returned[k] = along_core(sent[k])
        both[k] = add(kept[k][half:], returned[k][half:])

    def go_home(k, after):
        back = along_y(both[k] if k else when(both[k], after))
        home[k] = add(kept[k][:half], returned[k][:half], back)
        if k:
            value = when(home[k], after) if after else home[k]
            results[k] = along_z(value, -k)
        else:
            results[k] = home[k]

    compute(0, [])
    for g, group in enumerate(groups):
        if g:
            earlier = groups[g - 1]
            after = [straight[k] for k in earlier] + [across[0], weights[0]][: 2 if g == 1 else 0]
            buckets = pack(placement, ids, tokens, n_blocks, parts, group, after)
            after = [across[k] for k in earlier] + [both[earlier[0]]]
            for k in group:
                straight[k] = when(along_z(buckets[k], k), after)
        for k in group:
            across[k] = along_y(straight[k])
        if g:
            after = [home[earlier[0]]] + [both[k] for k in earlier[1:]]
        else:
            after = [sent[0]]
        for k in group:
            compute(k, after)
        for k in group:
            go_home(k, [results[earlier[0]]] if g else [])
    go_home(0, [home[groups[-1][-1]]])
    return mix(placement, ids, gates.T, [results[k] for k in range(n_blocks)], n_blocks, parts)


def solution(mesh):
    placed = (
        P(("group", "node"), None),
        P(("group", "node"), None),
        P(("group", "node"), None),
        P(),
        P(None, "node"),
        P(None, "node"),
        P("node", None),
    )
    return jax.shard_map(
        local, mesh=mesh, in_specs=placed, out_specs=P(("group", "node"), None), check_vma=False
    )
```

```python
import functools

import jax
import jax.numpy as jnp
from jax import lax
from jax.experimental import pallas as pl
from jax.experimental.pallas import tpu as pltpu
from jax.sharding import PartitionSpec as P

VMEM_BYTES = 24 * 2**20
VMEM = pl.BlockSpec(memory_space=pltpu.VMEM)
SMEM = pl.BlockSpec(memory_space=pltpu.SMEM)
ANYWHERE = pl.BlockSpec(memory_space=pl.ANY)
LOADS = 4
NO_COST = pl.CostEstimate(flops=0, bytes_accessed=0, transcendentals=0)


def in_vmem(value):
    return pltpu.with_memory_space_constraint(value, pltpu.VMEM)


def in_hbm(value):
    return pltpu.with_memory_space_constraint(value, pltpu.HBM)


def product(lhs, rhs):
    return jnp.dot(lhs, rhs, preferred_element_type=jnp.float32)


def slots_of(ids, n_blocks):
    top, rows = ids.shape
    experts = lax.broadcasted_iota(jnp.int32, (n_blocks, rows), 0)
    picks = jnp.zeros((n_blocks, rows), jnp.float32)
    for k in range(top):
        picks = picks + jnp.where(ids[k : k + 1, :] == experts, 1.0, 0.0)
    before = lax.broadcasted_iota(jnp.int32, (rows, rows), 0) < lax.broadcasted_iota(
        jnp.int32, (rows, rows), 1
    )
    earlier = product(picks.astype(jnp.bfloat16), jnp.where(before, 1.0, 0.0).astype(jnp.bfloat16))
    return experts, picks, earlier


def expert_at(placement_ref, block):
    found = jnp.int32(0)
    for e in range(placement_ref.shape[0]):
        found = jnp.where(placement_ref[e] == block, jnp.int32(e), found)
    return found


def row_of(values, experts, expert):
    return jnp.sum(jnp.where(experts == expert, values, 0.0), axis=0, keepdims=True)


def bucket_rows(rows):
    row = lax.broadcasted_iota(jnp.int32, (rows, rows), 0)
    half, quarter = rows // 2, rows // 4
    return jnp.where(row < half, row, half + row % quarter).astype(jnp.float32)


def pack_kernel(n_blocks, parts, distances, placement_ref, ids_ref, tokens_ref, *refs):
    rows, width = tokens_ref.shape
    half, quarter = rows // 2, rows // 4
    block = lax.axis_index("node") // parts
    experts, picks, earlier = slots_of(ids_ref[...], n_blocks)
    wanted = bucket_rows(rows)
    upper = lax.broadcasted_iota(jnp.int32, (half, width // 2), 0) < quarter
    for k, out_ref in zip(distances, refs[-len(distances) :]):
        expert = expert_at(placement_ref, lax.bitwise_xor(block, jnp.int32(k)))
        named = row_of(picks, experts, expert) > 0.5
        slot = row_of(earlier, experts, expert)
        chooser = jnp.where(named & (slot == wanted), 1.0, 0.0).astype(jnp.bfloat16)
        packed = product(chooser, tokens_ref[...])
        out_ref[:, :width] = packed[:half].astype(jnp.bfloat16)
        rest = jnp.where(upper, packed[half:, : width // 2], packed[half:, width // 2 :])
        out_ref[:, width:] = rest.astype(jnp.bfloat16)


def pack(placement, ids, tokens, n_blocks, parts, distances, after):
    rows, width = tokens.shape
    shape = pltpu.VMEM((rows // 2, width + width // 2), jnp.bfloat16)
    out = pl.pallas_call(
        functools.partial(pack_kernel, n_blocks, parts, distances),
        out_shape=[shape] * len(distances),
        in_specs=[SMEM, VMEM, VMEM] + [ANYWHERE] * len(after),
        out_specs=[VMEM] * len(distances),
        compiler_params=pltpu.CompilerParams(vmem_limit_bytes=VMEM_BYTES),
        cost_estimate=NO_COST,
    )(in_hbm(placement), in_hbm(ids), in_hbm(tokens), *after)
    return dict(zip(distances, out))


def nothing(*refs):
    pass


def when(value, after):
    if not after:
        return value
    return pl.pallas_call(
        nothing,
        out_shape=pltpu.VMEM(value.shape, value.dtype),
        in_specs=[ANYWHERE] * (1 + len(after)),
        out_specs=ANYWHERE,
        input_output_aliases={0: 0},
        compiler_params=pltpu.CompilerParams(vmem_limit_bytes=VMEM_BYTES),
        cost_estimate=NO_COST,
    )(in_vmem(value), *after)


def load_kernel(*refs):
    sources, targets, sems = refs[:3], refs[4:7], refs[7]
    copies = []
    for i, (source, target) in enumerate(zip(sources, targets)):
        rows = source.shape[0] // LOADS
        for j in range(LOADS):
            part = pl.ds(j * rows, rows)
            copies.append(pltpu.make_async_copy(source.at[part], target.at[part], sems.at[i, j]))
    for copy in copies:
        copy.start()
    for copy in copies:
        copy.wait()


def load(weights, after):
    return pl.pallas_call(
        load_kernel,
        out_shape=[pltpu.VMEM(w.shape, w.dtype) for w in weights],
        in_specs=[pl.BlockSpec(memory_space=pltpu.HBM)] * 3 + [ANYWHERE],
        out_specs=[VMEM] * 3,
        scratch_shapes=[pltpu.SemaphoreType.DMA((3, LOADS))],
        compiler_params=pltpu.CompilerParams(vmem_limit_bytes=VMEM_BYTES),
        cost_estimate=NO_COST,
    )(*[pltpu.with_memory_space_constraint(w, pltpu.HBM) for w in weights], after)


def experts_kernel(*refs):
    straight_ref, across_ref, straight_other_ref, across_other_ref = refs[:4]
    gate_ref, up_ref, down_ref = refs[4:7]
    kept_ref, sent_ref = refs[-2:]
    pieces = (straight_ref, across_ref, straight_other_ref, across_other_ref)
    width, hid = gate_ref.shape
    middle = width // 2
    height = straight_ref.shape[0]
    total = len(pieces) * height
    rest = jnp.concatenate([p[:, width:] for p in pieces], axis=0)
    left = jnp.concatenate([p[:, :middle] for p in pieces] + [rest], axis=0)
    right = jnp.concatenate([p[:, middle:width] for p in pieces] + [rest], axis=0)
    upper = lax.broadcasted_iota(jnp.int32, (total, 1), 0) % height < height // 2
    shift = height // 2

    def whole_rows(ref):
        a, b = product(left, ref[:middle, :]), product(right, ref[middle:, :])
        tail = jnp.where(
            upper,
            a[total:] + pltpu.roll(b[total:], total - shift, axis=0),
            b[total:] + pltpu.roll(a[total:], shift, axis=0),
        )
        return jnp.concatenate([a[:total] + b[:total], tail], axis=0)

    gate_rows, up_rows = whole_rows(gate_ref), whole_rows(up_ref)
    hidden = (jax.nn.silu(gate_rows) * up_rows).astype(jnp.bfloat16)

    def store(start, values):
        values = values.astype(jnp.bfloat16)
        stop = start + values.shape[1]
        kept_ref[:, start:stop] = values[: 2 * height]
        sent_ref[:, start:stop] = values[2 * height :]

    step = middle // 4
    for i in range(4):
        begin = i * step
        a = product(hidden, down_ref[:, begin : begin + step])
        b = product(hidden, down_ref[:, middle + begin : middle + begin + step])
        store(begin, a[:total])
        store(middle + begin, b[:total])
        store(width + begin, jnp.where(upper, a[total:], b[total:]))


def run_experts(pieces, weights, after):
    width, hid = weights[0].shape
    height, packed_width = pieces[0].shape
    rows = len(pieces) * height
    shape = pltpu.VMEM((rows // 2, packed_width), jnp.bfloat16)
    operands = [in_vmem(p) for p in pieces] + [in_vmem(w) for w in weights]
    return pl.pallas_call(
        experts_kernel,
        out_shape=[shape] * 2,
        in_specs=[VMEM] * 7 + [ANYWHERE] * len(after),
        out_specs=[VMEM] * 2,
        compiler_params=pltpu.CompilerParams(vmem_limit_bytes=VMEM_BYTES),
        cost_estimate=pl.CostEstimate(
            flops=0, bytes_accessed=4 * width * hid, transcendentals=0
        ),
    )(*operands, *after)


def mix_kernel(n_blocks, parts, placement_ref, ids_ref, gates_ref, *refs):
    results, out_ref = refs[:-1], refs[-1]
    rows, width = out_ref.shape
    half, quarter, middle = rows // 2, rows // 4, width // 2
    block = lax.axis_index("node") // parts
    ids, gates = ids_ref[...], gates_ref[...]
    experts, picks, earlier = slots_of(ids, n_blocks)
    wanted = bucket_rows(rows)
    terms = []
    for k in range(n_blocks):
        expert = expert_at(placement_ref, lax.bitwise_xor(block, jnp.int32(k)))
        named = row_of(picks, experts, expert) > 0.5
        slot = row_of(earlier, experts, expert)
        weight = jnp.sum(jnp.where(ids == expert, gates, 0.0), axis=0, keepdims=True)
        terms.append(jnp.where(named & (slot == wanted), weight, 0.0))
    term = jnp.concatenate(terms, axis=0)
    row = lax.broadcasted_iota(jnp.int32, term.shape, 0) % rows
    rest = jnp.concatenate([r[:, width:] for r in results], axis=0)
    for side in range(2):
        first = half + side * quarter
        mine = jnp.where((row < half) | ((row >= first) & (row < first + quarter)), term, 0.0)
        high = mine.astype(jnp.bfloat16)
        lower = mine - high.astype(jnp.float32)
        mid = lower.astype(jnp.bfloat16)
        low = (lower - mid.astype(jnp.float32)).astype(jnp.bfloat16)
        lhs = jnp.concatenate([high, mid, low], axis=1)
        pieces = []
        for r in results:
            pieces += [r[:, side * middle : (side + 1) * middle], r[:, width:]]
        rhs = jnp.concatenate(pieces, axis=0)
        value = lax.dot_general(
            lhs, rhs, (((0,), (0,)), ((), ())), preferred_element_type=jnp.float32
        )
        value = value[:rows] + value[rows : 2 * rows] + value[2 * rows :]
        out_ref[:, side * middle : (side + 1) * middle] = value.astype(jnp.bfloat16)


def mix(placement, ids, gates, results, n_blocks, parts):
    rows = ids.shape[1]
    width = results[0].shape[1] // 3 * 2
    return pl.pallas_call(
        functools.partial(mix_kernel, n_blocks, parts),
        out_shape=jax.ShapeDtypeStruct((rows, width), jnp.bfloat16),
        in_specs=[SMEM] + [VMEM] * (2 + n_blocks),
        out_specs=VMEM,
        compiler_params=pltpu.CompilerParams(vmem_limit_bytes=VMEM_BYTES),
        cost_estimate=pl.CostEstimate(
            flops=6 * n_blocks * rows * rows * width,
            bytes_accessed=2 * (n_blocks + 1) * rows * width,
            transcendentals=0,
        ),
    )(placement, ids, gates, *[in_vmem(r) for r in results])


def add(*values):
    return sum(v.astype(jnp.float32) for v in values).astype(jnp.bfloat16)


def local(tokens, expert_ids, gates, placement, gate_weight, up_weight, down_weight):
    n_blocks = placement.shape[0]
    devices = lax.axis_size("node")
    parts = devices // n_blocks
    half = tokens.shape[0] // 2

    def along_z(value, k):
        pairs = [(i, i ^ (k * parts)) for i in range(devices)]
        return lax.ppermute(value, "node", pairs)

    def along_y(value):
        return lax.ppermute(value, "node", [(i, i ^ 2) for i in range(devices)])

    def along_core(value):
        return lax.ppermute(value, "node", [(i, i ^ 1) for i in range(devices)])

    ids = expert_ids.T
    groups = [[n_blocks - d, d] for d in range(1, n_blocks // 2)] + [[n_blocks // 2]]
    last = groups[-1][0]
    straight, arrived, across, results = {}, {}, {}, {}
    both, home, kept, sent, returned = {}, {}, {}, {}, {}

    def compute(k, after):
        theirs = [along_core(straight[k]), along_core(across[k])]
        kept[k], sent[k] = run_experts([straight[k], across[k]] + theirs, weights, after)
        returned[k] = along_core(sent[k])
        both[k] = add(kept[k][half:], returned[k][half:])

    def go_home(k, after_y, after_z):
        back = along_y(when(both[k], after_y))
        home[k] = add(kept[k][:half], returned[k][:half], back)
        results[k] = along_z(when(home[k], after_z), k) if k else home[k]

    for g, group in enumerate(groups):
        members = [0] + group if g == 0 else group
        after = [arrived[k] for k in groups[g - 1]] + [weights[0]] if g else []
        buckets = pack(placement, ids, tokens, n_blocks, parts, members, after)
        if g == 0:
            straight[0] = buckets[0]
            across[0] = along_y(straight[0])
            weights = load((gate_weight, up_weight, down_weight), buckets[0])
        for k in group:
            straight[k] = arrived[k] = along_z(buckets[k], k)
        if g == 0:
            compute(0, [])
        for i, k in enumerate(group):
            across[k] = along_y(straight[k])
            compute(k, [both[j] for j in groups[g - 1]] if g else [sent[0]][:i])
            go_home(k, [], [results[j] for j in groups[g - 1]] if g else [])
    go_home(0, [home[last]], [])
    return mix(placement, ids, gates.T, [results[k] for k in range(n_blocks)], n_blocks, parts)


def solution(mesh):
    placed = (
        P(("group", "node"), None),
        P(("group", "node"), None),
        P(("group", "node"), None),
        P(),
        P(None, "node"),
        P(None, "node"),
        P("node", None),
    )
    return jax.shard_map(
        local, mesh=mesh, in_specs=placed, out_specs=P(("group", "node"), None), check_vma=False
    )
```

```python
import functools

import jax
import jax.numpy as jnp
from jax import lax
from jax.experimental import pallas as pl
from jax.experimental.pallas import tpu as pltpu
from jax.sharding import PartitionSpec as P

VMEM_BYTES = 24 * 2**20
VMEM = pl.BlockSpec(memory_space=pltpu.VMEM)
SMEM = pl.BlockSpec(memory_space=pltpu.SMEM)
ANYWHERE = pl.BlockSpec(memory_space=pl.ANY)
LOADS = 4
N1, N2, N3, N4 = 30,30,30,30
NO_COST = pl.CostEstimate(flops=0, bytes_accessed=0, transcendentals=0)


def in_vmem(value):
    return pltpu.with_memory_space_constraint(value, pltpu.VMEM)


def in_hbm(value):
    return pltpu.with_memory_space_constraint(value, pltpu.HBM)


def product(lhs, rhs):
    return jnp.dot(lhs, rhs, preferred_element_type=jnp.float32)


def slots_of(ids, n_blocks):
    top, rows = ids.shape
    experts = lax.broadcasted_iota(jnp.int32, (n_blocks, rows), 0)
    picks = jnp.zeros((n_blocks, rows), jnp.float32)
    for k in range(top):
        picks = picks + jnp.where(ids[k : k + 1, :] == experts, 1.0, 0.0)
    before = lax.broadcasted_iota(jnp.int32, (rows, rows), 0) < lax.broadcasted_iota(
        jnp.int32, (rows, rows), 1
    )
    earlier = product(picks.astype(jnp.bfloat16), jnp.where(before, 1.0, 0.0).astype(jnp.bfloat16))
    return experts, picks, earlier


def expert_at(placement_ref, block):
    found = jnp.int32(0)
    for e in range(placement_ref.shape[0]):
        found = jnp.where(placement_ref[e] == block, jnp.int32(e), found)
    return found


def row_of(values, experts, expert):
    return jnp.sum(jnp.where(experts == expert, values, 0.0), axis=0, keepdims=True)


def bucket_rows(rows):
    row = lax.broadcasted_iota(jnp.int32, (rows, rows), 0)
    half, quarter = rows // 2, rows // 4
    return jnp.where(row < half, row, half + row % quarter).astype(jnp.float32)


def pack_kernel(n_blocks, parts, placement_ref, ids_ref, tokens_ref, *out_refs):
    rows, width = tokens_ref.shape
    half, quarter = rows // 2, rows // 4
    block = lax.axis_index("node") // parts
    experts, picks, earlier = slots_of(ids_ref[...], n_blocks)
    wanted = bucket_rows(rows)
    upper = lax.broadcasted_iota(jnp.int32, (half, width // 2), 0) < quarter
    for k, out_ref in enumerate(out_refs):
        expert = expert_at(placement_ref, lax.bitwise_xor(block, jnp.int32(k)))
        named = row_of(picks, experts, expert) > 0.5
        slot = row_of(earlier, experts, expert)
        chooser = jnp.where(named & (slot == wanted), 1.0, 0.0).astype(jnp.bfloat16)
        packed = product(chooser, tokens_ref[...])
        out_ref[:, :width] = packed[:half].astype(jnp.bfloat16)
        rest = jnp.where(upper, packed[half:, : width // 2], packed[half:, width // 2 :])
        out_ref[:, width:] = rest.astype(jnp.bfloat16)


def pack(placement, ids, tokens, n_blocks, parts):
    rows, width = tokens.shape
    shape = pltpu.VMEM((rows // 2, width + width // 2), jnp.bfloat16)
    return pl.pallas_call(
        functools.partial(pack_kernel, n_blocks, parts),
        out_shape=[shape] * n_blocks,
        in_specs=[SMEM, VMEM, VMEM],
        out_specs=[VMEM] * n_blocks,
        compiler_params=pltpu.CompilerParams(vmem_limit_bytes=VMEM_BYTES),
        cost_estimate=NO_COST,
    )(in_hbm(placement), in_hbm(ids), in_hbm(tokens))


def nothing(*refs):
    pass


def when(value, after):
    if not after:
        return value
    return pl.pallas_call(
        nothing,
        out_shape=pltpu.VMEM(value.shape, value.dtype),
        in_specs=[ANYWHERE] * (1 + len(after)),
        out_specs=ANYWHERE,
        input_output_aliases={0: 0},
        compiler_params=pltpu.CompilerParams(vmem_limit_bytes=VMEM_BYTES),
        cost_estimate=NO_COST,
    )(in_vmem(value), *after)


def load_kernel(*refs):
    sources, targets, sems = refs[:3], refs[4:7], refs[7]
    copies = []
    for i, (source, target) in enumerate(zip(sources, targets)):
        rows = source.shape[0] // LOADS
        for j in range(LOADS):
            part = pl.ds(j * rows, rows)
            copies.append(pltpu.make_async_copy(source.at[part], target.at[part], sems.at[i, j]))
    for copy in copies:
        copy.start()
    for copy in copies:
        copy.wait()


def load(weights, after):
    return pl.pallas_call(
        load_kernel,
        out_shape=[pltpu.VMEM(w.shape, w.dtype) for w in weights],
        in_specs=[pl.BlockSpec(memory_space=pltpu.HBM)] * 3 + [ANYWHERE],
        out_specs=[VMEM] * 3,
        scratch_shapes=[pltpu.SemaphoreType.DMA((3, LOADS))],
        compiler_params=pltpu.CompilerParams(vmem_limit_bytes=VMEM_BYTES),
        cost_estimate=NO_COST,
    )(*[pltpu.with_memory_space_constraint(w, pltpu.HBM) for w in weights], after)


def experts_kernel(*refs):
    straight_ref, across_ref, straight_other_ref, across_other_ref = refs[:4]
    gate_ref, up_ref, down_ref = refs[4:7]
    kept_ref, sent_ref = refs[-2:]
    pieces = (straight_ref, across_ref, straight_other_ref, across_other_ref)
    width, hid = gate_ref.shape
    middle = width // 2
    height = straight_ref.shape[0]
    total = len(pieces) * height
    rest = jnp.concatenate([p[:, width:] for p in pieces], axis=0)
    left = jnp.concatenate([p[:, :middle] for p in pieces] + [rest], axis=0)
    right = jnp.concatenate([p[:, middle:width] for p in pieces] + [rest], axis=0)
    upper = lax.broadcasted_iota(jnp.int32, (total, 1), 0) % height < height // 2
    shift = height // 2

    def whole_rows(ref):
        a, b = product(left, ref[:middle, :]), product(right, ref[middle:, :])
        tail = jnp.where(
            upper,
            a[total:] + pltpu.roll(b[total:], total - shift, axis=0),
            b[total:] + pltpu.roll(a[total:], shift, axis=0),
        )
        return jnp.concatenate([a[:total] + b[:total], tail], axis=0)

    gate_rows, up_rows = whole_rows(gate_ref), whole_rows(up_ref)
    hidden = (jax.nn.silu(gate_rows) * up_rows).astype(jnp.bfloat16)

    def store(start, values):
        values = values.astype(jnp.bfloat16)
        stop = start + values.shape[1]
        kept_ref[:, start:stop] = values[: 2 * height]
        sent_ref[:, start:stop] = values[2 * height :]

    step = middle // 4
    for i in range(4):
        begin = i * step
        a = product(hidden, down_ref[:, begin : begin + step])
        b = product(hidden, down_ref[:, middle + begin : middle + begin + step])
        store(begin, a[:total])
        store(middle + begin, b[:total])
        store(width + begin, jnp.where(upper, a[total:], b[total:]))


def run_experts(pieces, weights, after):
    width, hid = weights[0].shape
    height, packed_width = pieces[0].shape
    rows = len(pieces) * height
    shape = pltpu.VMEM((rows // 2, packed_width), jnp.bfloat16)
    operands = [in_vmem(p) for p in pieces] + [in_vmem(w) for w in weights]
    return pl.pallas_call(
        experts_kernel,
        out_shape=[shape] * 2,
        in_specs=[VMEM] * 7 + [ANYWHERE] * len(after),
        out_specs=[VMEM] * 2,
        compiler_params=pltpu.CompilerParams(vmem_limit_bytes=VMEM_BYTES),
        cost_estimate=pl.CostEstimate(
            flops=0, bytes_accessed=4 * width * hid, transcendentals=0
        ),
    )(*operands, *after)


def mix_kernel(n_blocks, parts, placement_ref, ids_ref, gates_ref, *refs):
    results, out_ref = refs[:-1], refs[-1]
    rows, width = out_ref.shape
    half, quarter, middle = rows // 2, rows // 4, width // 2
    block = lax.axis_index("node") // parts
    ids, gates = ids_ref[...], gates_ref[...]
    experts, picks, earlier = slots_of(ids, n_blocks)
    wanted = bucket_rows(rows)
    terms = []
    for k in range(n_blocks):
        expert = expert_at(placement_ref, lax.bitwise_xor(block, jnp.int32(k)))
        named = row_of(picks, experts, expert) > 0.5
        slot = row_of(earlier, experts, expert)
        weight = jnp.sum(jnp.where(ids == expert, gates, 0.0), axis=0, keepdims=True)
        terms.append(jnp.where(named & (slot == wanted), weight, 0.0))
    term = jnp.concatenate(terms, axis=0)
    row = lax.broadcasted_iota(jnp.int32, term.shape, 0) % rows
    rest = jnp.concatenate([r[:, width:] for r in results], axis=0)
    for side in range(2):
        first = half + side * quarter
        mine = jnp.where((row < half) | ((row >= first) & (row < first + quarter)), term, 0.0)
        high = mine.astype(jnp.bfloat16)
        lower = mine - high.astype(jnp.float32)
        mid = lower.astype(jnp.bfloat16)
        low = (lower - mid.astype(jnp.float32)).astype(jnp.bfloat16)
        lhs = jnp.concatenate([high, mid, low], axis=1)
        pieces = []
        for r in results:
            pieces += [r[:, side * middle : (side + 1) * middle], r[:, width:]]
        rhs = jnp.concatenate(pieces, axis=0)
        value = lax.dot_general(
            lhs, rhs, (((0,), (0,)), ((), ())), preferred_element_type=jnp.float32
        )
        value = value[:rows] + value[rows : 2 * rows] + value[2 * rows :]
        out_ref[:, side * middle : (side + 1) * middle] = value.astype(jnp.bfloat16)


def mix(placement, ids, gates, results, n_blocks, parts):
    rows = ids.shape[1]
    width = results[0].shape[1] // 3 * 2
    return pl.pallas_call(
        functools.partial(mix_kernel, n_blocks, parts),
        out_shape=jax.ShapeDtypeStruct((rows, width), jnp.bfloat16),
        in_specs=[SMEM] + [VMEM] * (2 + n_blocks),
        out_specs=VMEM,
        compiler_params=pltpu.CompilerParams(vmem_limit_bytes=VMEM_BYTES),
        cost_estimate=pl.CostEstimate(
            flops=6 * n_blocks * rows * rows * width,
            bytes_accessed=2 * (n_blocks + 1) * rows * width,
            transcendentals=0,
        ),
    )(placement, ids, gates, *[in_vmem(r) for r in results])


def add(*values):
    return sum(v.astype(jnp.float32) for v in values).astype(jnp.bfloat16)


def local(tokens, expert_ids, gates, placement, gate_weight, up_weight, down_weight):
    n_blocks = placement.shape[0]
    devices = lax.axis_size("node")
    parts = devices // n_blocks
    half = tokens.shape[0] // 2

    def along_z(value, k):
        pairs = [(i, i ^ (k * parts)) for i in range(devices)]
        return lax.ppermute(value, "node", pairs)

    def along_y(value):
        return lax.ppermute(value, "node", [(i, i ^ 2) for i in range(devices)])

    def along_core(value):
        return lax.ppermute(value, "node", [(i, i ^ 1) for i in range(devices)])

    ids = expert_ids.T
    groups = [[n_blocks - d, d] for d in range(1, n_blocks // 2)] + [[n_blocks // 2]]
    last = groups[-1][0]
    straight, arrived, across, results = {}, {}, {}, {}
    both, home, kept, sent, returned = {}, {}, {}, {}, {}

    def compute(k, after):
        theirs = [along_core(straight[k]), along_core(across[k])]
        kept[k], sent[k] = run_experts([straight[k], across[k]] + theirs, weights, after)
        returned[k] = along_core(sent[k])
        both[k] = add(kept[k][half:], returned[k][half:])

    def go_home(k, after_y, after_z):
        back = along_y(when(both[k], after_y))
        home[k] = add(kept[k][:half], returned[k][:half], back)
        results[k] = along_z(when(home[k], after_z), k) if k else home[k]

    buckets = list(pack(placement, ids, tokens, n_blocks, parts))
    straight[0] = buckets[0]
    across[0] = along_y(straight[0])
    for g, group in enumerate(groups):
        previous = groups[g - 1] if g else []
        if g:
            after = [arrived[k] for k in previous] + [across[0]]
            for k in group:
                buckets[k] = when(buckets[k], after)
        for k in group:
            straight[k] = arrived[k] = along_z(buckets[k], k)
    for k in groups[0]:
        across[k] = along_y(straight[k])
    weights = load((gate_weight, up_weight, down_weight), across[groups[0][0]])
    compute(0, [])
    for g, group in enumerate(groups):
        previous = groups[g - 1] if g else []
        for i, k in enumerate(group):
            if g:
                across[k] = along_y(straight[k])
            compute(k, [both[j] for j in previous] if g else [sent[0]][:i])
            go_home(k, [], [results[j] for j in previous])
    go_home(0, [home[last]], [])
    return mix(placement, ids, gates.T, [results[k] for k in range(n_blocks)], n_blocks, parts)


def solution(mesh):
    placed = (
        P(("group", "node"), None),
        P(("group", "node"), None),
        P(("group", "node"), None),
        P(),
        P(None, "node"),
        P(None, "node"),
        P("node", None),
    )
    return jax.shard_map(
        local, mesh=mesh, in_specs=placed, out_specs=P(("group", "node"), None), check_vma=False
    )
```

```python
import functools

import jax
import jax.numpy as jnp
from jax import lax
from jax.experimental import pallas as pl
from jax.experimental.pallas import tpu as pltpu
from jax.sharding import PartitionSpec as P

VMEM_BYTES = 24 * 2**20
VMEM = pl.BlockSpec(memory_space=pltpu.VMEM)
SMEM = pl.BlockSpec(memory_space=pltpu.SMEM)
ANYWHERE = pl.BlockSpec(memory_space=pl.ANY)
LOADS = 4
N1, N2, N3, N4 = 30,30,30,30
NO_COST = pl.CostEstimate(flops=0, bytes_accessed=0, transcendentals=0)


def in_vmem(value):
    return pltpu.with_memory_space_constraint(value, pltpu.VMEM)


def in_hbm(value):
    return pltpu.with_memory_space_constraint(value, pltpu.HBM)


def product(lhs, rhs):
    return jnp.dot(lhs, rhs, preferred_element_type=jnp.float32)


def slots_of(ids, n_blocks):
    top, rows = ids.shape
    experts = lax.broadcasted_iota(jnp.int32, (n_blocks, rows), 0)
    picks = jnp.zeros((n_blocks, rows), jnp.float32)
    for k in range(top):
        picks = picks + jnp.where(ids[k : k + 1, :] == experts, 1.0, 0.0)
    before = lax.broadcasted_iota(jnp.int32, (rows, rows), 0) < lax.broadcasted_iota(
        jnp.int32, (rows, rows), 1
    )
    earlier = product(picks.astype(jnp.bfloat16), jnp.where(before, 1.0, 0.0).astype(jnp.bfloat16))
    return experts, picks, earlier


def expert_at(placement_ref, block):
    found = jnp.int32(0)
    for e in range(placement_ref.shape[0]):
        found = jnp.where(placement_ref[e] == block, jnp.int32(e), found)
    return found


def row_of(values, experts, expert):
    return jnp.sum(jnp.where(experts == expert, values, 0.0), axis=0, keepdims=True)


def bucket_rows(rows):
    row = lax.broadcasted_iota(jnp.int32, (rows, rows), 0)
    half, quarter = rows // 2, rows // 4
    return jnp.where(row < half, row, half + row % quarter).astype(jnp.float32)


def pack_kernel(n_blocks, parts, placement_ref, ids_ref, tokens_ref, *out_refs):
    rows, width = tokens_ref.shape
    half, quarter = rows // 2, rows // 4
    block = lax.axis_index("node") // parts
    experts, picks, earlier = slots_of(ids_ref[...], n_blocks)
    wanted = bucket_rows(rows)
    upper = lax.broadcasted_iota(jnp.int32, (half, width // 2), 0) < quarter
    for k, out_ref in enumerate(out_refs):
        expert = expert_at(placement_ref, lax.bitwise_xor(block, jnp.int32(k)))
        named = row_of(picks, experts, expert) > 0.5
        slot = row_of(earlier, experts, expert)
        chooser = jnp.where(named & (slot == wanted), 1.0, 0.0).astype(jnp.bfloat16)
        packed = product(chooser, tokens_ref[...])
        out_ref[:, :width] = packed[:half].astype(jnp.bfloat16)
        rest = jnp.where(upper, packed[half:, : width // 2], packed[half:, width // 2 :])
        out_ref[:, width:] = rest.astype(jnp.bfloat16)


def pack(placement, ids, tokens, n_blocks, parts):
    rows, width = tokens.shape
    shape = pltpu.VMEM((rows // 2, width + width // 2), jnp.bfloat16)
    return pl.pallas_call(
        functools.partial(pack_kernel, n_blocks, parts),
        out_shape=[shape] * n_blocks,
        in_specs=[SMEM, VMEM, VMEM],
        out_specs=[VMEM] * n_blocks,
        compiler_params=pltpu.CompilerParams(vmem_limit_bytes=VMEM_BYTES),
        cost_estimate=NO_COST,
    )(in_hbm(placement), in_hbm(ids), in_hbm(tokens))


def nothing(*refs):
    pass


def when(value, after):
    if not after:
        return value
    return pl.pallas_call(
        nothing,
        out_shape=pltpu.VMEM(value.shape, value.dtype),
        in_specs=[ANYWHERE] * (1 + len(after)),
        out_specs=ANYWHERE,
        input_output_aliases={0: 0},
        compiler_params=pltpu.CompilerParams(vmem_limit_bytes=VMEM_BYTES),
        cost_estimate=NO_COST,
    )(in_vmem(value), *after)


def load_kernel(*refs):
    sources, targets, sems = refs[:3], refs[4:7], refs[7]
    copies = []
    for i, (source, target) in enumerate(zip(sources, targets)):
        rows = source.shape[0] // LOADS
        for j in range(LOADS):
            part = pl.ds(j * rows, rows)
            copies.append(pltpu.make_async_copy(source.at[part], target.at[part], sems.at[i, j]))
    for copy in copies:
        copy.start()
    for copy in copies:
        copy.wait()


def load(weights, after):
    return pl.pallas_call(
        load_kernel,
        out_shape=[pltpu.VMEM(w.shape, w.dtype) for w in weights],
        in_specs=[pl.BlockSpec(memory_space=pltpu.HBM)] * 3 + [ANYWHERE],
        out_specs=[VMEM] * 3,
        scratch_shapes=[pltpu.SemaphoreType.DMA((3, LOADS))],
        compiler_params=pltpu.CompilerParams(vmem_limit_bytes=VMEM_BYTES),
        cost_estimate=NO_COST,
    )(*[pltpu.with_memory_space_constraint(w, pltpu.HBM) for w in weights], after)


def experts_kernel(*refs):
    straight_ref, across_ref, straight_other_ref, across_other_ref = refs[:4]
    gate_ref, up_ref, down_ref = refs[4:7]
    out_refs = refs[-4:]
    pieces = (straight_ref, across_ref, straight_other_ref, across_other_ref)
    width, hid = gate_ref.shape
    middle = width // 2
    height = straight_ref.shape[0]
    total = len(pieces) * height
    rest = jnp.concatenate([p[:, width:] for p in pieces], axis=0)
    left = jnp.concatenate([p[:, :middle] for p in pieces] + [rest], axis=0)
    right = jnp.concatenate([p[:, middle:width] for p in pieces] + [rest], axis=0)
    upper = lax.broadcasted_iota(jnp.int32, (total, 1), 0) % height < height // 2
    shift = height // 2

    def whole_rows(ref):
        a, b = product(left, ref[:middle, :]), product(right, ref[middle:, :])
        tail = jnp.where(
            upper,
            a[total:] + pltpu.roll(b[total:], total - shift, axis=0),
            b[total:] + pltpu.roll(a[total:], shift, axis=0),
        )
        return jnp.concatenate([a[:total] + b[:total], tail], axis=0)

    gate_rows, up_rows = whole_rows(gate_ref), whole_rows(up_ref)
    hidden = (jax.nn.silu(gate_rows) * up_rows).astype(jnp.bfloat16)

    def store(start, values):
        values = values.astype(jnp.bfloat16)
        stop = start + values.shape[1]
        for i, out_ref in enumerate(out_refs):
            out_ref[:, start:stop] = values[i * height : (i + 1) * height]

    step = middle // 4
    for i in range(4):
        begin = i * step
        a = product(hidden, down_ref[:, begin : begin + step])
        b = product(hidden, down_ref[:, middle + begin : middle + begin + step])
        store(begin, a[:total])
        store(middle + begin, b[:total])
        store(width + begin, jnp.where(upper, a[total:], b[total:]))


def run_experts(pieces, weights, after):
    width, hid = weights[0].shape
    height, packed_width = pieces[0].shape
    rows = len(pieces) * height
    shape = pltpu.VMEM((height, packed_width), jnp.bfloat16)
    operands = [in_vmem(p) for p in pieces] + [in_vmem(w) for w in weights]
    return pl.pallas_call(
        experts_kernel,
        out_shape=[shape] * len(pieces),
        in_specs=[VMEM] * 7 + [ANYWHERE] * len(after),
        out_specs=[VMEM] * len(pieces),
        compiler_params=pltpu.CompilerParams(vmem_limit_bytes=VMEM_BYTES),
        cost_estimate=pl.CostEstimate(
            flops=0, bytes_accessed=4 * width * hid, transcendentals=0
        ),
    )(*operands, *after)


def mix_kernel(n_blocks, parts, placement_ref, ids_ref, gates_ref, *refs):
    results, out_ref = refs[:-1], refs[-1]
    rows, width = out_ref.shape
    half, quarter, middle = rows // 2, rows // 4, width // 2
    block = lax.axis_index("node") // parts
    ids, gates = ids_ref[...], gates_ref[...]
    experts, picks, earlier = slots_of(ids, n_blocks)
    wanted = bucket_rows(rows)
    terms = []
    for k in range(n_blocks):
        expert = expert_at(placement_ref, lax.bitwise_xor(block, jnp.int32(k)))
        named = row_of(picks, experts, expert) > 0.5
        slot = row_of(earlier, experts, expert)
        weight = jnp.sum(jnp.where(ids == expert, gates, 0.0), axis=0, keepdims=True)
        terms.append(jnp.where(named & (slot == wanted), weight, 0.0))
    term = jnp.concatenate(terms, axis=0)
    row = lax.broadcasted_iota(jnp.int32, term.shape, 0) % rows
    rest = jnp.concatenate([r[:, width:] for r in results], axis=0)
    for side in range(2):
        first = half + side * quarter
        mine = jnp.where((row < half) | ((row >= first) & (row < first + quarter)), term, 0.0)
        high = mine.astype(jnp.bfloat16)
        lower = mine - high.astype(jnp.float32)
        mid = lower.astype(jnp.bfloat16)
        low = (lower - mid.astype(jnp.float32)).astype(jnp.bfloat16)
        lhs = jnp.concatenate([high, mid, low], axis=1)
        pieces = []
        for r in results:
            pieces += [r[:, side * middle : (side + 1) * middle], r[:, width:]]
        rhs = jnp.concatenate(pieces, axis=0)
        value = lax.dot_general(
            lhs, rhs, (((0,), (0,)), ((), ())), preferred_element_type=jnp.float32
        )
        value = value[:rows] + value[rows : 2 * rows] + value[2 * rows :]
        out_ref[:, side * middle : (side + 1) * middle] = value.astype(jnp.bfloat16)


def mix(placement, ids, gates, results, n_blocks, parts):
    rows = ids.shape[1]
    width = results[0].shape[1] // 3 * 2
    return pl.pallas_call(
        functools.partial(mix_kernel, n_blocks, parts),
        out_shape=jax.ShapeDtypeStruct((rows, width), jnp.bfloat16),
        in_specs=[SMEM] + [VMEM] * (2 + n_blocks),
        out_specs=VMEM,
        compiler_params=pltpu.CompilerParams(vmem_limit_bytes=VMEM_BYTES),
        cost_estimate=pl.CostEstimate(
            flops=6 * n_blocks * rows * rows * width,
            bytes_accessed=2 * (n_blocks + 1) * rows * width,
            transcendentals=0,
        ),
    )(placement, ids, gates, *[in_vmem(r) for r in results])


def add(*values):
    return sum(v.astype(jnp.float32) for v in values).astype(jnp.bfloat16)


def local(tokens, expert_ids, gates, placement, gate_weight, up_weight, down_weight):
    n_blocks = placement.shape[0]
    devices = lax.axis_size("node")
    parts = devices // n_blocks

    def along_z(value, k):
        pairs = [(i, i ^ (k * parts)) for i in range(devices)]
        return lax.ppermute(value, "node", pairs)

    def along_y(value):
        return lax.ppermute(value, "node", [(i, i ^ 2) for i in range(devices)])

    def along_core(value):
        return lax.ppermute(value, "node", [(i, i ^ 1) for i in range(devices)])

    ids = expert_ids.T
    groups = [[n_blocks - d, d] for d in range(1, n_blocks // 2)] + [[n_blocks // 2]]
    last = groups[-1][0]
    straight, across, results = {}, {}, {}
    both, home, kept, sent = {}, {}, {}, {}

    def compute(k, after):
        theirs = [along_core(straight[k]), along_core(across[k])]
        out = run_experts([straight[k], across[k]] + theirs, weights, after)
        sent[k] = out[3]
        both[k] = add(out[1], along_core(out[3]))
        kept[k] = out[0], along_core(out[2])

    def go_home(k, after):
        back = along_y(both[k] if k else when(both[k], after))
        home[k] = add(*kept[k], back)
        results[k] = along_z(when(home[k], after), k) if k else home[k]

    buckets = list(pack(placement, ids, tokens, n_blocks, parts))
    weights = load((gate_weight, up_weight, down_weight), buckets[0])
    straight[0] = buckets[0]
    across[0] = along_y(straight[0])
    compute(0, [])
    second = None
    for g, group in enumerate(groups):
        first = group[0]
        if g == 0:
            straight[first] = along_z(buckets[first], first)
            across[first] = along_y(straight[first])
            compute(first, [])
            go_home(first, [])
        else:
            previous = groups[g - 1][0]
            straight[first] = along_z(when(buckets[first], [straight[previous], across[0]]), first)
            after = [sent[0]] + ([across[second]] if second else [])
            straight[first] = when(straight[first], after)
            across[first] = along_y(straight[first])
            compute(first, [])
            go_home(first, [results[previous]])
        if second:
            compute(second, [sent[first]] + ([both[previous]] if g else []))
            go_home(second, [])
        second = group[1] if len(group) > 1 else None
        if second:
            straight[second] = along_z(when(buckets[second], [weights[0]] if g == 0 else []), second)
            across[second] = along_y(straight[second])
    go_home(0, [home[last]])
    return mix(placement, ids, gates.T, [results[k] for k in range(n_blocks)], n_blocks, parts)


def solution(mesh):
    placed = (
        P(("group", "node"), None),
        P(("group", "node"), None),
        P(("group", "node"), None),
        P(),
        P(None, "node"),
        P(None, "node"),
        P("node", None),
    )
    return jax.shard_map(
        local, mesh=mesh, in_specs=placed, out_specs=P(("group", "node"), None), check_vma=False
    )
```

```python
import functools

import jax
import jax.numpy as jnp
from jax import lax
from jax.experimental import pallas as pl
from jax.experimental.pallas import tpu as pltpu
from jax.sharding import PartitionSpec as P

VMEM_BYTES = 24 * 2**20
VMEM = pl.BlockSpec(memory_space=pltpu.VMEM)
SMEM = pl.BlockSpec(memory_space=pltpu.SMEM)
ANYWHERE = pl.BlockSpec(memory_space=pl.ANY)
LOADS = 4
N1, N2, N3, N4 = 30,30,30,30
NO_COST = pl.CostEstimate(flops=0, bytes_accessed=0, transcendentals=0)


def in_vmem(value):
    return pltpu.with_memory_space_constraint(value, pltpu.VMEM)


def in_hbm(value):
    return pltpu.with_memory_space_constraint(value, pltpu.HBM)


def product(lhs, rhs):
    return jnp.dot(lhs, rhs, preferred_element_type=jnp.float32)


def slots_of(ids, n_blocks):
    top, rows = ids.shape
    experts = lax.broadcasted_iota(jnp.int32, (n_blocks, rows), 0)
    picks = jnp.zeros((n_blocks, rows), jnp.float32)
    for k in range(top):
        picks = picks + jnp.where(ids[k : k + 1, :] == experts, 1.0, 0.0)
    before = lax.broadcasted_iota(jnp.int32, (rows, rows), 0) < lax.broadcasted_iota(
        jnp.int32, (rows, rows), 1
    )
    earlier = product(picks.astype(jnp.bfloat16), jnp.where(before, 1.0, 0.0).astype(jnp.bfloat16))
    return experts, picks, earlier


def expert_at(placement_ref, block):
    found = jnp.int32(0)
    for e in range(placement_ref.shape[0]):
        found = jnp.where(placement_ref[e] == block, jnp.int32(e), found)
    return found


def row_of(values, experts, expert):
    return jnp.sum(jnp.where(experts == expert, values, 0.0), axis=0, keepdims=True)


def bucket_rows(rows):
    row = lax.broadcasted_iota(jnp.int32, (rows, rows), 0)
    half, quarter = rows // 2, rows // 4
    return jnp.where(row < half, row, half + row % quarter).astype(jnp.float32)


def pack_kernel(n_blocks, parts, placement_ref, ids_ref, tokens_ref, *out_refs):
    rows, width = tokens_ref.shape
    half, quarter = rows // 2, rows // 4
    block = lax.axis_index("node") // parts
    experts, picks, earlier = slots_of(ids_ref[...], n_blocks)
    wanted = bucket_rows(rows)
    upper = lax.broadcasted_iota(jnp.int32, (half, width // 2), 0) < quarter
    for k, out_ref in enumerate(out_refs):
        expert = expert_at(placement_ref, lax.bitwise_xor(block, jnp.int32(k)))
        named = row_of(picks, experts, expert) > 0.5
        slot = row_of(earlier, experts, expert)
        chooser = jnp.where(named & (slot == wanted), 1.0, 0.0).astype(jnp.bfloat16)
        packed = product(chooser, tokens_ref[...])
        out_ref[:, :width] = packed[:half].astype(jnp.bfloat16)
        rest = jnp.where(upper, packed[half:, : width // 2], packed[half:, width // 2 :])
        out_ref[:, width:] = rest.astype(jnp.bfloat16)


def pack(placement, ids, tokens, n_blocks, parts):
    rows, width = tokens.shape
    shape = pltpu.VMEM((rows // 2, width + width // 2), jnp.bfloat16)
    return pl.pallas_call(
        functools.partial(pack_kernel, n_blocks, parts),
        out_shape=[shape] * n_blocks,
        in_specs=[SMEM, VMEM, VMEM],
        out_specs=[VMEM] * n_blocks,
        compiler_params=pltpu.CompilerParams(vmem_limit_bytes=VMEM_BYTES),
        cost_estimate=NO_COST,
    )(in_hbm(placement), in_hbm(ids), in_hbm(tokens))


def nothing(*refs):
    pass


def when(value, after):
    if not after:
        return value
    return pl.pallas_call(
        nothing,
        out_shape=pltpu.VMEM(value.shape, value.dtype),
        in_specs=[ANYWHERE] * (1 + len(after)),
        out_specs=ANYWHERE,
        input_output_aliases={0: 0},
        compiler_params=pltpu.CompilerParams(vmem_limit_bytes=VMEM_BYTES),
        cost_estimate=NO_COST,
    )(in_vmem(value), *after)


def load_kernel(*refs):
    sources, targets, sems = refs[:3], refs[4:7], refs[7]
    copies = []
    for i, (source, target) in enumerate(zip(sources, targets)):
        rows = source.shape[0] // LOADS
        for j in range(LOADS):
            part = pl.ds(j * rows, rows)
            copies.append(pltpu.make_async_copy(source.at[part], target.at[part], sems.at[i, j]))
    for copy in copies:
        copy.start()
    for copy in copies:
        copy.wait()


def load(weights, after):
    return pl.pallas_call(
        load_kernel,
        out_shape=[pltpu.VMEM(w.shape, w.dtype) for w in weights],
        in_specs=[pl.BlockSpec(memory_space=pltpu.HBM)] * 3 + [ANYWHERE],
        out_specs=[VMEM] * 3,
        scratch_shapes=[pltpu.SemaphoreType.DMA((3, LOADS))],
        compiler_params=pltpu.CompilerParams(vmem_limit_bytes=VMEM_BYTES),
        cost_estimate=NO_COST,
    )(*[pltpu.with_memory_space_constraint(w, pltpu.HBM) for w in weights], after)


def experts_kernel(*refs):
    straight_ref, across_ref, straight_other_ref, across_other_ref = refs[:4]
    gate_ref, up_ref, down_ref = refs[4:7]
    out_refs = refs[-4:]
    pieces = (straight_ref, across_ref, straight_other_ref, across_other_ref)
    width, hid = gate_ref.shape
    middle = width // 2
    height = straight_ref.shape[0]
    total = len(pieces) * height
    rest = jnp.concatenate([p[:, width:] for p in pieces], axis=0)
    left = jnp.concatenate([p[:, :middle] for p in pieces] + [rest], axis=0)
    right = jnp.concatenate([p[:, middle:width] for p in pieces] + [rest], axis=0)
    upper = lax.broadcasted_iota(jnp.int32, (total, 1), 0) % height < height // 2
    shift = height // 2

    def whole_rows(ref):
        a, b = product(left, ref[:middle, :]), product(right, ref[middle:, :])
        tail = jnp.where(
            upper,
            a[total:] + pltpu.roll(b[total:], total - shift, axis=0),
            b[total:] + pltpu.roll(a[total:], shift, axis=0),
        )
        return jnp.concatenate([a[:total] + b[:total], tail], axis=0)

    gate_rows, up_rows = whole_rows(gate_ref), whole_rows(up_ref)
    hidden = (jax.nn.silu(gate_rows) * up_rows).astype(jnp.bfloat16)

    def store(start, values):
        values = values.astype(jnp.bfloat16)
        stop = start + values.shape[1]
        for i, out_ref in enumerate(out_refs):
            out_ref[:, start:stop] = values[i * height : (i + 1) * height]

    step = middle // 4
    for i in range(4):
        begin = i * step
        a = product(hidden, down_ref[:, begin : begin + step])
        b = product(hidden, down_ref[:, middle + begin : middle + begin + step])
        store(begin, a[:total])
        store(middle + begin, b[:total])
        store(width + begin, jnp.where(upper, a[total:], b[total:]))


def run_experts(pieces, weights, after):
    width, hid = weights[0].shape
    height, packed_width = pieces[0].shape
    rows = len(pieces) * height
    shape = pltpu.VMEM((height, packed_width), jnp.bfloat16)
    operands = [in_vmem(p) for p in pieces] + [in_vmem(w) for w in weights]
    return pl.pallas_call(
        experts_kernel,
        out_shape=[shape] * len(pieces),
        in_specs=[VMEM] * 7 + [ANYWHERE] * len(after),
        out_specs=[VMEM] * len(pieces),
        compiler_params=pltpu.CompilerParams(vmem_limit_bytes=VMEM_BYTES),
        cost_estimate=pl.CostEstimate(
            flops=0, bytes_accessed=4 * width * hid, transcendentals=0
        ),
    )(*operands, *after)


def mix_kernel(n_blocks, parts, placement_ref, ids_ref, gates_ref, *refs):
    results, out_ref = refs[:n_blocks], refs[-1]
    rows, width = out_ref.shape
    half, quarter, middle = rows // 2, rows // 4, width // 2
    block = lax.axis_index("node") // parts
    ids, gates = ids_ref[...], gates_ref[...]
    experts, picks, earlier = slots_of(ids, n_blocks)
    wanted = bucket_rows(rows)
    terms = []
    for k in range(n_blocks):
        expert = expert_at(placement_ref, lax.bitwise_xor(block, jnp.int32(k)))
        named = row_of(picks, experts, expert) > 0.5
        slot = row_of(earlier, experts, expert)
        weight = jnp.sum(jnp.where(ids == expert, gates, 0.0), axis=0, keepdims=True)
        terms.append(jnp.where(named & (slot == wanted), weight, 0.0))
    term = jnp.concatenate(terms, axis=0)
    row = lax.broadcasted_iota(jnp.int32, term.shape, 0) % rows
    rest = jnp.concatenate([r[:, width:] for r in results], axis=0)
    for side in range(2):
        first = half + side * quarter
        mine = jnp.where((row < half) | ((row >= first) & (row < first + quarter)), term, 0.0)
        high = mine.astype(jnp.bfloat16)
        lower = mine - high.astype(jnp.float32)
        mid = lower.astype(jnp.bfloat16)
        low = (lower - mid.astype(jnp.float32)).astype(jnp.bfloat16)
        lhs = jnp.concatenate([high, mid, low], axis=1)
        pieces = []
        for r in results:
            pieces += [r[:, side * middle : (side + 1) * middle], r[:, width:]]
        rhs = jnp.concatenate(pieces, axis=0)
        value = lax.dot_general(
            lhs, rhs, (((0,), (0,)), ((), ())), preferred_element_type=jnp.float32
        )
        value = value[:rows] + value[rows : 2 * rows] + value[2 * rows :]
        out_ref[:, side * middle : (side + 1) * middle] = value.astype(jnp.bfloat16)


def mix(placement, ids, gates, results, after, n_blocks, parts):
    rows = ids.shape[1]
    width = results[0].shape[1] // 3 * 2
    return pl.pallas_call(
        functools.partial(mix_kernel, n_blocks, parts),
        out_shape=jax.ShapeDtypeStruct((rows, width), jnp.bfloat16),
        in_specs=[SMEM] + [VMEM] * (2 + n_blocks) + [ANYWHERE] * len(after),
        out_specs=VMEM,
        compiler_params=pltpu.CompilerParams(vmem_limit_bytes=VMEM_BYTES),
        cost_estimate=pl.CostEstimate(
            flops=6 * n_blocks * rows * rows * width,
            bytes_accessed=2 * (n_blocks + 1) * rows * width,
            transcendentals=0,
        ),
    )(placement, ids, gates, *[in_vmem(r) for r in results], *after)


def add_kernel(*refs):
    total = refs[0][...].astype(jnp.float32)
    for ref in refs[1:-1]:
        total = total + ref[...].astype(jnp.float32)
    refs[-1][...] = total.astype(refs[-1].dtype)


def add(*values):
    return pl.pallas_call(
        add_kernel,
        out_shape=pltpu.VMEM(values[0].shape, values[0].dtype),
        in_specs=[VMEM] * len(values),
        out_specs=VMEM,
        compiler_params=pltpu.CompilerParams(vmem_limit_bytes=VMEM_BYTES),
        cost_estimate=NO_COST,
    )(*[in_vmem(v) for v in values])


def local(tokens, expert_ids, gates, placement, gate_weight, up_weight, down_weight):
    n_blocks = placement.shape[0]
    devices = lax.axis_size("node")
    parts = devices // n_blocks

    def along_z(value, k):
        pairs = [(i, i ^ (k * parts)) for i in range(devices)]
        return lax.ppermute(value, "node", pairs)

    def along_y(value):
        return lax.ppermute(value, "node", [(i, i ^ 2) for i in range(devices)])

    def along_core(value):
        return lax.ppermute(value, "node", [(i, i ^ 1) for i in range(devices)])

    ids = expert_ids.T
    groups = [[n_blocks - d, d] for d in range(1, n_blocks // 2)] + [[n_blocks // 2]]
    last = groups[-1][0]
    straight, across, results = {}, {}, {}
    both, home, kept, sent = {}, {}, {}, {}

    def compute(k, after):
        theirs = [along_core(straight[k]), along_core(across[k])]
        out = run_experts([straight[k], across[k]] + theirs, weights, after)
        sent[k] = out[3]
        both[k] = add(out[1], along_core(out[3]))
        kept[k] = out[0], along_core(out[2])

    def go_home(k, after):
        back = along_y(both[k] if k else when(both[k], after))
        home[k] = add(*kept[k], back)
        results[k] = along_z(when(home[k], after), k) if k else home[k]

    buckets = list(pack(placement, ids, tokens, n_blocks, parts))
    weights = load((gate_weight, up_weight, down_weight), buckets[0])
    straight[0] = buckets[0]
    across[0] = along_y(straight[0])
    compute(0, [])
    second, marks = None, []
    for g, group in enumerate(groups):
        first = group[0]
        if g == 0:
            straight[first] = along_z(buckets[first], first)
            across[first] = along_y(straight[first])
            compute(first, [])
            go_home(first, [])
        else:
            previous = groups[g - 1][0]
            straight[first] = along_z(when(buckets[first], [straight[previous], across[0]]), first)
            after = [sent[0]] + ([across[second]] if second else [])
            straight[first] = when(straight[first], after)
            across[first] = along_y(straight[first])
            compute(first, [both[previous]])
            go_home(first, [])
            marks.append(along_core(results[previous]))
        if second:
            compute(second, [sent[first]])
            go_home(second, [])
        second = group[1] if len(group) > 1 else None
        if second:
            straight[second] = along_z(when(buckets[second], [weights[0]] if g == 0 else []), second)
            across[second] = along_y(straight[second])
    go_home(0, [home[last]])
    return mix(placement, ids, gates.T, [results[k] for k in range(n_blocks)], marks, n_blocks, parts)


def solution(mesh):
    placed = (
        P(("group", "node"), None),
        P(("group", "node"), None),
        P(("group", "node"), None),
        P(),
        P(None, "node"),
        P(None, "node"),
        P("node", None),
    )
    return jax.shard_map(
        local, mesh=mesh, in_specs=placed, out_specs=P(("group", "node"), None), check_vma=False
    )
```

```python
import functools

import jax
import jax.numpy as jnp
from jax import lax
from jax.experimental import pallas as pl
from jax.experimental.pallas import tpu as pltpu
from jax.sharding import PartitionSpec as P

VMEM_BYTES = 24 * 2**20
VMEM = pl.BlockSpec(memory_space=pltpu.VMEM)
SMEM = pl.BlockSpec(memory_space=pltpu.SMEM)
ANYWHERE = pl.BlockSpec(memory_space=pl.ANY)
LOADS = 4
SHARE = 95
N1, N2, N3, N4 = 30,30,30,30
NO_COST = pl.CostEstimate(flops=0, bytes_accessed=0, transcendentals=0)


def in_vmem(value):
    return pltpu.with_memory_space_constraint(value, pltpu.VMEM)


def in_hbm(value):
    return pltpu.with_memory_space_constraint(value, pltpu.HBM)


def product(lhs, rhs):
    return jnp.dot(lhs, rhs, preferred_element_type=jnp.float32)


def slots_of(ids, n_blocks):
    top, rows = ids.shape
    experts = lax.broadcasted_iota(jnp.int32, (n_blocks, rows), 0)
    picks = jnp.zeros((n_blocks, rows), jnp.float32)
    for k in range(top):
        picks = picks + jnp.where(ids[k : k + 1, :] == experts, 1.0, 0.0)
    before = lax.broadcasted_iota(jnp.int32, (rows, rows), 0) < lax.broadcasted_iota(
        jnp.int32, (rows, rows), 1
    )
    earlier = product(picks.astype(jnp.bfloat16), jnp.where(before, 1.0, 0.0).astype(jnp.bfloat16))
    return experts, picks, earlier


def expert_at(placement_ref, block):
    found = jnp.int32(0)
    for e in range(placement_ref.shape[0]):
        found = jnp.where(placement_ref[e] == block, jnp.int32(e), found)
    return found


def row_of(values, experts, expert):
    return jnp.sum(jnp.where(experts == expert, values, 0.0), axis=0, keepdims=True)


def bucket_rows(rows):
    row = lax.broadcasted_iota(jnp.int32, (rows, rows), 0)
    half, quarter = rows // 2, rows // 4
    return jnp.where(row < half, row, half + row % quarter).astype(jnp.float32)


def pack_kernel(n_blocks, parts, placement_ref, ids_ref, tokens_ref, *out_refs):
    rows, width = tokens_ref.shape
    half, quarter = rows // 2, rows // 4
    block = lax.axis_index("node") // parts
    experts, picks, earlier = slots_of(ids_ref[...], n_blocks)
    wanted = bucket_rows(rows)
    upper = lax.broadcasted_iota(jnp.int32, (half, width // 2), 0) < quarter
    for k, out_ref in enumerate(out_refs):
        expert = expert_at(placement_ref, lax.bitwise_xor(block, jnp.int32(k)))
        named = row_of(picks, experts, expert) > 0.5
        slot = row_of(earlier, experts, expert)
        chooser = jnp.where(named & (slot == wanted), 1.0, 0.0).astype(jnp.bfloat16)
        packed = product(chooser, tokens_ref[...])
        out_ref[:, :width] = packed[:half].astype(jnp.bfloat16)
        rest = jnp.where(upper, packed[half:, : width // 2], packed[half:, width // 2 :])
        out_ref[:, width:] = rest.astype(jnp.bfloat16)


def pack(placement, ids, tokens, n_blocks, parts):
    rows, width = tokens.shape
    shape = pltpu.VMEM((rows // 2, width + width // 2), jnp.bfloat16)
    return pl.pallas_call(
        functools.partial(pack_kernel, n_blocks, parts),
        out_shape=[shape] * n_blocks,
        in_specs=[SMEM, VMEM, VMEM],
        out_specs=[VMEM] * n_blocks,
        compiler_params=pltpu.CompilerParams(vmem_limit_bytes=VMEM_BYTES),
        cost_estimate=NO_COST,
    )(in_hbm(placement), in_hbm(ids), in_hbm(tokens))


def nothing(*refs):
    pass


def clear(*refs):
    refs[-1][...] = jnp.zeros_like(refs[-1])


def token(after):
    rows, width = after.shape
    return pl.pallas_call(
        clear,
        out_shape=pltpu.VMEM((rows, width * SHARE // 12800 * 128), after.dtype),
        in_specs=[ANYWHERE],
        out_specs=VMEM,
        compiler_params=pltpu.CompilerParams(vmem_limit_bytes=VMEM_BYTES),
        cost_estimate=NO_COST,
    )(after)


def when(value, after):
    if not after:
        return value
    return pl.pallas_call(
        nothing,
        out_shape=pltpu.VMEM(value.shape, value.dtype),
        in_specs=[ANYWHERE] * (1 + len(after)),
        out_specs=ANYWHERE,
        input_output_aliases={0: 0},
        compiler_params=pltpu.CompilerParams(vmem_limit_bytes=VMEM_BYTES),
        cost_estimate=NO_COST,
    )(in_vmem(value), *after)


def load_kernel(*refs):
    sources, targets, sems = refs[:3], refs[4:7], refs[7]
    copies = []
    for i, (source, target) in enumerate(zip(sources, targets)):
        rows = source.shape[0] // LOADS
        for j in range(LOADS):
            part = pl.ds(j * rows, rows)
            copies.append(pltpu.make_async_copy(source.at[part], target.at[part], sems.at[i, j]))
    for copy in copies:
        copy.start()
    for copy in copies:
        copy.wait()


def load(weights, after):
    return pl.pallas_call(
        load_kernel,
        out_shape=[pltpu.VMEM(w.shape, w.dtype) for w in weights],
        in_specs=[pl.BlockSpec(memory_space=pltpu.HBM)] * 3 + [ANYWHERE],
        out_specs=[VMEM] * 3,
        scratch_shapes=[pltpu.SemaphoreType.DMA((3, LOADS))],
        compiler_params=pltpu.CompilerParams(vmem_limit_bytes=VMEM_BYTES),
        cost_estimate=NO_COST,
    )(*[pltpu.with_memory_space_constraint(w, pltpu.HBM) for w in weights], after)


def split_kernel(whole_ref, *part_refs):
    width = part_refs[0].shape[1]
    for i, part_ref in enumerate(part_refs):
        part_ref[...] = whole_ref[:, i * width : (i + 1) * width]


def split(value):
    rows, width = value.shape
    return pl.pallas_call(
        split_kernel,
        out_shape=[pltpu.VMEM((rows, width // 3), value.dtype)] * 3,
        in_specs=[VMEM],
        out_specs=[VMEM] * 3,
        compiler_params=pltpu.CompilerParams(vmem_limit_bytes=VMEM_BYTES),
        cost_estimate=NO_COST,
    )(in_vmem(value))


def experts_kernel(*refs):
    whole, parts = refs[:3], refs[3:6]
    gate_ref, up_ref, down_ref = refs[6:9]
    out_whole, out_parts = refs[-6:-3], refs[-3:]
    width, hid = gate_ref.shape
    middle = width // 2
    height = whole[0].shape[0]
    total = 4 * height

    def third(i):
        return [p[:, i * middle : (i + 1) * middle] for p in whole] + [parts[i][...]]

    rest = third(2)
    left = jnp.concatenate(third(0) + rest, axis=0)
    right = jnp.concatenate(third(1) + rest, axis=0)
    upper = lax.broadcasted_iota(jnp.int32, (total, 1), 0) % height < height // 2
    shift = height // 2

    def whole_rows(ref):
        a, b = product(left, ref[:middle, :]), product(right, ref[middle:, :])
        tail = jnp.where(
            upper,
            a[total:] + pltpu.roll(b[total:], total - shift, axis=0),
            b[total:] + pltpu.roll(a[total:], shift, axis=0),
        )
        return jnp.concatenate([a[:total] + b[:total], tail], axis=0)

    gate_rows, up_rows = whole_rows(gate_ref), whole_rows(up_ref)
    hidden = (jax.nn.silu(gate_rows) * up_rows).astype(jnp.bfloat16)

    def store(i, begin, values):
        values = values.astype(jnp.bfloat16)
        stop = begin + values.shape[1]
        for p, out_ref in enumerate(out_whole):
            out_ref[:, i * middle + begin : i * middle + stop] = values[p * height : (p + 1) * height]
        out_parts[i][:, begin:stop] = values[3 * height :]

    step = middle // 4
    for j in range(4):
        begin = j * step
        a = product(hidden, down_ref[:, begin : begin + step])
        b = product(hidden, down_ref[:, middle + begin : middle + begin + step])
        store(0, begin, a[:total])
        store(1, begin, b[:total])
        store(2, begin, jnp.where(upper, a[total:], b[total:]))


def run_experts(whole, parts, weights, after):
    rows, width = whole[0].shape
    shapes = [pltpu.VMEM((rows, width), jnp.bfloat16)] * 3
    shapes += [pltpu.VMEM((rows, width // 3), jnp.bfloat16)] * 3
    operands = [in_vmem(value) for value in [*whole, *parts, *weights]]
    return pl.pallas_call(
        experts_kernel,
        out_shape=shapes,
        in_specs=[VMEM] * len(operands) + [ANYWHERE] * len(after),
        out_specs=[VMEM] * len(shapes),
        compiler_params=pltpu.CompilerParams(vmem_limit_bytes=VMEM_BYTES),
        cost_estimate=NO_COST,
    )(*operands, *after)


def mix_kernel(n_blocks, parts, placement_ref, ids_ref, gates_ref, *refs):
    results, out_ref = refs[:n_blocks], refs[-1]
    rows, width = out_ref.shape
    half, quarter, middle = rows // 2, rows // 4, width // 2
    block = lax.axis_index("node") // parts
    ids, gates = ids_ref[...], gates_ref[...]
    experts, picks, earlier = slots_of(ids, n_blocks)
    wanted = bucket_rows(rows)
    terms = []
    for k in range(n_blocks):
        expert = expert_at(placement_ref, lax.bitwise_xor(block, jnp.int32(k)))
        named = row_of(picks, experts, expert) > 0.5
        slot = row_of(earlier, experts, expert)
        weight = jnp.sum(jnp.where(ids == expert, gates, 0.0), axis=0, keepdims=True)
        terms.append(jnp.where(named & (slot == wanted), weight, 0.0))
    term = jnp.concatenate(terms, axis=0)
    row = lax.broadcasted_iota(jnp.int32, term.shape, 0) % rows
    for side in range(2):
        first = half + side * quarter
        mine = jnp.where((row < half) | ((row >= first) & (row < first + quarter)), term, 0.0)
        high = mine.astype(jnp.bfloat16)
        lower = mine - high.astype(jnp.float32)
        mid = lower.astype(jnp.bfloat16)
        low = (lower - mid.astype(jnp.float32)).astype(jnp.bfloat16)
        lhs = jnp.concatenate([high, mid, low], axis=1)
        pieces = []
        for r in results:
            pieces += [r[:, side * middle : (side + 1) * middle], r[:, width:]]
        rhs = jnp.concatenate([p.astype(jnp.bfloat16) for p in pieces], axis=0)
        value = lax.dot_general(
            lhs, rhs, (((0,), (0,)), ((), ())), preferred_element_type=jnp.float32
        )
        value = value[:rows] + value[rows : 2 * rows] + value[2 * rows :]
        out_ref[:, side * middle : (side + 1) * middle] = value.astype(jnp.bfloat16)


def mix(placement, ids, gates, results, after, n_blocks, parts):
    rows = ids.shape[1]
    width = results[0].shape[1] // 3 * 2
    return pl.pallas_call(
        functools.partial(mix_kernel, n_blocks, parts),
        out_shape=jax.ShapeDtypeStruct((rows, width), jnp.bfloat16),
        in_specs=[SMEM] + [VMEM] * (2 + n_blocks) + [ANYWHERE] * len(after),
        out_specs=VMEM,
        compiler_params=pltpu.CompilerParams(vmem_limit_bytes=VMEM_BYTES),
        cost_estimate=pl.CostEstimate(
            flops=6 * n_blocks * rows * rows * width,
            bytes_accessed=2 * (n_blocks + 1) * rows * width,
            transcendentals=0,
        ),
    )(placement, ids, gates, *[in_vmem(r) for r in results], *after)


def add_kernel(*refs):
    total = refs[0][...].astype(jnp.float32)
    for ref in refs[1:-1]:
        total = total + ref[...].astype(jnp.float32)
    refs[-1][...] = total.astype(refs[-1].dtype)


def add_parts_kernel(whole_ref, *refs):
    width = refs[0].shape[1]
    for i, part_ref in enumerate(refs[:-1]):
        columns = slice(i * width, (i + 1) * width)
        total = whole_ref[:, columns].astype(jnp.float32) + part_ref[...].astype(jnp.float32)
        refs[-1][:, columns] = total.astype(refs[-1].dtype)


def add(kernel, *values):
    return pl.pallas_call(
        kernel,
        out_shape=pltpu.VMEM(values[0].shape, values[0].dtype),
        in_specs=[VMEM] * len(values),
        out_specs=VMEM,
        compiler_params=pltpu.CompilerParams(vmem_limit_bytes=VMEM_BYTES),
        cost_estimate=NO_COST,
    )(*[in_vmem(v) for v in values])


def local(tokens, expert_ids, gates, placement, gate_weight, up_weight, down_weight):
    n_blocks = placement.shape[0]
    devices = lax.axis_size("node")
    parts = devices // n_blocks

    def along_z(value, k):
        pairs = [(i, i ^ (k * parts)) for i in range(devices)]
        return lax.ppermute(value, "node", pairs)

    def along_y(value):
        return lax.ppermute(value, "node", [(i, i ^ 2) for i in range(devices)])

    def along_core(value):
        return lax.ppermute(value, "node", [(i, i ^ 1) for i in range(devices)])

    ids = expert_ids.T
    groups = [[n_blocks - d, d] for d in range(1, n_blocks // 2)] + [[n_blocks // 2]]
    last = groups[-1][0]
    straight, across, results = {}, {}, {}
    both, home, kept, sent = {}, {}, {}, {}

    def compute(k, after):
        whole = [straight[k], across[k], along_core(straight[k])]
        parts = [along_core(part) for part in split(across[k])]
        out = run_experts(whole, parts, weights, after)
        sent[k] = out[3]
        both[k] = add(add_parts_kernel, out[1], *[along_core(part) for part in out[3:]])
        kept[k] = out[0], along_core(out[2])

    def go_home(k, after):
        back = along_y(both[k] if k else when(both[k], after))
        early = k in [group[0] for group in groups[:-1]]
        home[k] = add(add_kernel, *kept[k], back)
        results[k] = along_z(home[k], k) if k else home[k]
        if early:
            marks.append(along_core(token(results[k])))
        if k == last:
            results[k] = results[k].astype(jnp.float32)

    buckets = list(pack(placement, ids, tokens, n_blocks, parts))
    weights = load((gate_weight, up_weight, down_weight), buckets[0])
    straight[0] = buckets[0]
    across[0] = along_y(straight[0])
    compute(0, [])
    second, marks = None, []
    for g, group in enumerate(groups):
        first = group[0]
        if g == 0:
            straight[first] = along_z(buckets[first], first)
            across[first] = along_y(straight[first])
            compute(first, [])
            go_home(first, [])
        else:
            previous = groups[g - 1][0]
            straight[first] = along_z(when(buckets[first], [straight[previous], across[0]]), first)
            after = [sent[0]] + ([across[second]] if second else [])
            straight[first] = when(straight[first], after)
            across[first] = along_y(straight[first])
            compute(first, [both[previous]])
            go_home(first, [])
        if second:
            compute(second, [sent[first]])
            go_home(second, [])
        second = group[1] if len(group) > 1 else None
        if second:
            straight[second] = along_z(when(buckets[second], [weights[0]] if g == 0 else []), second)
            across[second] = along_y(straight[second])
    go_home(0, [home[last]])
    return mix(placement, ids, gates.T, [results[k] for k in range(n_blocks)], marks, n_blocks, parts)


def solution(mesh):
    placed = (
        P(("group", "node"), None),
        P(("group", "node"), None),
        P(("group", "node"), None),
        P(),
        P(None, "node"),
        P(None, "node"),
        P("node", None),
    )
    return jax.shard_map(
        local, mesh=mesh, in_specs=placed, out_specs=P(("group", "node"), None), check_vma=False
    )
```

```python
import functools

import jax
import jax.numpy as jnp
from jax import lax
from jax.experimental import pallas as pl
from jax.experimental.pallas import tpu as pltpu
from jax.sharding import PartitionSpec as P

VMEM_BYTES = 24 * 2**20
VMEM = pl.BlockSpec(memory_space=pltpu.VMEM)
SMEM = pl.BlockSpec(memory_space=pltpu.SMEM)
ANYWHERE = pl.BlockSpec(memory_space=pl.ANY)
LOADS = 4
N1, N2, N3, N4 = 30,30,30,30
NO_COST = pl.CostEstimate(flops=0, bytes_accessed=0, transcendentals=0)


def in_vmem(value):
    return pltpu.with_memory_space_constraint(value, pltpu.VMEM)


def in_hbm(value):
    return pltpu.with_memory_space_constraint(value, pltpu.HBM)


def product(lhs, rhs):
    return jnp.dot(lhs, rhs, preferred_element_type=jnp.float32)


def slots_of(ids, n_blocks):
    top, rows = ids.shape
    experts = lax.broadcasted_iota(jnp.int32, (n_blocks, rows), 0)
    picks = jnp.zeros((n_blocks, rows), jnp.float32)
    for k in range(top):
        picks = picks + jnp.where(ids[k : k + 1, :] == experts, 1.0, 0.0)
    before = lax.broadcasted_iota(jnp.int32, (rows, rows), 0) < lax.broadcasted_iota(
        jnp.int32, (rows, rows), 1
    )
    earlier = product(picks.astype(jnp.bfloat16), jnp.where(before, 1.0, 0.0).astype(jnp.bfloat16))
    return experts, picks, earlier


def expert_at(placement_ref, block):
    found = jnp.int32(0)
    for e in range(placement_ref.shape[0]):
        found = jnp.where(placement_ref[e] == block, jnp.int32(e), found)
    return found


def row_of(values, experts, expert):
    return jnp.sum(jnp.where(experts == expert, values, 0.0), axis=0, keepdims=True)


def bucket_rows(rows):
    row = lax.broadcasted_iota(jnp.int32, (rows, rows), 0)
    half, quarter = rows // 2, rows // 4
    return jnp.where(row < half, row, half + row % quarter).astype(jnp.float32)


def pack_kernel(n_blocks, parts, placement_ref, ids_ref, tokens_ref, *out_refs):
    rows, width = tokens_ref.shape
    half, quarter = rows // 2, rows // 4
    block = lax.axis_index("node") // parts
    experts, picks, earlier = slots_of(ids_ref[...], n_blocks)
    wanted = bucket_rows(rows)
    upper = lax.broadcasted_iota(jnp.int32, (half, width // 2), 0) < quarter
    for k, out_ref in enumerate(out_refs):
        expert = expert_at(placement_ref, lax.bitwise_xor(block, jnp.int32(k)))
        named = row_of(picks, experts, expert) > 0.5
        slot = row_of(earlier, experts, expert)
        chooser = jnp.where(named & (slot == wanted), 1.0, 0.0).astype(jnp.bfloat16)
        packed = product(chooser, tokens_ref[...])
        out_ref[:, :width] = packed[:half].astype(jnp.bfloat16)
        rest = jnp.where(upper, packed[half:, : width // 2], packed[half:, width // 2 :])
        out_ref[:, width:] = rest.astype(jnp.bfloat16)


def pack(placement, ids, tokens, n_blocks, parts):
    rows, width = tokens.shape
    shape = pltpu.VMEM((rows // 2, width + width // 2), jnp.bfloat16)
    return pl.pallas_call(
        functools.partial(pack_kernel, n_blocks, parts),
        out_shape=[shape] * n_blocks,
        in_specs=[SMEM, VMEM, VMEM],
        out_specs=[VMEM] * n_blocks,
        compiler_params=pltpu.CompilerParams(vmem_limit_bytes=VMEM_BYTES),
        cost_estimate=NO_COST,
    )(in_hbm(placement), in_hbm(ids), in_hbm(tokens))


def nothing(*refs):
    pass


def clear(*refs):
    refs[-1][...] = jnp.zeros_like(refs[-1])


def token(after):
    return pl.pallas_call(
        clear,
        out_shape=pltpu.VMEM(after.shape, after.dtype),
        in_specs=[ANYWHERE],
        out_specs=VMEM,
        compiler_params=pltpu.CompilerParams(vmem_limit_bytes=VMEM_BYTES),
        cost_estimate=NO_COST,
    )(after)


def when(value, after):
    if not after:
        return value
    return pl.pallas_call(
        nothing,
        out_shape=pltpu.VMEM(value.shape, value.dtype),
        in_specs=[ANYWHERE] * (1 + len(after)),
        out_specs=ANYWHERE,
        input_output_aliases={0: 0},
        compiler_params=pltpu.CompilerParams(vmem_limit_bytes=VMEM_BYTES),
        cost_estimate=NO_COST,
    )(in_vmem(value), *after)


def load_kernel(*refs):
    sources, targets, sems = refs[:3], refs[4:7], refs[7]
    copies = []
    for i, (source, target) in enumerate(zip(sources, targets)):
        rows = source.shape[0] // LOADS
        for j in range(LOADS):
            part = pl.ds(j * rows, rows)
            copies.append(pltpu.make_async_copy(source.at[part], target.at[part], sems.at[i, j]))
    for copy in copies:
        copy.start()
    for copy in copies:
        copy.wait()


def load(weights, after):
    return pl.pallas_call(
        load_kernel,
        out_shape=[pltpu.VMEM(w.shape, w.dtype) for w in weights],
        in_specs=[pl.BlockSpec(memory_space=pltpu.HBM)] * 3 + [ANYWHERE],
        out_specs=[VMEM] * 3,
        scratch_shapes=[pltpu.SemaphoreType.DMA((3, LOADS))],
        compiler_params=pltpu.CompilerParams(vmem_limit_bytes=VMEM_BYTES),
        cost_estimate=NO_COST,
    )(*[pltpu.with_memory_space_constraint(w, pltpu.HBM) for w in weights], after)


def experts_kernel(count, *refs):
    pieces = refs[:count]
    gate_ref, up_ref, down_ref = refs[count : count + 3]
    out_refs = refs[-count:]
    width, hid = gate_ref.shape
    middle = width // 2
    height = pieces[0].shape[0]
    total = count * height
    rest = jnp.concatenate([p[:, width:] for p in pieces], axis=0)
    left = jnp.concatenate([p[:, :middle] for p in pieces] + [rest], axis=0)
    right = jnp.concatenate([p[:, middle:width] for p in pieces] + [rest], axis=0)
    upper = lax.broadcasted_iota(jnp.int32, (total, 1), 0) % height < height // 2
    shift = height // 2

    def whole_rows(ref):
        a, b = product(left, ref[:middle, :]), product(right, ref[middle:, :])
        tail = jnp.where(
            upper,
            a[total:] + pltpu.roll(b[total:], total - shift, axis=0),
            b[total:] + pltpu.roll(a[total:], shift, axis=0),
        )
        return jnp.concatenate([a[:total] + b[:total], tail], axis=0)

    gate_rows, up_rows = whole_rows(gate_ref), whole_rows(up_ref)
    hidden = (jax.nn.silu(gate_rows) * up_rows).astype(jnp.bfloat16)

    def store(start, values):
        values = values.astype(jnp.bfloat16)
        stop = start + values.shape[1]
        for i, out_ref in enumerate(out_refs):
            out_ref[:, start:stop] = values[i * height : (i + 1) * height]

    step = middle // 4
    for i in range(4):
        begin = i * step
        a = product(hidden, down_ref[:, begin : begin + step])
        b = product(hidden, down_ref[:, middle + begin : middle + begin + step])
        store(begin, a[:total])
        store(middle + begin, b[:total])
        store(width + begin, jnp.where(upper, a[total:], b[total:]))


def run_experts(pieces, weights, after):
    count = len(pieces)
    shape = pltpu.VMEM(pieces[0].shape, jnp.bfloat16)
    operands = [in_vmem(value) for value in [*pieces, *weights]]
    return pl.pallas_call(
        functools.partial(experts_kernel, count),
        out_shape=[shape] * count,
        in_specs=[VMEM] * len(operands) + [ANYWHERE] * len(after),
        out_specs=[VMEM] * count,
        compiler_params=pltpu.CompilerParams(vmem_limit_bytes=VMEM_BYTES),
        cost_estimate=NO_COST,
    )(*operands, *after)


def mix_kernel(n_blocks, parts, placement_ref, ids_ref, gates_ref, *refs):
    results, out_ref = refs[:n_blocks], refs[-1]
    rows, width = out_ref.shape
    half, quarter, middle = rows // 2, rows // 4, width // 2
    block = lax.axis_index("node") // parts
    ids, gates = ids_ref[...], gates_ref[...]
    experts, picks, earlier = slots_of(ids, n_blocks)
    wanted = bucket_rows(rows)
    terms = []
    for k in range(n_blocks):
        expert = expert_at(placement_ref, lax.bitwise_xor(block, jnp.int32(k)))
        named = row_of(picks, experts, expert) > 0.5
        slot = row_of(earlier, experts, expert)
        weight = jnp.sum(jnp.where(ids == expert, gates, 0.0), axis=0, keepdims=True)
        terms.append(jnp.where(named & (slot == wanted), weight, 0.0))
    term = jnp.concatenate(terms, axis=0)
    row = lax.broadcasted_iota(jnp.int32, term.shape, 0) % rows
    for side in range(2):
        first = half + side * quarter
        mine = jnp.where((row < half) | ((row >= first) & (row < first + quarter)), term, 0.0)
        high = mine.astype(jnp.bfloat16)
        lower = mine - high.astype(jnp.float32)
        mid = lower.astype(jnp.bfloat16)
        low = (lower - mid.astype(jnp.float32)).astype(jnp.bfloat16)
        lhs = jnp.concatenate([high, mid, low], axis=1)
        pieces = []
        for r in results:
            pieces += [r[:, side * middle : (side + 1) * middle], r[:, width:]]
        rhs = jnp.concatenate([p.astype(jnp.bfloat16) for p in pieces], axis=0)
        value = lax.dot_general(
            lhs, rhs, (((0,), (0,)), ((), ())), preferred_element_type=jnp.float32
        )
        value = value[:rows] + value[rows : 2 * rows] + value[2 * rows :]
        out_ref[:, side * middle : (side + 1) * middle] = value.astype(jnp.bfloat16)


def mix(placement, ids, gates, results, after, n_blocks, parts):
    rows = ids.shape[1]
    width = results[0].shape[1] // 3 * 2
    return pl.pallas_call(
        functools.partial(mix_kernel, n_blocks, parts),
        out_shape=jax.ShapeDtypeStruct((rows, width), jnp.bfloat16),
        in_specs=[SMEM] + [VMEM] * (2 + n_blocks) + [ANYWHERE] * len(after),
        out_specs=VMEM,
        compiler_params=pltpu.CompilerParams(vmem_limit_bytes=VMEM_BYTES),
        cost_estimate=pl.CostEstimate(
            flops=6 * n_blocks * rows * rows * width,
            bytes_accessed=2 * (n_blocks + 1) * rows * width,
            transcendentals=0,
        ),
    )(placement, ids, gates, *[in_vmem(r) for r in results], *after)


def add_kernel(*refs):
    total = refs[0][...].astype(jnp.float32)
    for ref in refs[1:-1]:
        total = total + ref[...].astype(jnp.float32)
    refs[-1][...] = total.astype(refs[-1].dtype)


def add(*values):
    return pl.pallas_call(
        add_kernel,
        out_shape=pltpu.VMEM(values[0].shape, values[0].dtype),
        in_specs=[VMEM] * len(values),
        out_specs=VMEM,
        compiler_params=pltpu.CompilerParams(vmem_limit_bytes=VMEM_BYTES),
        cost_estimate=NO_COST,
    )(*[in_vmem(v) for v in values])


def local(tokens, expert_ids, gates, placement, gate_weight, up_weight, down_weight):
    n_blocks = placement.shape[0]
    devices = lax.axis_size("node")
    parts = devices // n_blocks

    def along_z(value, k):
        pairs = [(i, i ^ (k * parts)) for i in range(devices)]
        return lax.ppermute(value, "node", pairs)

    def along_y(value):
        return lax.ppermute(value, "node", [(i, i ^ 2) for i in range(devices)])

    def along_core(value):
        return lax.ppermute(value, "node", [(i, i ^ 1) for i in range(devices)])

    ids = expert_ids.T
    groups = [[n_blocks - d, d] for d in range(1, n_blocks // 2)] + [[n_blocks // 2]]
    last = groups[-1][0]
    straight, across, results = {}, {}, {}
    both, home, kept, sent = {}, {}, {}, {}

    def compute(blocks, after):
        pieces = []
        for k in blocks:
            pieces += [straight[k], across[k], along_core(straight[k]), along_core(across[k])]
        out = run_experts(pieces, weights, after)
        for i, k in enumerate(blocks):
            sent[k] = out[4 * i + 3]
            both[k] = add(out[4 * i + 1], along_core(out[4 * i + 3]))
            kept[k] = out[4 * i], along_core(out[4 * i + 2])

    def go_home(k, after):
        home[k] = add(*kept[k], along_y(when(both[k], after)))
        results[k] = along_z(home[k], k) if k else home[k]

    buckets = list(pack(placement, ids, tokens, n_blocks, parts))
    weights = load((gate_weight, up_weight, down_weight), buckets[0])
    straight[0] = buckets[0]
    across[0] = along_y(straight[0])
    second = None
    for g, group in enumerate(groups):
        first = group[0]
        if g == 0:
            straight[first] = along_z(buckets[first], first)
            across[first] = along_y(straight[first])
            compute([0, first], [])
        else:
            previous = groups[g - 1][0]
            straight[first] = along_z(when(buckets[first], [straight[previous], across[0]]), first)
            straight[first] = when(straight[first], [across[second], across[previous]])
            across[first] = along_y(straight[first])
            go_home(previous, [])
            compute([second, first], [both[previous]])
            go_home(second, [])
        if len(group) > 1:
            second = group[1]
            straight[second] = along_z(when(buckets[second], [weights[0]] if g == 0 else []), second)
            across[second] = along_y(straight[second])
    go_home(last, [])
    marks = [along_core(token(results[group[0]])) for group in groups[:-1]]
    results[last] = results[last].astype(jnp.float32)
    go_home(0, [home[last]])
    results = [results[k] for k in range(n_blocks)]
    return mix(placement, ids, gates.T, results, marks, n_blocks, parts)


def solution(mesh):
    placed = (
        P(("group", "node"), None),
        P(("group", "node"), None),
        P(("group", "node"), None),
        P(),
        P(None, "node"),
        P(None, "node"),
        P("node", None),
    )
    return jax.shard_map(
        local, mesh=mesh, in_specs=placed, out_specs=P(("group", "node"), None), check_vma=False
    )
```

```python
import functools

import jax
import jax.numpy as jnp
from jax import lax
from jax.experimental import pallas as pl
from jax.experimental.pallas import tpu as pltpu
from jax.sharding import PartitionSpec as P

VMEM_BYTES = 24 * 2**20
VMEM = pl.BlockSpec(memory_space=pltpu.VMEM)
SMEM = pl.BlockSpec(memory_space=pltpu.SMEM)
ANYWHERE = pl.BlockSpec(memory_space=pl.ANY)
LOADS = 4
N1, N2, N3, N4 = 30,30,30,30
NO_COST = pl.CostEstimate(flops=0, bytes_accessed=0, transcendentals=0)


def in_vmem(value):
    return pltpu.with_memory_space_constraint(value, pltpu.VMEM)


def in_hbm(value):
    return pltpu.with_memory_space_constraint(value, pltpu.HBM)


def product(lhs, rhs):
    return jnp.dot(lhs, rhs, preferred_element_type=jnp.float32)


def slots_of(ids, n_blocks):
    top, rows = ids.shape
    experts = lax.broadcasted_iota(jnp.int32, (n_blocks, rows), 0)
    picks = jnp.zeros((n_blocks, rows), jnp.float32)
    for k in range(top):
        picks = picks + jnp.where(ids[k : k + 1, :] == experts, 1.0, 0.0)
    before = lax.broadcasted_iota(jnp.int32, (rows, rows), 0) < lax.broadcasted_iota(
        jnp.int32, (rows, rows), 1
    )
    earlier = product(picks.astype(jnp.bfloat16), jnp.where(before, 1.0, 0.0).astype(jnp.bfloat16))
    return experts, picks, earlier


def expert_at(placement_ref, block):
    found = jnp.int32(0)
    for e in range(placement_ref.shape[0]):
        found = jnp.where(placement_ref[e] == block, jnp.int32(e), found)
    return found


def row_of(values, experts, expert):
    return jnp.sum(jnp.where(experts == expert, values, 0.0), axis=0, keepdims=True)


def bucket_rows(rows):
    row = lax.broadcasted_iota(jnp.int32, (rows, rows), 0)
    half, quarter = rows // 2, rows // 4
    return jnp.where(row < half, row, half + row % quarter).astype(jnp.float32)


def pack_kernel(n_blocks, parts, placement_ref, ids_ref, tokens_ref, *out_refs):
    rows, width = tokens_ref.shape
    half, quarter = rows // 2, rows // 4
    block = lax.axis_index("node") // parts
    experts, picks, earlier = slots_of(ids_ref[...], n_blocks)
    wanted = bucket_rows(rows)
    upper = lax.broadcasted_iota(jnp.int32, (half, width // 2), 0) < quarter
    for k, out_ref in enumerate(out_refs):
        expert = expert_at(placement_ref, lax.bitwise_xor(block, jnp.int32(k)))
        named = row_of(picks, experts, expert) > 0.5
        slot = row_of(earlier, experts, expert)
        chooser = jnp.where(named & (slot == wanted), 1.0, 0.0).astype(jnp.bfloat16)
        packed = product(chooser, tokens_ref[...])
        out_ref[:, :width] = packed[:half].astype(jnp.bfloat16)
        rest = jnp.where(upper, packed[half:, : width // 2], packed[half:, width // 2 :])
        out_ref[:, width:] = rest.astype(jnp.bfloat16)


def pack(placement, ids, tokens, n_blocks, parts):
    rows, width = tokens.shape
    shape = pltpu.VMEM((rows // 2, width + width // 2), jnp.bfloat16)
    return pl.pallas_call(
        functools.partial(pack_kernel, n_blocks, parts),
        out_shape=[shape] * n_blocks,
        in_specs=[SMEM, VMEM, VMEM],
        out_specs=[VMEM] * n_blocks,
        compiler_params=pltpu.CompilerParams(vmem_limit_bytes=VMEM_BYTES),
        cost_estimate=NO_COST,
    )(in_hbm(placement), in_hbm(ids), in_hbm(tokens))


def nothing(*refs):
    pass


def clear(*refs):
    refs[-1][...] = jnp.zeros_like(refs[-1])


def token(after, percent):
    rows, width = after.shape
    return pl.pallas_call(
        clear,
        out_shape=pltpu.VMEM((rows, width * percent // 12800 * 128), after.dtype),
        in_specs=[ANYWHERE],
        out_specs=VMEM,
        compiler_params=pltpu.CompilerParams(vmem_limit_bytes=VMEM_BYTES),
        cost_estimate=NO_COST,
    )(after)


def when(value, after):
    if not after:
        return value
    return pl.pallas_call(
        nothing,
        out_shape=pltpu.VMEM(value.shape, value.dtype),
        in_specs=[ANYWHERE] * (1 + len(after)),
        out_specs=ANYWHERE,
        input_output_aliases={0: 0},
        compiler_params=pltpu.CompilerParams(vmem_limit_bytes=VMEM_BYTES),
        cost_estimate=NO_COST,
    )(in_vmem(value), *after)


def load_kernel(*refs):
    sources, targets, sems = refs[:3], refs[4:7], refs[7]
    copies = []
    for i, (source, target) in enumerate(zip(sources, targets)):
        rows = source.shape[0] // LOADS
        for j in range(LOADS):
            part = pl.ds(j * rows, rows)
            copies.append(pltpu.make_async_copy(source.at[part], target.at[part], sems.at[i, j]))
    for copy in copies:
        copy.start()
    for copy in copies:
        copy.wait()


def load(weights, after):
    return pl.pallas_call(
        load_kernel,
        out_shape=[pltpu.VMEM(w.shape, w.dtype) for w in weights],
        in_specs=[pl.BlockSpec(memory_space=pltpu.HBM)] * 3 + [ANYWHERE],
        out_specs=[VMEM] * 3,
        scratch_shapes=[pltpu.SemaphoreType.DMA((3, LOADS))],
        compiler_params=pltpu.CompilerParams(vmem_limit_bytes=VMEM_BYTES),
        cost_estimate=NO_COST,
    )(*[pltpu.with_memory_space_constraint(w, pltpu.HBM) for w in weights], after)


def experts_kernel(count, *refs):
    pieces = refs[:count]
    gate_ref, up_ref, down_ref = refs[count : count + 3]
    out_refs = refs[-count:]
    width, hid = gate_ref.shape
    middle = width // 2
    height = pieces[0].shape[0]
    total = count * height
    rest = jnp.concatenate([p[:, width:] for p in pieces], axis=0)
    left = jnp.concatenate([p[:, :middle] for p in pieces] + [rest], axis=0)
    right = jnp.concatenate([p[:, middle:width] for p in pieces] + [rest], axis=0)
    upper = lax.broadcasted_iota(jnp.int32, (total, 1), 0) % height < height // 2
    shift = height // 2

    def whole_rows(ref):
        a, b = product(left, ref[:middle, :]), product(right, ref[middle:, :])
        tail = jnp.where(
            upper,
            a[total:] + pltpu.roll(b[total:], total - shift, axis=0),
            b[total:] + pltpu.roll(a[total:], shift, axis=0),
        )
        return jnp.concatenate([a[:total] + b[:total], tail], axis=0)

    gate_rows, up_rows = whole_rows(gate_ref), whole_rows(up_ref)
    hidden = (jax.nn.silu(gate_rows) * up_rows).astype(jnp.bfloat16)

    def store(start, values):
        values = values.astype(jnp.bfloat16)
        stop = start + values.shape[1]
        for i, out_ref in enumerate(out_refs):
            out_ref[:, start:stop] = values[i * height : (i + 1) * height]

    step = middle // 4
    for i in range(4):
        begin = i * step
        a = product(hidden, down_ref[:, begin : begin + step])
        b = product(hidden, down_ref[:, middle + begin : middle + begin + step])
        store(begin, a[:total])
        store(middle + begin, b[:total])
        store(width + begin, jnp.where(upper, a[total:], b[total:]))


def run_experts(pieces, weights, after):
    count = len(pieces)
    shape = pltpu.VMEM(pieces[0].shape, jnp.bfloat16)
    operands = [in_vmem(value) for value in [*pieces, *weights]]
    return pl.pallas_call(
        functools.partial(experts_kernel, count),
        out_shape=[shape] * count,
        in_specs=[VMEM] * len(operands) + [ANYWHERE] * len(after),
        out_specs=[VMEM] * count,
        compiler_params=pltpu.CompilerParams(vmem_limit_bytes=VMEM_BYTES),
        cost_estimate=NO_COST,
    )(*operands, *after)


def mix_kernel(n_blocks, parts, placement_ref, ids_ref, gates_ref, *refs):
    results, out_ref = refs[:n_blocks], refs[-1]
    rows, width = out_ref.shape
    half, quarter, middle = rows // 2, rows // 4, width // 2
    block = lax.axis_index("node") // parts
    ids, gates = ids_ref[...], gates_ref[...]
    experts, picks, earlier = slots_of(ids, n_blocks)
    wanted = bucket_rows(rows)
    terms = []
    for k in range(n_blocks):
        expert = expert_at(placement_ref, lax.bitwise_xor(block, jnp.int32(k)))
        named = row_of(picks, experts, expert) > 0.5
        slot = row_of(earlier, experts, expert)
        weight = jnp.sum(jnp.where(ids == expert, gates, 0.0), axis=0, keepdims=True)
        terms.append(jnp.where(named & (slot == wanted), weight, 0.0))
    term = jnp.concatenate(terms, axis=0)
    row = lax.broadcasted_iota(jnp.int32, term.shape, 0) % rows
    for side in range(2):
        first = half + side * quarter
        mine = jnp.where((row < half) | ((row >= first) & (row < first + quarter)), term, 0.0)
        high = mine.astype(jnp.bfloat16)
        lower = mine - high.astype(jnp.float32)
        mid = lower.astype(jnp.bfloat16)
        low = (lower - mid.astype(jnp.float32)).astype(jnp.bfloat16)
        lhs = jnp.concatenate([high, mid, low], axis=1)
        pieces = []
        for r in results:
            pieces += [r[:, side * middle : (side + 1) * middle], r[:, width:]]
        rhs = jnp.concatenate([p.astype(jnp.bfloat16) for p in pieces], axis=0)
        value = lax.dot_general(
            lhs, rhs, (((0,), (0,)), ((), ())), preferred_element_type=jnp.float32
        )
        value = value[:rows] + value[rows : 2 * rows] + value[2 * rows :]
        out_ref[:, side * middle : (side + 1) * middle] = value.astype(jnp.bfloat16)


def mix(placement, ids, gates, results, after, n_blocks, parts):
    rows = ids.shape[1]
    width = results[0].shape[1] // 3 * 2
    return pl.pallas_call(
        functools.partial(mix_kernel, n_blocks, parts),
        out_shape=jax.ShapeDtypeStruct((rows, width), jnp.bfloat16),
        in_specs=[SMEM] + [VMEM] * (2 + n_blocks) + [ANYWHERE] * len(after),
        out_specs=VMEM,
        compiler_params=pltpu.CompilerParams(vmem_limit_bytes=VMEM_BYTES),
        cost_estimate=pl.CostEstimate(
            flops=6 * n_blocks * rows * rows * width,
            bytes_accessed=2 * (n_blocks + 1) * rows * width,
            transcendentals=0,
        ),
    )(placement, ids, gates, *[in_vmem(r) for r in results], *after)


def add_kernel(*refs):
    total = refs[0][...].astype(jnp.float32)
    for ref in refs[1:-1]:
        total = total + ref[...].astype(jnp.float32)
    refs[-1][...] = total.astype(refs[-1].dtype)


def add(*values):
    return pl.pallas_call(
        add_kernel,
        out_shape=pltpu.VMEM(values[0].shape, values[0].dtype),
        in_specs=[VMEM] * len(values),
        out_specs=VMEM,
        compiler_params=pltpu.CompilerParams(vmem_limit_bytes=VMEM_BYTES),
        cost_estimate=NO_COST,
    )(*[in_vmem(v) for v in values])


def local(tokens, expert_ids, gates, placement, gate_weight, up_weight, down_weight):
    n_blocks = placement.shape[0]
    devices = lax.axis_size("node")
    parts = devices // n_blocks

    def along_z(value, k):
        pairs = [(i, i ^ (k * parts)) for i in range(devices)]
        return lax.ppermute(value, "node", pairs)

    def along_y(value):
        return lax.ppermute(value, "node", [(i, i ^ 2) for i in range(devices)])

    def along_core(value):
        return lax.ppermute(value, "node", [(i, i ^ 1) for i in range(devices)])

    ids = expert_ids.T
    groups = [[n_blocks - d, d] for d in range(1, n_blocks // 2)] + [[n_blocks // 2]]
    last, early = groups[-1][0], [group[0] for group in groups[:-1]]
    straight, across, results = {}, {}, {}
    both, home, kept, sent = {}, {}, {}, {}

    def compute(blocks, after):
        pieces = []
        for k in blocks:
            pieces += [straight[k], across[k], along_core(straight[k]), along_core(across[k])]
        out = run_experts(pieces, weights, after)
        for i, k in enumerate(blocks):
            sent[k] = out[4 * i + 3]
            both[k] = add(out[4 * i + 1], along_core(out[4 * i + 3]))
            kept[k] = out[4 * i], along_core(out[4 * i + 2])

    def go_home(k, after):
        home[k] = add(*kept[k], along_y(when(both[k], after)))
        if k in early:
            home[k] = when(home[k], [along_core(token(home[k], 20))])
        results[k] = along_z(home[k], k) if k else home[k]

    buckets = list(pack(placement, ids, tokens, n_blocks, parts))
    weights = load((gate_weight, up_weight, down_weight), buckets[0])
    straight[0] = buckets[0]
    across[0] = along_y(straight[0])
    second = None
    for g, group in enumerate(groups):
        first = group[0]
        if g == 0:
            straight[first] = along_z(buckets[first], first)
            across[first] = along_y(straight[first])
            compute([0, first], [])
        else:
            previous = groups[g - 1][0]
            straight[first] = along_z(when(buckets[first], [straight[previous]]), first)
            straight[first] = when(straight[first], [across[second], across[previous]])
            across[first] = along_y(straight[first])
            go_home(previous, [])
            compute([second, first], [both[previous]])
            go_home(second, [])
        if len(group) > 1:
            second = group[1]
            straight[second] = along_z(when(buckets[second], [weights[0]] if g == 0 else []), second)
            across[second] = along_y(straight[second])
    go_home(last, [])
    marks = [along_core(token(results[k], 85)) for k in early]
    go_home(0, [home[last]])
    results = [results[k] for k in range(n_blocks)]
    return mix(placement, ids, gates.T, results, marks, n_blocks, parts)


def solution(mesh):
    placed = (
        P(("group", "node"), None),
        P(("group", "node"), None),
        P(("group", "node"), None),
        P(),
        P(None, "node"),
        P(None, "node"),
        P("node", None),
    )
    return jax.shard_map(
        local, mesh=mesh, in_specs=placed, out_specs=P(("group", "node"), None), check_vma=False
    )
```

```python
import functools

import jax
import jax.numpy as jnp
from jax import lax
from jax.experimental import pallas as pl
from jax.experimental.pallas import tpu as pltpu
from jax.sharding import PartitionSpec as P

VMEM_BYTES = 24 * 2**20
VMEM = pl.BlockSpec(memory_space=pltpu.VMEM)
SMEM = pl.BlockSpec(memory_space=pltpu.SMEM)
ANYWHERE = pl.BlockSpec(memory_space=pl.ANY)
LOADS = 4
EXTRA = 512
SHARE = 94
N1, N2, N3, N4 = 30,30,30,30
NO_COST = pl.CostEstimate(flops=0, bytes_accessed=0, transcendentals=0)


def in_vmem(value):
    return pltpu.with_memory_space_constraint(value, pltpu.VMEM)


def in_hbm(value):
    return pltpu.with_memory_space_constraint(value, pltpu.HBM)


def product(lhs, rhs):
    return jnp.dot(lhs, rhs, preferred_element_type=jnp.float32)


def slots_of(ids, n_blocks):
    top, rows = ids.shape
    experts = lax.broadcasted_iota(jnp.int32, (n_blocks, rows), 0)
    picks = jnp.zeros((n_blocks, rows), jnp.float32)
    for k in range(top):
        picks = picks + jnp.where(ids[k : k + 1, :] == experts, 1.0, 0.0)
    before = lax.broadcasted_iota(jnp.int32, (rows, rows), 0) < lax.broadcasted_iota(
        jnp.int32, (rows, rows), 1
    )
    earlier = product(picks.astype(jnp.bfloat16), jnp.where(before, 1.0, 0.0).astype(jnp.bfloat16))
    return experts, picks, earlier


def expert_at(placement_ref, block):
    found = jnp.int32(0)
    for e in range(placement_ref.shape[0]):
        found = jnp.where(placement_ref[e] == block, jnp.int32(e), found)
    return found


def row_of(values, experts, expert):
    return jnp.sum(jnp.where(experts == expert, values, 0.0), axis=0, keepdims=True)


def bucket_rows(rows):
    row = lax.broadcasted_iota(jnp.int32, (rows, rows), 0)
    half, quarter = rows // 2, rows // 4
    return jnp.where(row < half, row, half + row % quarter).astype(jnp.float32)


def pack_kernel(n_blocks, parts, placement_ref, ids_ref, tokens_ref, *out_refs):
    rows, width = tokens_ref.shape
    half, quarter = rows // 2, rows // 4
    block = lax.axis_index("node") // parts
    experts, picks, earlier = slots_of(ids_ref[...], n_blocks)
    wanted = bucket_rows(rows)
    upper = lax.broadcasted_iota(jnp.int32, (half, width // 2), 0) < quarter
    for k, out_ref in enumerate(out_refs):
        expert = expert_at(placement_ref, lax.bitwise_xor(block, jnp.int32(k)))
        named = row_of(picks, experts, expert) > 0.5
        slot = row_of(earlier, experts, expert)
        chooser = jnp.where(named & (slot == wanted), 1.0, 0.0).astype(jnp.bfloat16)
        packed = product(chooser, tokens_ref[...])
        out_ref[:, :width] = packed[:half].astype(jnp.bfloat16)
        rest = jnp.where(upper, packed[half:, : width // 2], packed[half:, width // 2 :])
        out_ref[:, width:] = rest.astype(jnp.bfloat16)


def pack(placement, ids, tokens, n_blocks, parts):
    rows, width = tokens.shape
    shape = pltpu.VMEM((rows // 2, width + width // 2), jnp.bfloat16)
    return pl.pallas_call(
        functools.partial(pack_kernel, n_blocks, parts),
        out_shape=[shape] * n_blocks,
        in_specs=[SMEM, VMEM, VMEM],
        out_specs=[VMEM] * n_blocks,
        compiler_params=pltpu.CompilerParams(vmem_limit_bytes=VMEM_BYTES),
        cost_estimate=NO_COST,
    )(in_hbm(placement), in_hbm(ids), in_hbm(tokens))


def nothing(*refs):
    pass


def clear(*refs):
    refs[-1][...] = jnp.zeros_like(refs[-1])


def token(after, percent):
    rows, width = after.shape
    return pl.pallas_call(
        clear,
        out_shape=pltpu.VMEM((rows, width * percent // 12800 * 128), after.dtype),
        in_specs=[ANYWHERE],
        out_specs=VMEM,
        compiler_params=pltpu.CompilerParams(vmem_limit_bytes=VMEM_BYTES),
        cost_estimate=NO_COST,
    )(after)


def when(value, after):
    if not after:
        return value
    return pl.pallas_call(
        nothing,
        out_shape=pltpu.VMEM(value.shape, value.dtype),
        in_specs=[ANYWHERE] * (1 + len(after)),
        out_specs=ANYWHERE,
        input_output_aliases={0: 0},
        compiler_params=pltpu.CompilerParams(vmem_limit_bytes=VMEM_BYTES),
        cost_estimate=NO_COST,
    )(in_vmem(value), *after)


def load_kernel(*refs):
    sources, targets, sems = refs[:3], refs[4:7], refs[7]
    copies = []
    for i, (source, target) in enumerate(zip(sources, targets)):
        rows = source.shape[0] // LOADS
        for j in range(LOADS):
            part = pl.ds(j * rows, rows)
            copies.append(pltpu.make_async_copy(source.at[part], target.at[part], sems.at[i, j]))
    for copy in copies:
        copy.start()
    for copy in copies:
        copy.wait()


def load(weights, after):
    return pl.pallas_call(
        load_kernel,
        out_shape=[pltpu.VMEM(w.shape, w.dtype) for w in weights],
        in_specs=[pl.BlockSpec(memory_space=pltpu.HBM)] * 3 + [ANYWHERE],
        out_specs=[VMEM] * 3,
        scratch_shapes=[pltpu.SemaphoreType.DMA((3, LOADS))],
        compiler_params=pltpu.CompilerParams(vmem_limit_bytes=VMEM_BYTES),
        cost_estimate=NO_COST,
    )(*[pltpu.with_memory_space_constraint(w, pltpu.HBM) for w in weights], after)


def experts_kernel(count, *refs):
    pieces = refs[:count]
    gate_ref, up_ref, down_ref = refs[count : count + 3]
    out_refs = refs[-count:]
    width, hid = gate_ref.shape
    middle = width // 2
    height = pieces[0].shape[0]
    total = count * height
    rest = jnp.concatenate([p[:, width:] for p in pieces], axis=0)
    left = jnp.concatenate([p[:, :middle] for p in pieces] + [rest], axis=0)
    right = jnp.concatenate([p[:, middle:width] for p in pieces] + [rest], axis=0)
    upper = lax.broadcasted_iota(jnp.int32, (total, 1), 0) % height < height // 2
    shift = height // 2

    def whole_rows(ref):
        a, b = product(left, ref[:middle, :]), product(right, ref[middle:, :])
        tail = jnp.where(
            upper,
            a[total:] + pltpu.roll(b[total:], total - shift, axis=0),
            b[total:] + pltpu.roll(a[total:], shift, axis=0),
        )
        return jnp.concatenate([a[:total] + b[:total], tail], axis=0)

    gate_rows, up_rows = whole_rows(gate_ref), whole_rows(up_ref)
    hidden = (jax.nn.silu(gate_rows) * up_rows).astype(jnp.bfloat16)

    def store(start, values):
        values = values.astype(jnp.bfloat16)
        stop = start + values.shape[1]
        for i, out_ref in enumerate(out_refs):
            out_ref[:, start:stop] = values[i * height : (i + 1) * height]

    step = middle // 4
    for i in range(4):
        begin = i * step
        a = product(hidden, down_ref[:, begin : begin + step])
        b = product(hidden, down_ref[:, middle + begin : middle + begin + step])
        store(begin, a[:total])
        store(middle + begin, b[:total])
        store(width + begin, jnp.where(upper, a[total:], b[total:]))


def run_experts(pieces, weights, after):
    count = len(pieces)
    shape = pltpu.VMEM(pieces[0].shape, jnp.bfloat16)
    operands = [in_vmem(value) for value in [*pieces, *weights]]
    return pl.pallas_call(
        functools.partial(experts_kernel, count),
        out_shape=[shape] * count,
        in_specs=[VMEM] * len(operands) + [ANYWHERE] * len(after),
        out_specs=[VMEM] * count,
        compiler_params=pltpu.CompilerParams(vmem_limit_bytes=VMEM_BYTES),
        cost_estimate=NO_COST,
    )(*operands, *after)


def mix_kernel(n_blocks, parts, placement_ref, ids_ref, gates_ref, *refs):
    results, out_ref = refs[:n_blocks], refs[-1]
    rows, width = out_ref.shape
    half, quarter, middle = rows // 2, rows // 4, width // 2
    block = lax.axis_index("node") // parts
    ids, gates = ids_ref[...], gates_ref[...]
    experts, picks, earlier = slots_of(ids, n_blocks)
    wanted = bucket_rows(rows)
    terms = []
    for k in range(n_blocks):
        expert = expert_at(placement_ref, lax.bitwise_xor(block, jnp.int32(k)))
        named = row_of(picks, experts, expert) > 0.5
        slot = row_of(earlier, experts, expert)
        weight = jnp.sum(jnp.where(ids == expert, gates, 0.0), axis=0, keepdims=True)
        terms.append(jnp.where(named & (slot == wanted), weight, 0.0))
    term = jnp.concatenate(terms, axis=0)
    row = lax.broadcasted_iota(jnp.int32, term.shape, 0) % rows
    for side in range(2):
        first = half + side * quarter
        mine = jnp.where((row < half) | ((row >= first) & (row < first + quarter)), term, 0.0)
        high = mine.astype(jnp.bfloat16)
        lower = mine - high.astype(jnp.float32)
        mid = lower.astype(jnp.bfloat16)
        low = (lower - mid.astype(jnp.float32)).astype(jnp.bfloat16)
        lhs = jnp.concatenate([high, mid, low], axis=1)
        pieces = []
        for r in results:
            pieces += [r[:, side * middle : (side + 1) * middle], r[:, width : width + middle]]
        rhs = jnp.concatenate([p.astype(jnp.bfloat16) for p in pieces], axis=0)
        value = lax.dot_general(
            lhs, rhs, (((0,), (0,)), ((), ())), preferred_element_type=jnp.float32
        )
        value = value[:rows] + value[rows : 2 * rows] + value[2 * rows :]
        out_ref[:, side * middle : (side + 1) * middle] = value.astype(jnp.bfloat16)


def mix(placement, ids, gates, results, after, n_blocks, parts):
    rows = ids.shape[1]
    width = results[0].shape[1] // 3 * 2
    return pl.pallas_call(
        functools.partial(mix_kernel, n_blocks, parts),
        out_shape=jax.ShapeDtypeStruct((rows, width), jnp.bfloat16),
        in_specs=[SMEM] + [VMEM] * (2 + n_blocks) + [ANYWHERE] * len(after),
        out_specs=VMEM,
        compiler_params=pltpu.CompilerParams(vmem_limit_bytes=VMEM_BYTES),
        cost_estimate=pl.CostEstimate(
            flops=6 * n_blocks * rows * rows * width,
            bytes_accessed=2 * (n_blocks + 1) * rows * width,
            transcendentals=0,
        ),
    )(placement, ids, gates, *[in_vmem(r) for r in results], *after)


def add_kernel(*refs):
    total = refs[0][...].astype(jnp.float32)
    for ref in refs[1:-1]:
        total = total + ref[...].astype(jnp.float32)
    width = total.shape[1]
    refs[-1][:, :width] = total.astype(refs[-1].dtype)
    if refs[-1].shape[1] > width:
        refs[-1][:, width:] = jnp.zeros_like(refs[-1][:, width:])


def add(*values, extra=0):
    rows, width = values[0].shape
    return pl.pallas_call(
        add_kernel,
        out_shape=pltpu.VMEM((rows, width + extra), values[0].dtype),
        in_specs=[VMEM] * len(values),
        out_specs=VMEM,
        compiler_params=pltpu.CompilerParams(vmem_limit_bytes=VMEM_BYTES),
        cost_estimate=NO_COST,
    )(*[in_vmem(v) for v in values])


def local(tokens, expert_ids, gates, placement, gate_weight, up_weight, down_weight):
    n_blocks = placement.shape[0]
    devices = lax.axis_size("node")
    parts = devices // n_blocks

    def along_z(value, k):
        pairs = [(i, i ^ (k * parts)) for i in range(devices)]
        return lax.ppermute(value, "node", pairs)

    def along_y(value):
        return lax.ppermute(value, "node", [(i, i ^ 2) for i in range(devices)])

    def along_core(value):
        return lax.ppermute(value, "node", [(i, i ^ 1) for i in range(devices)])

    ids = expert_ids.T
    groups = [[n_blocks - d, d] for d in range(1, n_blocks // 2)] + [[n_blocks // 2]]
    last, early = groups[-1][0], [group[0] for group in groups[:-1]]
    straight, across, results = {}, {}, {}
    both, home, kept, sent = {}, {}, {}, {}

    def compute(blocks, after):
        pieces = []
        for k in blocks:
            pieces += [straight[k], across[k], along_core(straight[k]), along_core(across[k])]
        out = run_experts(pieces, weights, after)
        for i, k in enumerate(blocks):
            sent[k] = out[4 * i + 3]
            both[k] = add(out[4 * i + 1], along_core(out[4 * i + 3]))
            kept[k] = out[4 * i], along_core(out[4 * i + 2])

    def go_home(k, after):
        back = along_y(when(both[k], after))
        home[k] = add(*kept[k], back, extra=EXTRA if k in early else 0)
        results[k] = along_z(home[k], k) if k else home[k]

    buckets = list(pack(placement, ids, tokens, n_blocks, parts))
    weights = load((gate_weight, up_weight, down_weight), buckets[0])
    straight[0] = buckets[0]
    across[0] = along_y(straight[0])
    second = None
    for g, group in enumerate(groups):
        first = group[0]
        if g == 0:
            straight[first] = along_z(buckets[first], first)
            across[first] = along_y(straight[first])
            compute([0, first], [])
        else:
            previous = groups[g - 1][0]
            straight[first] = along_z(when(buckets[first], [straight[previous]]), first)
            straight[first] = when(straight[first], [across[second], across[previous]])
            across[first] = along_y(straight[first])
            go_home(previous, [])
            compute([second, first], [both[previous]])
            go_home(second, [])
        if len(group) > 1:
            second = group[1]
            straight[second] = along_z(when(buckets[second], [weights[0]] if g == 0 else []), second)
            across[second] = along_y(straight[second])
    go_home(last, [])
    marks = [along_core(token(results[k], SHARE)) for k in early]
    go_home(0, [home[last]])
    results = [results[k] for k in range(n_blocks)]
    return mix(placement, ids, gates.T, results, marks, n_blocks, parts)


def solution(mesh):
    placed = (
        P(("group", "node"), None),
        P(("group", "node"), None),
        P(("group", "node"), None),
        P(),
        P(None, "node"),
        P(None, "node"),
        P("node", None),
    )
    return jax.shard_map(
        local, mesh=mesh, in_specs=placed, out_specs=P(("group", "node"), None), check_vma=False
    )
```

```python
import functools

import jax
import jax.numpy as jnp
from jax import lax
from jax.experimental import pallas as pl
from jax.experimental.pallas import tpu as pltpu
from jax.sharding import PartitionSpec as P

VMEM_BYTES = 24 * 2**20
VMEM = pl.BlockSpec(memory_space=pltpu.VMEM)
SMEM = pl.BlockSpec(memory_space=pltpu.SMEM)
ANYWHERE = pl.BlockSpec(memory_space=pl.ANY)
LOADS = 4
N1, N2, N3, N4 = 30,30,30,30
NO_COST = pl.CostEstimate(flops=0, bytes_accessed=0, transcendentals=0)


def in_vmem(value):
    return pltpu.with_memory_space_constraint(value, pltpu.VMEM)


def in_hbm(value):
    return pltpu.with_memory_space_constraint(value, pltpu.HBM)


def product(lhs, rhs):
    return jnp.dot(lhs, rhs, preferred_element_type=jnp.float32)


def slots_of(ids, n_blocks):
    top, rows = ids.shape
    experts = lax.broadcasted_iota(jnp.int32, (n_blocks, rows), 0)
    picks = jnp.zeros((n_blocks, rows), jnp.float32)
    for k in range(top):
        picks = picks + jnp.where(ids[k : k + 1, :] == experts, 1.0, 0.0)
    before = lax.broadcasted_iota(jnp.int32, (rows, rows), 0) < lax.broadcasted_iota(
        jnp.int32, (rows, rows), 1
    )
    earlier = product(picks.astype(jnp.bfloat16), jnp.where(before, 1.0, 0.0).astype(jnp.bfloat16))
    return experts, picks, earlier


def expert_at(placement_ref, block):
    found = jnp.int32(0)
    for e in range(placement_ref.shape[0]):
        found = jnp.where(placement_ref[e] == block, jnp.int32(e), found)
    return found


def row_of(values, experts, expert):
    return jnp.sum(jnp.where(experts == expert, values, 0.0), axis=0, keepdims=True)


def bucket_rows(rows):
    row = lax.broadcasted_iota(jnp.int32, (rows, rows), 0)
    half, quarter = rows // 2, rows // 4
    return jnp.where(row < half, row, half + row % quarter).astype(jnp.float32)


def pack_kernel(n_blocks, parts, placement_ref, ids_ref, tokens_ref, *out_refs):
    rows, width = tokens_ref.shape
    half, quarter = rows // 2, rows // 4
    block = lax.axis_index("node") // parts
    experts, picks, earlier = slots_of(ids_ref[...], n_blocks)
    wanted = bucket_rows(rows)
    upper = lax.broadcasted_iota(jnp.int32, (half, width // 2), 0) < quarter
    for k, out_ref in enumerate(out_refs):
        expert = expert_at(placement_ref, lax.bitwise_xor(block, jnp.int32(k)))
        named = row_of(picks, experts, expert) > 0.5
        slot = row_of(earlier, experts, expert)
        chooser = jnp.where(named & (slot == wanted), 1.0, 0.0).astype(jnp.bfloat16)
        packed = product(chooser, tokens_ref[...])
        out_ref[:, :width] = packed[:half].astype(jnp.bfloat16)
        rest = jnp.where(upper, packed[half:, : width // 2], packed[half:, width // 2 :])
        out_ref[:, width:] = rest.astype(jnp.bfloat16)


def pack(placement, ids, tokens, n_blocks, parts):
    rows, width = tokens.shape
    shape = pltpu.VMEM((rows // 2, width + width // 2), jnp.bfloat16)
    return pl.pallas_call(
        functools.partial(pack_kernel, n_blocks, parts),
        out_shape=[shape] * n_blocks,
        in_specs=[SMEM, VMEM, VMEM],
        out_specs=[VMEM] * n_blocks,
        compiler_params=pltpu.CompilerParams(vmem_limit_bytes=VMEM_BYTES),
        cost_estimate=NO_COST,
    )(in_hbm(placement), in_hbm(ids), in_hbm(tokens))


def nothing(*refs):
    pass


def clear(*refs):
    refs[-1][...] = jnp.zeros_like(refs[-1])


def token(after, percent):
    rows, width = after.shape
    return pl.pallas_call(
        clear,
        out_shape=pltpu.VMEM((rows, width * percent // 12800 * 128), after.dtype),
        in_specs=[ANYWHERE],
        out_specs=VMEM,
        compiler_params=pltpu.CompilerParams(vmem_limit_bytes=VMEM_BYTES),
        cost_estimate=NO_COST,
    )(after)


def when(value, after):
    if not after:
        return value
    return pl.pallas_call(
        nothing,
        out_shape=pltpu.VMEM(value.shape, value.dtype),
        in_specs=[ANYWHERE] * (1 + len(after)),
        out_specs=ANYWHERE,
        input_output_aliases={0: 0},
        compiler_params=pltpu.CompilerParams(vmem_limit_bytes=VMEM_BYTES),
        cost_estimate=NO_COST,
    )(in_vmem(value), *after)


def load_kernel(*refs):
    sources, targets, sems = refs[:3], refs[4:7], refs[7]
    copies = []
    for i, (source, target) in enumerate(zip(sources, targets)):
        rows = source.shape[0] // LOADS
        for j in range(LOADS):
            part = pl.ds(j * rows, rows)
            copies.append(pltpu.make_async_copy(source.at[part], target.at[part], sems.at[i, j]))
    for copy in copies:
        copy.start()
    for copy in copies:
        copy.wait()


def load(weights, after):
    return pl.pallas_call(
        load_kernel,
        out_shape=[pltpu.VMEM(w.shape, w.dtype) for w in weights],
        in_specs=[pl.BlockSpec(memory_space=pltpu.HBM)] * 3 + [ANYWHERE],
        out_specs=[VMEM] * 3,
        scratch_shapes=[pltpu.SemaphoreType.DMA((3, LOADS))],
        compiler_params=pltpu.CompilerParams(vmem_limit_bytes=VMEM_BYTES),
        cost_estimate=NO_COST,
    )(*[pltpu.with_memory_space_constraint(w, pltpu.HBM) for w in weights], after)


def experts_kernel(count, *refs):
    pieces = refs[:count]
    gate_ref, up_ref, down_ref = refs[count : count + 3]
    out_refs = refs[-count:]
    width, hid = gate_ref.shape
    middle = width // 2
    height = pieces[0].shape[0]
    total = count * height
    rest = jnp.concatenate([p[:, width:] for p in pieces], axis=0)
    left = jnp.concatenate([p[:, :middle] for p in pieces] + [rest], axis=0)
    right = jnp.concatenate([p[:, middle:width] for p in pieces] + [rest], axis=0)
    upper = lax.broadcasted_iota(jnp.int32, (total, 1), 0) % height < height // 2
    shift = height // 2

    def whole_rows(ref):
        a, b = product(left, ref[:middle, :]), product(right, ref[middle:, :])
        tail = jnp.where(
            upper,
            a[total:] + pltpu.roll(b[total:], total - shift, axis=0),
            b[total:] + pltpu.roll(a[total:], shift, axis=0),
        )
        return jnp.concatenate([a[:total] + b[:total], tail], axis=0)

    gate_rows, up_rows = whole_rows(gate_ref), whole_rows(up_ref)
    hidden = (jax.nn.silu(gate_rows) * up_rows).astype(jnp.bfloat16)

    def store(start, values):
        values = values.astype(jnp.bfloat16)
        stop = start + values.shape[1]
        for i, out_ref in enumerate(out_refs):
            out_ref[:, start:stop] = values[i * height : (i + 1) * height]

    step = middle // 4
    for i in range(4):
        begin = i * step
        a = product(hidden, down_ref[:, begin : begin + step])
        b = product(hidden, down_ref[:, middle + begin : middle + begin + step])
        store(begin, a[:total])
        store(middle + begin, b[:total])
        store(width + begin, jnp.where(upper, a[total:], b[total:]))


def run_experts(pieces, weights, after):
    count = len(pieces)
    shape = pltpu.VMEM(pieces[0].shape, jnp.bfloat16)
    operands = [in_vmem(value) for value in [*pieces, *weights]]
    return pl.pallas_call(
        functools.partial(experts_kernel, count),
        out_shape=[shape] * count,
        in_specs=[VMEM] * len(operands) + [ANYWHERE] * len(after),
        out_specs=[VMEM] * count,
        compiler_params=pltpu.CompilerParams(vmem_limit_bytes=VMEM_BYTES),
        cost_estimate=NO_COST,
    )(*operands, *after)


def mix_kernel(n_blocks, parts, placement_ref, ids_ref, gates_ref, *refs):
    results, out_ref = refs[:n_blocks], refs[-1]
    rows, width = out_ref.shape
    half, quarter, middle = rows // 2, rows // 4, width // 2
    block = lax.axis_index("node") // parts
    ids, gates = ids_ref[...], gates_ref[...]
    experts, picks, earlier = slots_of(ids, n_blocks)
    wanted = bucket_rows(rows)
    terms = []
    for k in range(n_blocks):
        expert = expert_at(placement_ref, lax.bitwise_xor(block, jnp.int32(k)))
        named = row_of(picks, experts, expert) > 0.5
        slot = row_of(earlier, experts, expert)
        weight = jnp.sum(jnp.where(ids == expert, gates, 0.0), axis=0, keepdims=True)
        terms.append(jnp.where(named & (slot == wanted), weight, 0.0))
    term = jnp.concatenate(terms, axis=0)
    row = lax.broadcasted_iota(jnp.int32, term.shape, 0) % rows
    for side in range(2):
        first = half + side * quarter
        mine = jnp.where((row < half) | ((row >= first) & (row < first + quarter)), term, 0.0)
        high = mine.astype(jnp.bfloat16)
        lower = mine - high.astype(jnp.float32)
        mid = lower.astype(jnp.bfloat16)
        low = (lower - mid.astype(jnp.float32)).astype(jnp.bfloat16)
        lhs = jnp.concatenate([high, mid, low], axis=1)
        pieces = []
        for r in results:
            pieces += [r[:, side * middle : (side + 1) * middle], r[:, width:]]
        rhs = jnp.concatenate([p.astype(jnp.bfloat16) for p in pieces], axis=0)
        value = lax.dot_general(
            lhs, rhs, (((0,), (0,)), ((), ())), preferred_element_type=jnp.float32
        )
        value = value[:rows] + value[rows : 2 * rows] + value[2 * rows :]
        out_ref[:, side * middle : (side + 1) * middle] = value.astype(jnp.bfloat16)


def mix(placement, ids, gates, results, after, n_blocks, parts):
    rows = ids.shape[1]
    width = results[0].shape[1] // 3 * 2
    return pl.pallas_call(
        functools.partial(mix_kernel, n_blocks, parts),
        out_shape=jax.ShapeDtypeStruct((rows, width), jnp.bfloat16),
        in_specs=[SMEM] + [VMEM] * (2 + n_blocks) + [ANYWHERE] * len(after),
        out_specs=VMEM,
        compiler_params=pltpu.CompilerParams(vmem_limit_bytes=VMEM_BYTES),
        cost_estimate=pl.CostEstimate(
            flops=6 * n_blocks * rows * rows * width,
            bytes_accessed=2 * (n_blocks + 1) * rows * width,
            transcendentals=0,
        ),
    )(placement, ids, gates, *[in_vmem(r) for r in results], *after)


def add_kernel(*refs):
    total = refs[0][...].astype(jnp.float32)
    for ref in refs[1:-1]:
        total = total + ref[...].astype(jnp.float32)
    refs[-1][...] = total.astype(refs[-1].dtype)


def add(*values):
    return pl.pallas_call(
        add_kernel,
        out_shape=pltpu.VMEM(values[0].shape, values[0].dtype),
        in_specs=[VMEM] * len(values),
        out_specs=VMEM,
        compiler_params=pltpu.CompilerParams(vmem_limit_bytes=VMEM_BYTES),
        cost_estimate=NO_COST,
    )(*[in_vmem(v) for v in values])


def local(tokens, expert_ids, gates, placement, gate_weight, up_weight, down_weight):
    n_blocks = placement.shape[0]
    devices = lax.axis_size("node")
    parts = devices // n_blocks

    def along_z(value, k):
        pairs = [(i, i ^ (k * parts)) for i in range(devices)]
        return lax.ppermute(value, "node", pairs)

    def along_y(value):
        return lax.ppermute(value, "node", [(i, i ^ 2) for i in range(devices)])

    def along_core(value):
        return lax.ppermute(value, "node", [(i, i ^ 1) for i in range(devices)])

    ids = expert_ids.T
    far = [n_blocks // 2] + [n_blocks - d for d in range(1, n_blocks // 2)]
    groups = [[far[d - 1], d] for d in range(1, n_blocks // 2)] + [far[-1:]]
    last, early = groups[-1][0], [group[0] for group in groups[:-1]]
    straight, across, results = {}, {}, {}
    both, home, kept, sent = {}, {}, {}, {}

    def compute(blocks, after):
        pieces = []
        for k in blocks:
            pieces += [straight[k], across[k], along_core(straight[k]), along_core(across[k])]
        out = run_experts(pieces, weights, after)
        for i, k in enumerate(blocks):
            sent[k] = out[4 * i + 3]
            both[k] = add(out[4 * i + 1], along_core(out[4 * i + 3]))
            kept[k] = out[4 * i], along_core(out[4 * i + 2])

    def go_home(k, after):
        home[k] = add(*kept[k], along_y(when(both[k], after)))
        if k in early:
            home[k] = when(home[k], [along_core(token(home[k], 20))])
        results[k] = along_z(home[k], k) if k else home[k]

    buckets = list(pack(placement, ids, tokens, n_blocks, parts))
    weights = load((gate_weight, up_weight, down_weight), buckets[0])
    straight[0] = buckets[0]
    across[0] = along_y(straight[0])
    second = None
    for g, group in enumerate(groups):
        first = group[0]
        if g == 0:
            straight[first] = along_z(buckets[first], first)
            across[first] = along_y(straight[first])
            compute([0, first], [])
        else:
            previous = groups[g - 1][0]
            straight[first] = along_z(when(buckets[first], [straight[previous]]), first)
            straight[first] = when(straight[first], [across[second], across[previous]])
            across[first] = along_y(straight[first])
            go_home(previous, [])
            compute([second, first], [both[previous]])
            go_home(second, [])
        if len(group) > 1:
            second = group[1]
            straight[second] = along_z(when(buckets[second], [weights[0]] if g == 0 else []), second)
            across[second] = along_y(straight[second])
    go_home(last, [])
    marks = [along_core(token(results[k], 85)) for k in early]
    go_home(0, [home[last]])
    results = [results[k] for k in range(n_blocks)]
    return mix(placement, ids, gates.T, results, marks, n_blocks, parts)


def solution(mesh):
    placed = (
        P(("group", "node"), None),
        P(("group", "node"), None),
        P(("group", "node"), None),
        P(),
        P(None, "node"),
        P(None, "node"),
        P("node", None),
    )
    return jax.shard_map(
        local, mesh=mesh, in_specs=placed, out_specs=P(("group", "node"), None), check_vma=False
    )
```

```python
import functools

import jax
import jax.numpy as jnp
from jax import lax
from jax.experimental import pallas as pl
from jax.experimental.pallas import tpu as pltpu
from jax.sharding import PartitionSpec as P

VMEM_BYTES = 24 * 2**20
VMEM = pl.BlockSpec(memory_space=pltpu.VMEM)
SMEM = pl.BlockSpec(memory_space=pltpu.SMEM)
ANYWHERE = pl.BlockSpec(memory_space=pl.ANY)
LOADS = 4
N1, N2, N3, N4 = 30,30,30,30
NO_COST = pl.CostEstimate(flops=0, bytes_accessed=0, transcendentals=0)


def in_vmem(value):
    return pltpu.with_memory_space_constraint(value, pltpu.VMEM)


def in_hbm(value):
    return pltpu.with_memory_space_constraint(value, pltpu.HBM)


def product(lhs, rhs):
    return jnp.dot(lhs, rhs, preferred_element_type=jnp.float32)


def slots_of(ids, n_blocks):
    top, rows = ids.shape
    experts = lax.broadcasted_iota(jnp.int32, (n_blocks, rows), 0)
    picks = jnp.zeros((n_blocks, rows), jnp.float32)
    for k in range(top):
        picks = picks + jnp.where(ids[k : k + 1, :] == experts, 1.0, 0.0)
    before = lax.broadcasted_iota(jnp.int32, (rows, rows), 0) < lax.broadcasted_iota(
        jnp.int32, (rows, rows), 1
    )
    earlier = product(picks.astype(jnp.bfloat16), jnp.where(before, 1.0, 0.0).astype(jnp.bfloat16))
    return experts, picks, earlier


def expert_at(placement_ref, block):
    found = jnp.int32(0)
    for e in range(placement_ref.shape[0]):
        found = jnp.where(placement_ref[e] == block, jnp.int32(e), found)
    return found


def row_of(values, experts, expert):
    return jnp.sum(jnp.where(experts == expert, values, 0.0), axis=0, keepdims=True)


def bucket_rows(rows):
    row = lax.broadcasted_iota(jnp.int32, (rows, rows), 0)
    half, quarter = rows // 2, rows // 4
    return jnp.where(row < half, row, half + row % quarter).astype(jnp.float32)


def pack_kernel(n_blocks, parts, placement_ref, ids_ref, tokens_ref, *out_refs):
    rows, width = tokens_ref.shape
    half, quarter = rows // 2, rows // 4
    block = lax.axis_index("node") // parts
    experts, picks, earlier = slots_of(ids_ref[...], n_blocks)
    wanted = bucket_rows(rows)
    upper = lax.broadcasted_iota(jnp.int32, (half, width // 2), 0) < quarter
    for k, out_ref in enumerate(out_refs):
        expert = expert_at(placement_ref, lax.bitwise_xor(block, jnp.int32(k)))
        named = row_of(picks, experts, expert) > 0.5
        slot = row_of(earlier, experts, expert)
        chooser = jnp.where(named & (slot == wanted), 1.0, 0.0).astype(jnp.bfloat16)
        packed = product(chooser, tokens_ref[...])
        out_ref[:, :width] = packed[:half].astype(jnp.bfloat16)
        rest = jnp.where(upper, packed[half:, : width // 2], packed[half:, width // 2 :])
        out_ref[:, width:] = rest.astype(jnp.bfloat16)


def pack(placement, ids, tokens, n_blocks, parts):
    rows, width = tokens.shape
    shape = pltpu.VMEM((rows // 2, width + width // 2), jnp.bfloat16)
    return pl.pallas_call(
        functools.partial(pack_kernel, n_blocks, parts),
        out_shape=[shape] * n_blocks,
        in_specs=[SMEM, VMEM, VMEM],
        out_specs=[VMEM] * n_blocks,
        compiler_params=pltpu.CompilerParams(vmem_limit_bytes=VMEM_BYTES),
        cost_estimate=NO_COST,
    )(in_hbm(placement), in_hbm(ids), in_hbm(tokens))


def nothing(*refs):
    pass


def clear(*refs):
    refs[-1][...] = jnp.zeros_like(refs[-1])


def token(after, percent):
    rows, width = after.shape
    return pl.pallas_call(
        clear,
        out_shape=pltpu.VMEM((rows, width * percent // 12800 * 128), after.dtype),
        in_specs=[ANYWHERE],
        out_specs=VMEM,
        compiler_params=pltpu.CompilerParams(vmem_limit_bytes=VMEM_BYTES),
        cost_estimate=NO_COST,
    )(after)


def when(value, after):
    if not after:
        return value
    return pl.pallas_call(
        nothing,
        out_shape=pltpu.VMEM(value.shape, value.dtype),
        in_specs=[ANYWHERE] * (1 + len(after)),
        out_specs=ANYWHERE,
        input_output_aliases={0: 0},
        compiler_params=pltpu.CompilerParams(vmem_limit_bytes=VMEM_BYTES),
        cost_estimate=NO_COST,
    )(in_vmem(value), *after)


def load_kernel(*refs):
    sources, targets, sems = refs[:3], refs[4:7], refs[7]
    copies = []
    for i, (source, target) in enumerate(zip(sources, targets)):
        rows = source.shape[0] // LOADS
        for j in range(LOADS):
            part = pl.ds(j * rows, rows)
            copies.append(pltpu.make_async_copy(source.at[part], target.at[part], sems.at[i, j]))
    for copy in copies:
        copy.start()
    for copy in copies:
        copy.wait()


def load(weights, after):
    return pl.pallas_call(
        load_kernel,
        out_shape=[pltpu.VMEM(w.shape, w.dtype) for w in weights],
        in_specs=[pl.BlockSpec(memory_space=pltpu.HBM)] * 3 + [ANYWHERE],
        out_specs=[VMEM] * 3,
        scratch_shapes=[pltpu.SemaphoreType.DMA((3, LOADS))],
        compiler_params=pltpu.CompilerParams(vmem_limit_bytes=VMEM_BYTES),
        cost_estimate=NO_COST,
    )(*[pltpu.with_memory_space_constraint(w, pltpu.HBM) for w in weights], after)


def experts_kernel(count, *refs):
    pieces = refs[:count]
    gate_ref, up_ref, down_ref = refs[count : count + 3]
    out_refs = refs[-count:]
    width, hid = gate_ref.shape
    middle = width // 2
    height = pieces[0].shape[0]
    total = count * height
    rest = jnp.concatenate([p[:, width:] for p in pieces], axis=0)
    left = jnp.concatenate([p[:, :middle] for p in pieces] + [rest], axis=0)
    right = jnp.concatenate([p[:, middle:width] for p in pieces] + [rest], axis=0)
    upper = lax.broadcasted_iota(jnp.int32, (total, 1), 0) % height < height // 2
    shift = height // 2

    def whole_rows(ref):
        a, b = product(left, ref[:middle, :]), product(right, ref[middle:, :])
        tail = jnp.where(
            upper,
            a[total:] + pltpu.roll(b[total:], total - shift, axis=0),
            b[total:] + pltpu.roll(a[total:], shift, axis=0),
        )
        return jnp.concatenate([a[:total] + b[:total], tail], axis=0)

    gate_rows, up_rows = whole_rows(gate_ref), whole_rows(up_ref)
    hidden = (jax.nn.silu(gate_rows) * up_rows).astype(jnp.bfloat16)

    def store(start, values):
        values = values.astype(jnp.bfloat16)
        stop = start + values.shape[1]
        for i, out_ref in enumerate(out_refs):
            out_ref[:, start:stop] = values[i * height : (i + 1) * height]

    step = middle // 4
    for i in range(4):
        begin = i * step
        a = product(hidden, down_ref[:, begin : begin + step])
        b = product(hidden, down_ref[:, middle + begin : middle + begin + step])
        store(begin, a[:total])
        store(middle + begin, b[:total])
        store(width + begin, jnp.where(upper, a[total:], b[total:]))


def run_experts(pieces, weights, after):
    count = len(pieces)
    shape = pltpu.VMEM(pieces[0].shape, jnp.bfloat16)
    operands = [in_vmem(value) for value in [*pieces, *weights]]
    return pl.pallas_call(
        functools.partial(experts_kernel, count),
        out_shape=[shape] * count,
        in_specs=[VMEM] * len(operands) + [ANYWHERE] * len(after),
        out_specs=[VMEM] * count,
        compiler_params=pltpu.CompilerParams(vmem_limit_bytes=VMEM_BYTES),
        cost_estimate=NO_COST,
    )(*operands, *after)


def mix_kernel(n_blocks, parts, placement_ref, ids_ref, gates_ref, *refs):
    results, out_ref = refs[:n_blocks], refs[-1]
    rows, width = out_ref.shape
    half, quarter, middle = rows // 2, rows // 4, width // 2
    block = lax.axis_index("node") // parts
    ids, gates = ids_ref[...], gates_ref[...]
    experts, picks, earlier = slots_of(ids, n_blocks)
    wanted = bucket_rows(rows)
    terms = []
    for k in range(n_blocks):
        expert = expert_at(placement_ref, lax.bitwise_xor(block, jnp.int32(k)))
        named = row_of(picks, experts, expert) > 0.5
        slot = row_of(earlier, experts, expert)
        weight = jnp.sum(jnp.where(ids == expert, gates, 0.0), axis=0, keepdims=True)
        terms.append(jnp.where(named & (slot == wanted), weight, 0.0))
    term = jnp.concatenate(terms, axis=0)
    row = lax.broadcasted_iota(jnp.int32, term.shape, 0) % rows
    for side in range(2):
        first = half + side * quarter
        mine = jnp.where((row < half) | ((row >= first) & (row < first + quarter)), term, 0.0)
        high = mine.astype(jnp.bfloat16)
        lower = mine - high.astype(jnp.float32)
        mid = lower.astype(jnp.bfloat16)
        low = (lower - mid.astype(jnp.float32)).astype(jnp.bfloat16)
        lhs = jnp.concatenate([high, mid, low], axis=1)
        pieces = []
        for r in results:
            pieces += [r[:, side * middle : (side + 1) * middle], r[:, width:]]
        rhs = jnp.concatenate([p.astype(jnp.bfloat16) for p in pieces], axis=0)
        value = lax.dot_general(
            lhs, rhs, (((0,), (0,)), ((), ())), preferred_element_type=jnp.float32
        )
        value = value[:rows] + value[rows : 2 * rows] + value[2 * rows :]
        out_ref[:, side * middle : (side + 1) * middle] = value.astype(jnp.bfloat16)


def mix(placement, ids, gates, results, after, n_blocks, parts):
    rows = ids.shape[1]
    width = results[0].shape[1] // 3 * 2
    return pl.pallas_call(
        functools.partial(mix_kernel, n_blocks, parts),
        out_shape=jax.ShapeDtypeStruct((rows, width), jnp.bfloat16),
        in_specs=[SMEM] + [VMEM] * (2 + n_blocks) + [ANYWHERE] * len(after),
        out_specs=VMEM,
        compiler_params=pltpu.CompilerParams(vmem_limit_bytes=VMEM_BYTES),
        cost_estimate=pl.CostEstimate(
            flops=6 * n_blocks * rows * rows * width,
            bytes_accessed=2 * (n_blocks + 1) * rows * width,
            transcendentals=0,
        ),
    )(placement, ids, gates, *[in_vmem(r) for r in results], *after)


def add_kernel(*refs):
    total = refs[0][...].astype(jnp.float32)
    for ref in refs[1:-1]:
        total = total + ref[...].astype(jnp.float32)
    refs[-1][...] = total.astype(refs[-1].dtype)


def add(*values):
    return pl.pallas_call(
        add_kernel,
        out_shape=pltpu.VMEM(values[0].shape, values[0].dtype),
        in_specs=[VMEM] * len(values),
        out_specs=VMEM,
        compiler_params=pltpu.CompilerParams(vmem_limit_bytes=VMEM_BYTES),
        cost_estimate=NO_COST,
    )(*[in_vmem(v) for v in values])


def local(tokens, expert_ids, gates, placement, gate_weight, up_weight, down_weight):
    n_blocks = placement.shape[0]
    devices = lax.axis_size("node")
    parts = devices // n_blocks

    def along_z(value, k):
        pairs = [(i, i ^ (k * parts)) for i in range(devices)]
        return lax.ppermute(value, "node", pairs)

    def along_y(value):
        return lax.ppermute(value, "node", [(i, i ^ 2) for i in range(devices)])

    def along_core(value):
        return lax.ppermute(value, "node", [(i, i ^ 1) for i in range(devices)])

    ids = expert_ids.T
    groups = [[n_blocks - d, d] for d in range(1, n_blocks // 2)] + [[n_blocks // 2]]
    last, early = groups[-1][0], [group[0] for group in groups[:-1]]
    straight, across, results = {}, {}, {}
    both, home, kept, sent = {}, {}, {}, {}

    def compute(blocks, after):
        pieces = []
        for k in blocks:
            pieces += [straight[k], across[k], along_core(straight[k]), along_core(across[k])]
        out = run_experts(pieces, weights, after)
        for i, k in enumerate(blocks):
            sent[k] = out[4 * i + 3]
            both[k] = add(out[4 * i + 1], along_core(out[4 * i + 3]))
            kept[k] = out[4 * i], along_core(out[4 * i + 2])

    def go_home(k, after):
        home[k] = add(*kept[k], along_y(when(both[k], after)))
        if k in early:
            home[k] = when(home[k], [along_core(token(home[k], 20))])
        results[k] = along_z(home[k], k) if k else home[k]

    buckets = list(pack(placement, ids, tokens, n_blocks, parts))
    weights = load((gate_weight, up_weight, down_weight), buckets[0])
    straight[0] = buckets[0]
    across[0] = along_y(straight[0])
    second = None
    for g, group in enumerate(groups):
        first = group[0]
        if g == 0:
            straight[first] = along_z(buckets[first], first)
            across[first] = along_y(straight[first])
            compute([0, first], [])
        else:
            previous = groups[g - 1][0]
            straight[first] = along_z(when(buckets[first], [straight[previous], across[0]]), first)
            straight[first] = when(straight[first], [across[second], across[previous]])
            across[first] = along_y(straight[first])
            go_home(previous, [])
            compute([second, first], [both[previous]])
            go_home(second, [])
        if len(group) > 1:
            second = group[1]
            straight[second] = along_z(when(buckets[second], [weights[0]] if g == 0 else []), second)
            across[second] = along_y(straight[second])
    go_home(last, [])
    marks = [along_core(token(results[k], 85)) for k in early]
    go_home(0, [home[last]])
    results = [results[k] for k in range(n_blocks)]
    return mix(placement, ids, gates.T, results, marks, n_blocks, parts)


def solution(mesh):
    placed = (
        P(("group", "node"), None),
        P(("group", "node"), None),
        P(("group", "node"), None),
        P(),
        P(None, "node"),
        P(None, "node"),
        P("node", None),
    )
    return jax.shard_map(
        local, mesh=mesh, in_specs=placed, out_specs=P(("group", "node"), None), check_vma=False
    )
```

```python
import functools

import jax
import jax.numpy as jnp
from jax import lax
from jax.experimental import pallas as pl
from jax.experimental.pallas import tpu as pltpu
from jax.sharding import PartitionSpec as P

VMEM_BYTES = 24 * 2**20
VMEM = pl.BlockSpec(memory_space=pltpu.VMEM)
SMEM = pl.BlockSpec(memory_space=pltpu.SMEM)
ANYWHERE = pl.BlockSpec(memory_space=pl.ANY)
LOADS = 4
N1, N2, N3, N4 = 30,30,30,30
NO_COST = pl.CostEstimate(flops=0, bytes_accessed=0, transcendentals=0)


def in_vmem(value):
    return pltpu.with_memory_space_constraint(value, pltpu.VMEM)


def in_hbm(value):
    return pltpu.with_memory_space_constraint(value, pltpu.HBM)


def product(lhs, rhs):
    return jnp.dot(lhs, rhs, preferred_element_type=jnp.float32)


def slots_of(ids, n_blocks):
    top, rows = ids.shape
    experts = lax.broadcasted_iota(jnp.int32, (n_blocks, rows), 0)
    picks = jnp.zeros((n_blocks, rows), jnp.float32)
    for k in range(top):
        picks = picks + jnp.where(ids[k : k + 1, :] == experts, 1.0, 0.0)
    before = lax.broadcasted_iota(jnp.int32, (rows, rows), 0) < lax.broadcasted_iota(
        jnp.int32, (rows, rows), 1
    )
    earlier = product(picks.astype(jnp.bfloat16), jnp.where(before, 1.0, 0.0).astype(jnp.bfloat16))
    return experts, picks, earlier


def expert_at(placement_ref, block):
    found = jnp.int32(0)
    for e in range(placement_ref.shape[0]):
        found = jnp.where(placement_ref[e] == block, jnp.int32(e), found)
    return found


def row_of(values, experts, expert):
    return jnp.sum(jnp.where(experts == expert, values, 0.0), axis=0, keepdims=True)


def bucket_rows(rows):
    row = lax.broadcasted_iota(jnp.int32, (rows, rows), 0)
    half, quarter = rows // 2, rows // 4
    return jnp.where(row < half, row, half + row % quarter).astype(jnp.float32)


def pack_kernel(n_blocks, parts, placement_ref, ids_ref, tokens_ref, *out_refs):
    rows, width = tokens_ref.shape
    half, quarter = rows // 2, rows // 4
    block = lax.axis_index("node") // parts
    experts, picks, earlier = slots_of(ids_ref[...], n_blocks)
    wanted = bucket_rows(rows)
    upper = lax.broadcasted_iota(jnp.int32, (half, width // 2), 0) < quarter
    for k, out_ref in enumerate(out_refs):
        expert = expert_at(placement_ref, lax.bitwise_xor(block, jnp.int32(k)))
        named = row_of(picks, experts, expert) > 0.5
        slot = row_of(earlier, experts, expert)
        chooser = jnp.where(named & (slot == wanted), 1.0, 0.0).astype(jnp.bfloat16)
        packed = product(chooser, tokens_ref[...])
        out_ref[:, :width] = packed[:half].astype(jnp.bfloat16)
        rest = jnp.where(upper, packed[half:, : width // 2], packed[half:, width // 2 :])
        out_ref[:, width:] = rest.astype(jnp.bfloat16)


def pack(placement, ids, tokens, n_blocks, parts):
    rows, width = tokens.shape
    shape = pltpu.VMEM((rows // 2, width + width // 2), jnp.bfloat16)
    return pl.pallas_call(
        functools.partial(pack_kernel, n_blocks, parts),
        out_shape=[shape] * n_blocks,
        in_specs=[SMEM, VMEM, VMEM],
        out_specs=[VMEM] * n_blocks,
        compiler_params=pltpu.CompilerParams(vmem_limit_bytes=VMEM_BYTES),
        cost_estimate=NO_COST,
    )(in_hbm(placement), in_hbm(ids), in_hbm(tokens))


def nothing(*refs):
    pass


def clear(*refs):
    refs[-1][...] = jnp.zeros_like(refs[-1])


def token(after, percent):
    rows, width = after.shape
    return pl.pallas_call(
        clear,
        out_shape=pltpu.VMEM((rows, width * percent // 12800 * 128), after.dtype),
        in_specs=[ANYWHERE],
        out_specs=VMEM,
        compiler_params=pltpu.CompilerParams(vmem_limit_bytes=VMEM_BYTES),
        cost_estimate=NO_COST,
    )(after)


def when(value, after):
    if not after:
        return value
    return pl.pallas_call(
        nothing,
        out_shape=pltpu.VMEM(value.shape, value.dtype),
        in_specs=[ANYWHERE] * (1 + len(after)),
        out_specs=ANYWHERE,
        input_output_aliases={0: 0},
        compiler_params=pltpu.CompilerParams(vmem_limit_bytes=VMEM_BYTES),
        cost_estimate=NO_COST,
    )(in_vmem(value), *after)


def load_kernel(*refs):
    sources, targets, sems = refs[:3], refs[4:7], refs[7]
    copies = []
    for i, (source, target) in enumerate(zip(sources, targets)):
        rows = source.shape[0] // LOADS
        for j in range(LOADS):
            part = pl.ds(j * rows, rows)
            copies.append(pltpu.make_async_copy(source.at[part], target.at[part], sems.at[i, j]))
    for copy in copies:
        copy.start()
    for copy in copies:
        copy.wait()


def load(weights, after):
    return pl.pallas_call(
        load_kernel,
        out_shape=[pltpu.VMEM(w.shape, w.dtype) for w in weights],
        in_specs=[pl.BlockSpec(memory_space=pltpu.HBM)] * 3 + [ANYWHERE],
        out_specs=[VMEM] * 3,
        scratch_shapes=[pltpu.SemaphoreType.DMA((3, LOADS))],
        compiler_params=pltpu.CompilerParams(vmem_limit_bytes=VMEM_BYTES),
        cost_estimate=NO_COST,
    )(*[pltpu.with_memory_space_constraint(w, pltpu.HBM) for w in weights], after)


def experts_kernel(count, *refs):
    pieces = refs[:count]
    gate_ref, up_ref, down_ref = refs[count : count + 3]
    out_refs = refs[-count:]
    width, hid = gate_ref.shape
    middle = width // 2
    height = pieces[0].shape[0]
    total = count * height
    rest = jnp.concatenate([p[:, width:] for p in pieces], axis=0)
    left = jnp.concatenate([p[:, :middle] for p in pieces] + [rest], axis=0)
    right = jnp.concatenate([p[:, middle:width] for p in pieces] + [rest], axis=0)
    upper = lax.broadcasted_iota(jnp.int32, (total, 1), 0) % height < height // 2
    shift = height // 2

    def whole_rows(ref):
        a, b = product(left, ref[:middle, :]), product(right, ref[middle:, :])
        tail = jnp.where(
            upper,
            a[total:] + pltpu.roll(b[total:], total - shift, axis=0),
            b[total:] + pltpu.roll(a[total:], shift, axis=0),
        )
        return jnp.concatenate([a[:total] + b[:total], tail], axis=0)

    gate_rows, up_rows = whole_rows(gate_ref), whole_rows(up_ref)
    hidden = (jax.nn.silu(gate_rows) * up_rows).astype(jnp.bfloat16)

    def store(start, values):
        values = values.astype(jnp.bfloat16)
        stop = start + values.shape[1]
        for i, out_ref in enumerate(out_refs):
            out_ref[:, start:stop] = values[i * height : (i + 1) * height]

    step = middle // 4
    for i in range(4):
        begin = i * step
        a = product(hidden, down_ref[:, begin : begin + step])
        b = product(hidden, down_ref[:, middle + begin : middle + begin + step])
        store(begin, a[:total])
        store(middle + begin, b[:total])
        store(width + begin, jnp.where(upper, a[total:], b[total:]))


def run_experts(pieces, weights, after):
    count = len(pieces)
    shape = pltpu.VMEM(pieces[0].shape, jnp.bfloat16)
    operands = [in_vmem(value) for value in [*pieces, *weights]]
    return pl.pallas_call(
        functools.partial(experts_kernel, count),
        out_shape=[shape] * count,
        in_specs=[VMEM] * len(operands) + [ANYWHERE] * len(after),
        out_specs=[VMEM] * count,
        compiler_params=pltpu.CompilerParams(vmem_limit_bytes=VMEM_BYTES),
        cost_estimate=NO_COST,
    )(*operands, *after)


def mix_kernel(n_blocks, parts, placement_ref, ids_ref, gates_ref, *refs):
    results, (out_hbm, out_ref, sems) = refs[:n_blocks], refs[-3:]
    rows, width = out_ref.shape
    half, quarter, middle = rows // 2, rows // 4, width // 2
    block = lax.axis_index("node") // parts
    ids, gates = ids_ref[...], gates_ref[...]
    experts, picks, earlier = slots_of(ids, n_blocks)
    wanted = bucket_rows(rows)
    terms = []
    for k in range(n_blocks):
        expert = expert_at(placement_ref, lax.bitwise_xor(block, jnp.int32(k)))
        named = row_of(picks, experts, expert) > 0.5
        slot = row_of(earlier, experts, expert)
        weight = jnp.sum(jnp.where(ids == expert, gates, 0.0), axis=0, keepdims=True)
        terms.append(jnp.where(named & (slot == wanted), weight, 0.0))
    term = jnp.concatenate(terms, axis=0)
    row = lax.broadcasted_iota(jnp.int32, term.shape, 0) % rows
    copies = []
    for side in range(2):
        first = half + side * quarter
        mine = jnp.where((row < half) | ((row >= first) & (row < first + quarter)), term, 0.0)
        high = mine.astype(jnp.bfloat16)
        lower = mine - high.astype(jnp.float32)
        mid = lower.astype(jnp.bfloat16)
        low = (lower - mid.astype(jnp.float32)).astype(jnp.bfloat16)
        lhs = jnp.concatenate([high, mid, low], axis=1)
        pieces = []
        for r in results:
            pieces += [r[:, side * middle : (side + 1) * middle], r[:, width:]]
        rhs = jnp.concatenate([p.astype(jnp.bfloat16) for p in pieces], axis=0)
        value = lax.dot_general(
            lhs, rhs, (((0,), (0,)), ((), ())), preferred_element_type=jnp.float32
        )
        value = value[:rows] + value[rows : 2 * rows] + value[2 * rows :]
        out_ref[:, side * middle : (side + 1) * middle] = value.astype(jnp.bfloat16)
        half_columns = pl.ds(side * middle, middle)
        copy = pltpu.make_async_copy(
            out_ref.at[:, half_columns], out_hbm.at[:, half_columns], sems.at[side]
        )
        copy.start()
        copies.append(copy)
    for copy in copies:
        copy.wait()


def mix(placement, ids, gates, results, after, n_blocks, parts):
    rows = ids.shape[1]
    width = results[0].shape[1] // 3 * 2
    return pl.pallas_call(
        functools.partial(mix_kernel, n_blocks, parts),
        out_shape=jax.ShapeDtypeStruct((rows, width), jnp.bfloat16),
        in_specs=[SMEM] + [VMEM] * (2 + n_blocks) + [ANYWHERE] * len(after),
        out_specs=pl.BlockSpec(memory_space=pltpu.HBM),
        scratch_shapes=[pltpu.VMEM((rows, width), jnp.bfloat16), pltpu.SemaphoreType.DMA((2,))],
        compiler_params=pltpu.CompilerParams(vmem_limit_bytes=VMEM_BYTES),
        cost_estimate=pl.CostEstimate(
            flops=6 * n_blocks * rows * rows * width,
            bytes_accessed=2 * (n_blocks + 1) * rows * width,
            transcendentals=0,
        ),
    )(placement, ids, gates, *[in_vmem(r) for r in results], *after)


def add_kernel(*refs):
    total = refs[0][...].astype(jnp.float32)
    for ref in refs[1:-1]:
        total = total + ref[...].astype(jnp.float32)
    refs[-1][...] = total.astype(refs[-1].dtype)


def add(*values):
    return pl.pallas_call(
        add_kernel,
        out_shape=pltpu.VMEM(values[0].shape, values[0].dtype),
        in_specs=[VMEM] * len(values),
        out_specs=VMEM,
        compiler_params=pltpu.CompilerParams(vmem_limit_bytes=VMEM_BYTES),
        cost_estimate=NO_COST,
    )(*[in_vmem(v) for v in values])


def local(tokens, expert_ids, gates, placement, gate_weight, up_weight, down_weight):
    n_blocks = placement.shape[0]
    devices = lax.axis_size("node")
    parts = devices // n_blocks

    def along_z(value, k):
        pairs = [(i, i ^ (k * parts)) for i in range(devices)]
        return lax.ppermute(value, "node", pairs)

    def along_y(value):
        return lax.ppermute(value, "node", [(i, i ^ 2) for i in range(devices)])

    def along_core(value):
        return lax.ppermute(value, "node", [(i, i ^ 1) for i in range(devices)])

    ids = expert_ids.T
    groups = [[n_blocks - d, d] for d in range(1, n_blocks // 2)] + [[n_blocks // 2]]
    last, early = groups[-1][0], [group[0] for group in groups[:-1]]
    straight, across, results = {}, {}, {}
    both, home, kept, sent = {}, {}, {}, {}

    def compute(blocks, after):
        pieces = []
        for k in blocks:
            pieces += [straight[k], across[k], along_core(straight[k]), along_core(across[k])]
        out = run_experts(pieces, weights, after)
        for i, k in enumerate(blocks):
            sent[k] = out[4 * i + 3]
            both[k] = add(out[4 * i + 1], along_core(out[4 * i + 3]))
            kept[k] = out[4 * i], along_core(out[4 * i + 2])

    def go_home(k, after):
        home[k] = add(*kept[k], along_y(when(both[k], after)))
        if k in early:
            home[k] = when(home[k], [along_core(token(home[k], 20))])
        results[k] = along_z(home[k], k) if k else home[k]

    buckets = list(pack(placement, ids, tokens, n_blocks, parts))
    weights = load((gate_weight, up_weight, down_weight), buckets[0])
    straight[0] = buckets[0]
    across[0] = along_y(straight[0])
    second = None
    for g, group in enumerate(groups):
        first = group[0]
        if g == 0:
            straight[first] = along_z(buckets[first], first)
            across[first] = along_y(straight[first])
            compute([0, first], [])
        else:
            previous = groups[g - 1][0]
            straight[first] = along_z(when(buckets[first], [straight[previous]]), first)
            straight[first] = when(straight[first], [across[second], across[previous]])
            across[first] = along_y(straight[first])
            go_home(previous, [])
            compute([second, first], [both[previous]])
            go_home(second, [])
        if len(group) > 1:
            second = group[1]
            straight[second] = along_z(when(buckets[second], [weights[0]] if g == 0 else []), second)
            across[second] = along_y(straight[second])
    go_home(last, [])
    marks = [along_core(token(results[k], 85)) for k in early]
    go_home(0, [home[last]])
    results = [results[k] for k in range(n_blocks)]
    return mix(placement, ids, gates.T, results, marks, n_blocks, parts)


def solution(mesh):
    placed = (
        P(("group", "node"), None),
        P(("group", "node"), None),
        P(("group", "node"), None),
        P(),
        P(None, "node"),
        P(None, "node"),
        P("node", None),
    )
    return jax.shard_map(
        local, mesh=mesh, in_specs=placed, out_specs=P(("group", "node"), None), check_vma=False
    )
```
